32 devices in a mesh: seq: 8 (over z, x), dp: 2 (over y), domain: 2 (over core).
Axes of the slice: x: 2, y: 2, z: 4, core: 2. Of those that a mesh axis runs over, the one named last changes fastest.
Arguments:
- history: bfloat16 [2, 2, 2048, 1024], P('domain', 'dp', 'seq'), may hold values from -6 to 6
- qkv_weight: bfloat16 [2, 1024, 3072], P('domain', 'seq'), may hold values from -0.375 to 0.375
- norm_gain: float32 [2, 1024], P('domain'), may hold values from 0.1 to 1.9
- pool_gain: float32 [2, 1024], P('domain'), may hold values from 0.1 to 1.9
- lengths: int32 [2, 2], P('domain', 'dp'), may hold values from 256 to 2048, as said below
- positives: int32 [2], replicated, may hold values from 0 to 1, each once
Outputs:
- user_vec: bfloat16 [2, 2, 1024], P('domain', 'dp', 'seq')
- loss: float32 [2, 2], P('domain', 'dp')
The draws below stay inside these ranges and needn't reach their ends.
Inputs may be any that keep to these rules, and one draw needn't show every extreme that they name: `lengths`: in each domain one user has exactly 2048 valid events and another exactly 256. `positives`: each user of the second domain is named exactly once.
All inputs are finite; a program needn't handle non-finite values.
Results may differ from the reference program's by a relative error of at most 0.0085.
Values may be sent and summed in bfloat16 or wider, within the bound.
No kernel may reach another device: no remote copies, remote signals or barrier semaphores. Data moves between devices by JAX's collectives and lax.ppermute only.
A program may use at most 64 MiB of HBM per device.

```python
import jax
import jax.numpy as jnp
from jax import lax

HEADS = 8
HEAD_DIM = 128
D = 1024
TOK_DEV = 256
LEN = 2048
USERS = 2


def draw_lengths(key, part):
    key_base, key_first, key_second = jax.random.split(key, 3)
    drawn = jax.random.randint(key_base, (2, USERS), LEN // 8, LEN + 1)
    longest = jax.random.randint(key_first, (2, 1), 0, USERS)
    shortest = (longest + 1 + jax.random.randint(key_second, (2, 1), 0, USERS - 1)) % USERS
    column = jnp.arange(USERS)[None, :]
    drawn = jnp.where(column == longest, LEN, drawn)
    drawn = jnp.where(column == shortest, LEN // 8, drawn)
    return drawn.astype(jnp.int32)


def draw_history(key, part):
    key_coef, key_pick, key_load, key_noise, key_level = jax.random.split(jax.random.fold_in(key, 7), 5)
    directions = 16
    block_count = LEN // TOK_DEV
    pair_count = TOK_DEV // 2
    leading = (2, USERS, block_count)
    coefficient = jax.random.normal(key_coef, leading + (pair_count, directions), jnp.float32)
    loading = jax.random.normal(key_load, leading + (1, D), jnp.float32)
    fresh_noise = jax.random.normal(key_noise, leading + (pair_count, 2, D), jnp.float32)
    noise_level = 0.6 + 0.0 * jax.random.uniform(key_level, leading + (1, 1, 1), jnp.float32)
    chosen = jax.random.randint(key_pick, leading + (1, D), 0, directions)
    chosen = jnp.broadcast_to(chosen, leading + (pair_count, D))
    picked = jnp.take_along_axis(coefficient, chosen, axis=-1)
    shared = picked * loading
    pair_sign = jnp.array([1.0, -1.0], jnp.float32)
    events = shared[..., None, :] * pair_sign[:, None] + noise_level * fresh_noise
    events = jnp.clip(events, -6.0, 6.0)
    return events.reshape(2, USERS, LEN, D).astype(jnp.bfloat16)


def level_of(stream_key, dims, cuts, smallest, largest):
    loudness = 1.0
    for axis_at, parts in cuts:
        draws = jax.random.uniform(jax.random.fold_in(jax.random.fold_in(stream_key, 6), axis_at), (parts,), jnp.float32, smallest / len(cuts), largest / len(cuts))
        loudness = loudness * jnp.repeat(jnp.exp(draws), dims[axis_at] // parts).reshape((-1,) + (1,) * (len(dims) - 1 - axis_at))
    return loudness


def gaussian(own_key, extent, spread, limit, cuts=(), dtype=jnp.bfloat16):
    factor_of = level_of(own_key, extent, cuts, -0.22, 0.18) if cuts else 1.0
    values = jax.random.normal(own_key, extent, jnp.float32) * spread * factor_of
    return jnp.minimum(jnp.maximum(values, -limit), limit).astype(dtype)


def setup_inputs(seed: int = 0) -> dict:
    streams_of = jax.random.split(jax.random.key(seed), 7)
    return {
        "history": draw_history(jax.random.fold_in(streams_of[6], 71), 0),
        "qkv_weight": gaussian(streams_of[1], (2, D, 3 * D), (D // 4) ** -0.5, 0.375, ((0, 2), (1, 8))),
        "norm_gain": jnp.clip(1.0 + 0.18 * jax.random.normal(streams_of[2], (2, D), jnp.float32), 0.1, 1.9),
        "pool_gain": jnp.clip(1.0 + 0.18 * jax.random.normal(streams_of[3], (2, D), jnp.float32), 0.1, 1.9),
        "lengths": draw_lengths(jax.random.fold_in(streams_of[6], 71), 0),
        "positives": jax.random.permutation(streams_of[5], USERS).astype(jnp.int32),
    }


logit_scale = 20.0
epsilon = 1e-06
highest = lax.Precision.HIGHEST

def feature_map(values):
    return jax.nn.elu(values) + 1.0

def attend_block(carry, block):
    state, total = carry
    queries, key_feats, val_feats = block
    queries_f = queries.astype(jnp.float32)
    keys_f = key_feats.astype(jnp.float32)
    values_f = val_feats.astype(jnp.float32)
    causal = jnp.arange(TOK_DEV)[:, None] >= jnp.arange(TOK_DEV)[None, :]
    scores = jnp.einsum('thc,shc->hts', queries_f, keys_f)
    scores = jnp.where(causal[None], scores, 0.0)
    denominator = lax.optimization_barrier(jnp.sum(scores, axis=-1)) + jnp.einsum('thc,hc->ht', queries_f, total, precision=highest)
    rounded = lax.optimization_barrier(scores.astype(jnp.bfloat16)).astype(jnp.float32)
    state_low = lax.optimization_barrier(state.astype(jnp.bfloat16)).astype(jnp.float32)
    numerator = jnp.einsum('hts,shc->thc', rounded, values_f) + jnp.einsum('thc,hcd->thd', queries_f, state_low)
    attended = numerator / jnp.transpose(denominator)[:, :, None]
    state = state + jnp.einsum('shc,shd->hcd', keys_f, values_f)
    total = total + lax.optimization_barrier(jnp.sum(keys_f, axis=0))
    return ((state, total), attended)

def tower(history_dom, weight, norm_row, pool_row, lengths_dom):

    def one_user(pair):
        events, length = pair
        wide = events.astype(jnp.float32)
        normed = (wide * lax.rsqrt(lax.optimization_barrier(jnp.mean(wide * wide, -1, keepdims=True)) + epsilon) * norm_row).astype(jnp.bfloat16)
        projected = jnp.dot(normed, weight, preferred_element_type=jnp.float32)
        valid = jnp.arange(LEN) < length
        queries = feature_map(projected[:, :D]).astype(jnp.bfloat16)
        key_feats = jnp.where(valid[:, None], feature_map(projected[:, D:2 * D]), 0.0).astype(jnp.bfloat16)
        val_feats = projected[:, 2 * D:].astype(jnp.bfloat16)
        shape = (LEN // TOK_DEV, TOK_DEV, HEADS, HEAD_DIM)
        start = (jnp.zeros((HEADS, HEAD_DIM, HEAD_DIM), jnp.float32), jnp.zeros((HEADS, HEAD_DIM), jnp.float32))
        final_state, attended = lax.scan(attend_block, start, (queries.reshape(shape), key_feats.reshape(shape), val_feats.reshape(shape)))
        attended = attended.reshape(LEN, D)
        return lax.optimization_barrier(jnp.sum(jnp.where(valid[:, None], wide + attended, 0.0), axis=0))
    pooled = lax.map(one_user, (history_dom, lengths_dom))
    factor = lax.rsqrt(lax.optimization_barrier(jnp.mean(pooled * pooled, -1, keepdims=True)) + epsilon)
    return (pooled * factor * pool_row).astype(jnp.bfloat16)

def reference(history, qkv_weight, norm_gain, pool_gain, lengths, positives):
    first = tower(history[0], qkv_weight[0], norm_gain[0], pool_gain[0], lengths[0])
    second = tower(history[1], qkv_weight[1], norm_gain[1], pool_gain[1], lengths[1])
    user_vec = jnp.stack([first, second])
    logits = jnp.dot(first, second.T, preferred_element_type=jnp.float32) * (logit_scale / D)
    pairing = positives[:, None] == jnp.arange(USERS)[None, :]
    chosen = jnp.where(pairing, logits, 0.0)
    loss_first = jnp.log(lax.optimization_barrier(jnp.sum(jnp.exp(logits), axis=1))) - lax.optimization_barrier(jnp.sum(chosen, axis=1))
    loss_second = jnp.log(lax.optimization_barrier(jnp.sum(jnp.exp(logits), axis=0))) - lax.optimization_barrier(jnp.sum(chosen, axis=0))
    return (user_vec, jnp.stack([loss_first, loss_second]))
```

```python
import functools

import jax
import jax.numpy as jnp
from jax import lax
from jax.experimental import pallas as pl
from jax.experimental.pallas import tpu as pltpu
from jax.sharding import PartitionSpec as P

HEADS = 8
HEAD_DIM = 128


logit_scale = 20.0
epsilon = 1e-06
highest = lax.Precision.HIGHEST


def carried_in(part, axis, combine, identity):
    place = lax.axis_index(axis)
    gathered = jax.tree.map(lambda a: lax.all_gather(a, axis), part)
    state = jax.tree.map(lambda a, e: jnp.zeros_like(a) + jnp.asarray(e, a.dtype), part, identity)

    def one(hop, state):
        return combine(
            state, jax.tree.map(lambda a: lax.dynamic_index_in_dim(a, hop, 0, False), gathered)
        )

    return lax.fori_loop(0, place, one, state)


def partner_2(block, axis, stride):
    count = lax.axis_size(axis)
    route = []
    for low in range(count):
        high = low | 1 << stride
        if high != low and high < count:
            route += [(low, high), (high, low)]
    return lax.ppermute(block, axis, route)


def feature_map(values):
    return jax.nn.elu(values) + 1.0


def add_pair(earlier, later):
    return (earlier[0] + later[0], earlier[1] + later[1])


def shards(history, qkv_weight, norm_gain, pool_gain, lengths, positives):
    seq_count = lax.axis_size("seq")
    seq_place = lax.axis_index("seq")
    group_place = lax.axis_index("dp")
    domain_place = lax.axis_index("domain")
    events = history[0]
    users_dev, tokens_dev, width = events.shape
    row_count = users_dev * tokens_dev
    wide = events.astype(jnp.float32)
    normed = (
        wide * lax.rsqrt(jnp.mean(wide * wide, -1, keepdims=True) + epsilon) * norm_gain[0]
    ).astype(jnp.bfloat16)
    normed = normed.reshape(row_count, width)
    rows_here = qkv_weight[0]
    projected = jnp.dot(
        normed,
        lax.all_gather(rows_here, "seq", axis=0, tiled=True),
        preferred_element_type=jnp.float32,
    )
    query_raw = projected[:, :width]
    key_raw = projected[:, width : 2 * width]
    value_raw = projected[:, 2 * width :]
    positions = seq_place * tokens_dev + jnp.arange(tokens_dev)
    valid = positions[None, :] < lengths[0][:, None]
    shape_heads = (users_dev, tokens_dev, HEADS, HEAD_DIM)
    queries = feature_map(query_raw).astype(jnp.bfloat16).reshape(shape_heads)
    key_feats = (
        jnp.where(valid.reshape(row_count)[:, None], feature_map(key_raw), 0.0)
        .astype(jnp.bfloat16)
        .reshape(shape_heads)
    )
    val_feats = value_raw.astype(jnp.bfloat16).reshape(shape_heads)
    local_state = jnp.einsum(
        "uthc,uthd->uhcd", key_feats, val_feats, preferred_element_type=jnp.float32
    )
    local_total = jnp.sum(key_feats.astype(jnp.float32), axis=1)
    state_before, total_before = carried_in(
        (local_state, local_total),
        "seq",
        add_pair,
        (jnp.zeros_like(local_state), jnp.zeros_like(local_total)),
    )
    causal = jnp.arange(tokens_dev)[:, None] >= jnp.arange(tokens_dev)[None, :]
    scores = jnp.einsum("uthc,ushc->uhts", queries, key_feats, preferred_element_type=jnp.float32)
    scores = jnp.where(causal, scores, 0.0)
    denominator = jnp.sum(scores, axis=-1) + jnp.einsum(
        "uthc,uhc->uht", queries.astype(jnp.float32), total_before, precision=highest
    )
    numerator = jnp.einsum(
        "uhts,ushc->uthc",
        scores.astype(jnp.bfloat16),
        val_feats,
        preferred_element_type=jnp.float32,
    )
    numerator = numerator + jnp.einsum(
        "uthc,uhcd->uthd",
        queries,
        state_before.astype(jnp.bfloat16),
        preferred_element_type=jnp.float32,
    )
    attended = numerator / jnp.transpose(denominator, (0, 2, 1))[..., None]
    attended = attended.reshape(users_dev, tokens_dev, width)
    partial_value = jnp.sum(jnp.where(valid[..., None], wide + attended, 0.0), axis=1)
    piece_width = width // seq_count
    gain_row = pool_gain[0]
    pooled = lax.psum(partial_value, "seq")
    factor = lax.rsqrt(jnp.mean(pooled * pooled, -1, keepdims=True) + epsilon)
    full_vec = (pooled * factor * gain_row).astype(jnp.bfloat16)
    out_vec = lax.dynamic_slice_in_dim(full_vec, seq_place * piece_width, piece_width, 1)
    group = lax.all_gather(full_vec, "dp", axis=0, tiled=True)
    other = partner_2(group, "domain", 0)
    logits = jnp.einsum("uc,vc->uv", full_vec, other, preferred_element_type=jnp.float32) * (
        logit_scale / width
    )
    users_all = other.shape[0]
    own_index = group_place * users_dev + jnp.arange(users_dev)
    targets = lax.dynamic_slice_in_dim(positives, group_place * users_dev, users_dev)
    forward_pair = targets[:, None] == jnp.arange(users_all)[None, :]
    backward_pair = positives[None, :] == own_index[:, None]
    partner = jnp.where(domain_place == 0, forward_pair, backward_pair)
    loss = jnp.log(jnp.sum(jnp.exp(logits), axis=-1)) - jnp.sum(
        jnp.where(partner, logits, 0.0), axis=-1
    )
    return (out_vec[None], loss[None])


PLANE = 4
PLANES = 4
GROUP = 256
DOT_T = (((0,), (0,)), ((), ()))


def places():
    seq_place = lax.axis_index("seq")
    return lax.div(seq_place, 2), lax.rem(seq_place, 2), lax.axis_index("dp")


def head_sums(a):
    return [
        jnp.sum(a[:, h * HEAD_DIM : (h + 1) * HEAD_DIM], axis=1, keepdims=True)
        for h in range(GROUP // HEAD_DIM)
    ]


def by_head(columns):
    rows = columns[0].shape[0]
    return jnp.concatenate([jnp.broadcast_to(c, (rows, HEAD_DIM)) for c in columns], axis=1)


def split_two(a):
    high = a.astype(jnp.bfloat16)
    return high, (a - high.astype(jnp.float32)).astype(jnp.bfloat16)


def project_kernel(lengths, own, near, across, corner, w_own, w_near, *rest):
    shifted = rest[:6]
    gain, normed, feats, sums, raw, weights, sems = rest[6:]
    tokens, width = own.shape
    wide = 2 * GROUP
    z, x, u = places()
    own_long = lengths[0, 0] > tokens
    long_u = jnp.where(own_long, u, 1 - u)
    blocks = (own, near, across, corner)

    rows = width // (2 * PLANES)
    half_at = (x, 1 - x)
    copies = []
    for half, ref in enumerate((w_own, w_near)):
        at = pl.multiple_of((2 * z + half_at[half]) * rows, rows)
        copies.append((ref.at[:, pl.ds(0, wide)], at))
    for step in range(1, PLANES):
        other = lax.rem(z + PLANES - step, PLANES)
        for half in range(2):
            at = pl.multiple_of((2 * other + half_at[half]) * rows, rows)
            copies.append((shifted[2 * (step - 1) + half], at))
    for i, (ref, at) in enumerate(copies):
        pltpu.make_async_copy(ref, weights.at[pl.ds(at, rows)], sems.at[3 + i]).start()

    for slot in range(3):
        from_x = 1 if slot == 1 else 0
        from_u = 1 - long_u if slot == 2 else long_u
        pick = jnp.bitwise_xor(x, from_x) + 2 * jnp.bitwise_xor(u, from_u)
        for j, ref in enumerate(blocks):

            @pl.when(pick == j)
            def _():
                pltpu.make_async_copy(ref, raw.at[slot], sems.at[slot]).start()

    for i, (ref, at) in enumerate(copies):
        pltpu.make_async_copy(ref, weights.at[pl.ds(at, rows)], sems.at[3 + i]).wait()
    columns = pl.ds(pl.multiple_of((2 * x + u) * GROUP, GROUP), GROUP)

    def one(slot):
        values = raw[slot].astype(jnp.float32)
        scale = lax.rsqrt(jnp.mean(values * values, axis=1, keepdims=True) + epsilon)
        low = (values * scale * gain[...]).astype(jnp.bfloat16)
        normed[pl.ds(slot * tokens, tokens), :] = low
        out = jnp.dot(low, weights[...], preferred_element_type=jnp.float32)
        out = jnp.where(out > 0.0, out + 1.0, jnp.exp(jnp.minimum(out, 0.0))).astype(jnp.bfloat16)
        feats[pl.ds(slot * tokens, tokens), :] = out
        key_total = jnp.sum(out[:, GROUP:].astype(jnp.float32), axis=0, keepdims=True)
        part = raw[slot, :, columns].astype(jnp.float32)
        return key_total, jnp.sum(part, axis=0, keepdims=True)

    for slot in range(3):
        pltpu.make_async_copy(own, raw.at[slot], sems.at[slot]).wait()
    key_one, sum_one = one(0)
    key_two, sum_two = one(1)
    sums[0:1, :] = key_one + key_two
    sums[1:2, :] = sum_one + sum_two
    sums[2:3, :] = jnp.zeros_like(sum_one)

    @pl.when(z == 0)
    def _():
        _, sum_short = one(2)
        sums[2:3, :] = sum_short


def scan_kernel(sums, total_1, total_2, total_3, feats, weight_sum, local):
    tokens = feats.shape[0] // 3
    z, _, _ = places()
    row = lax.broadcasted_iota(jnp.int32, (tokens, tokens), 0)
    col = lax.broadcasted_iota(jnp.int32, (tokens, tokens), 1)
    lower = (row >= col).astype(jnp.bfloat16)
    upper = (row <= col).astype(jnp.bfloat16)
    before = jnp.zeros((1, GROUP), jnp.float32)
    for step, ref in enumerate((total_1, total_2, total_3), 1):
        before = before + jnp.where(z >= step, ref[...], 0.0)

    def block(slot, carry):
        part = pl.ds(slot * tokens, tokens)
        query = feats[part, :GROUP].astype(jnp.float32)
        key = feats[part, GROUP:]
        prefix = jnp.dot(lower, key, preferred_element_type=jnp.float32) + carry
        share = query / by_head(head_sums(query * prefix))
        return share, key, prefix[tokens - 1 : tokens, :]

    def suffix(share):
        high, low = split_two(share)
        return jnp.dot(upper, high, preferred_element_type=jnp.float32) + jnp.dot(
            upper, low, preferred_element_type=jnp.float32
        )

    def store(slot, key, after):
        sums_by_head = head_sums(key.astype(jnp.float32) * after)
        part = pl.ds(slot * tokens, tokens)
        local[part, :] = jnp.concatenate(
            [jnp.broadcast_to(c, (tokens, HEAD_DIM // 2)) for c in sums_by_head], axis=1
        )

    share_one, key_one, carry = block(0, before)
    share_two, key_two, _ = block(1, carry)
    after_two = suffix(share_two)
    after_one = suffix(share_one) + after_two[0:1, :]
    weight_sum[...] = after_one[0:1, :]
    store(0, key_one, after_one)
    store(1, key_two, after_two)

    @pl.when(z == 0)
    def _():
        share, key, _ = block(2, jnp.zeros((1, GROUP), jnp.float32))
        store(2, key, suffix(share))


def pool_kernel(
    lengths, sums, later_1, later_2, later_3, feats, local, normed, v_own, v_near, v_1, v_2, v_3, pooled, values, mixed
):
    tokens = feats.shape[0] // 3
    rows = v_own.shape[0]
    width = normed.shape[1]
    z, x, u = places()
    long_u = jnp.where(lengths[0, 0] > tokens, u, 1 - u)
    at = [pl.multiple_of((2 * z + half) * rows, rows) for half in (x, 1 - x)]
    values[pl.ds(at[0], rows), :] = v_own[...]
    values[pl.ds(at[1], rows), :] = v_near[...]
    for step, ref in enumerate((v_1, v_2, v_3), 1):
        other = lax.rem(z + PLANES - step, PLANES)
        for half, place in enumerate((x, 1 - x)):
            start = pl.multiple_of((2 * other + place) * rows, rows)
            values[pl.ds(start, rows), :] = ref[pl.ds(half * rows, rows), :]

    after = jnp.zeros((1, GROUP), jnp.float32)
    for step, ref in enumerate((later_1, later_2, later_3), 1):
        after = after + jnp.where(z < step, ref[...], 0.0)
    lane = lax.broadcasted_iota(jnp.int32, (1, HEAD_DIM), 1)

    def mix(weight, slot, count):
        high, low = split_two(weight)
        both = jnp.where(lax.rem(lane, 64) < 32, high.astype(jnp.float32), low.astype(jnp.float32))
        part = normed[pl.ds(slot * tokens, count), :]
        return lax.dot_general(both.astype(jnp.bfloat16), part, DOT_T, preferred_element_type=jnp.float32)

    key = feats[0 : 2 * tokens, GROUP:].astype(jnp.float32)
    extra = jnp.concatenate(
        [jnp.broadcast_to(c, (2 * tokens, HEAD_DIM // 2)) for c in head_sums(key * after)], axis=1
    )
    mixed[0:HEAD_DIM, :] = mix(local[0 : 2 * tokens, :] + extra, 0, 2 * tokens)
    mixed[HEAD_DIM:, :] = jnp.zeros((HEAD_DIM, width), jnp.float32)

    @pl.when(z == 0)
    def _():
        mixed[HEAD_DIM:, :] = mix(local[2 * tokens :, :], 2, tokens)

    picked = [mixed[h : h + 1, :] + mixed[h + 32 : h + 33, :] for h in (0, 64, 128, 192)]
    high, low = split_two(jnp.concatenate(picked + picked, axis=0))
    out = jnp.dot(high, values[...], preferred_element_type=jnp.float32) + jnp.dot(
        low, values[...], preferred_element_type=jnp.float32
    )
    half = HEAD_DIM
    long_row = jnp.concatenate([out[0:1, :half], out[1:2, half:]], axis=1) + sums[1:2, :]
    short_row = jnp.concatenate([out[2:3, :half], out[3:4, half:]], axis=1) + sums[2:3, :]
    pooled[0:1, :] = jnp.where(long_u == 0, long_row, short_row)
    pooled[1:2, :] = jnp.where(long_u == 0, short_row, long_row)


def loss_kernel(positives, parts, o_1, o_2, o_3, p_0, p_1, p_2, p_3, gain, gain_other, vec, loss, mine, theirs):
    z, x, u = places()
    domain = lax.axis_index("domain")
    group = 2 * x + u
    width = gain.shape[1]
    piece = vec.shape[2]

    def collect(refs, gains, dest):
        total = jnp.zeros((2, 1), jnp.float32)
        for move, ref in enumerate(refs):
            values = ref[...]
            total = total + jnp.sum(values * values, axis=1, keepdims=True)
            at = pl.multiple_of(jnp.bitwise_xor(group, move) * GROUP, GROUP)
            dest[:, pl.ds(at, GROUP)] = values * gains[:, pl.ds(at, GROUP)]
        factor = lax.rsqrt(total / width + epsilon)
        return (dest[...] * factor).astype(jnp.bfloat16).astype(jnp.float32)

    own = collect((parts, o_1, o_2, o_3), gain, mine)
    other = collect((p_0, p_1, p_2, p_3), gain_other, theirs)
    mine[...] = own
    start = pl.multiple_of((2 * z + x) * piece, piece)
    out = mine[:, pl.ds(start, piece)]
    vec[0] = jnp.where(u == 0, out[0:1], out[1:2]).astype(jnp.bfloat16)
    this = jnp.where(u == 0, own[0:1], own[1:2])
    logits = jnp.sum(this * other, axis=1, keepdims=True) * (logit_scale / width)
    top = jnp.max(logits, axis=0, keepdims=True)
    spread = jnp.log(jnp.sum(jnp.exp(logits - top), axis=0, keepdims=True)) + top
    forward = jnp.where(u == 0, positives[0], positives[1])
    backward = jnp.where(positives[0] == u, 0, 1)
    partner = jnp.where(domain == 0, forward, backward)
    rows = lax.broadcasted_iota(jnp.int32, (2, 1), 0)
    loss[...] = spread - jnp.sum(jnp.where(rows == partner, logits, 0.0), axis=0, keepdims=True)


def vmem():
    return pl.BlockSpec(memory_space=pltpu.VMEM)


def anywhere():
    return pl.BlockSpec(memory_space=pl.ANY)


def smem():
    return pl.BlockSpec(memory_space=pltpu.SMEM)


def call(kernel, outs, in_specs, scratch, flops):
    return pl.pallas_call(
        kernel,
        out_shape=outs,
        in_specs=in_specs,
        out_specs=jax.tree.map(lambda _: vmem(), outs),
        scratch_shapes=scratch,
        compiler_params=pltpu.CompilerParams(vmem_limit_bytes=40 * 1024 * 1024),
        cost_estimate=pl.CostEstimate(flops=flops, bytes_accessed=2**21, transcendentals=0),
    )


def towers(history, qkv_weight, norm_gain, pool_gain, lengths, positives):
    events = history[0, 0]
    tokens, width = events.shape
    weight = qkv_weight[0]
    rows = weight.shape[0]
    f32, bf16 = jnp.float32, jnp.bfloat16
    shape = jax.ShapeDtypeStruct
    z, x, u = places()
    group = 2 * x + u
    here = PLANE * PLANES

    def plane_hop(a, move):
        return lax.ppermute(a, ("seq", "dp"), [(i, i ^ move) for i in range(here)])

    def level_hop(a, step):
        return lax.ppermute(a, ("seq", "dp"), [(i, (i + PLANE * step) % here) for i in range(here)])

    def domain_hop(a, move):
        pairs = [(i, i ^ (2 * move + 1)) for i in range(2 * here)]
        return lax.ppermute(a, ("seq", "dp", "domain"), pairs)

    def columns(which):
        return jnp.concatenate(
            [lax.dynamic_slice(weight, (0, part * width + which * GROUP), (rows, GROUP)) for part in range(3)],
            axis=1,
        )

    near = plane_hop(events, 2)
    across = plane_hop(events, 1)
    corner = plane_hop(events, 3)
    w_own = columns(group)
    w_near = plane_hop(columns(jnp.bitwise_xor(group, 2)), 2)
    shifted = []
    for step in range(1, PLANES):
        shifted.append(level_hop(w_own[:, : 2 * GROUP], step))
        shifted.append(level_hop(w_near[:, : 2 * GROUP], step))
    v_own, v_near = w_own[:, 2 * GROUP :], w_near[:, 2 * GROUP :]
    v_both = jnp.concatenate([v_own, v_near], axis=0)
    v_far = [level_hop(v_both, step) for step in range(1, PLANES)]
    gain_other = domain_hop(pool_gain, 0)

    normed, feats, sums = call(
        project_kernel,
        (shape((3 * tokens, width), bf16), shape((3 * tokens, 2 * GROUP), bf16), shape((8, GROUP), f32)),
        [smem()] + [anywhere()] * 12 + [vmem()],
        [
            pltpu.VMEM((3, tokens, width), bf16),
            pltpu.VMEM((width, 2 * GROUP), bf16),
            pltpu.SemaphoreType.DMA((3 + 2 * PLANES,)),
        ],
        2 * 3 * tokens * width * 2 * GROUP,
    )(lengths, events, near, across, corner, w_own, w_near, *shifted, norm_gain)
    key_total = sums[0:1]
    totals = [level_hop(key_total, step) for step in range(1, PLANES)]
    weight_sum, local = call(
        scan_kernel,
        (shape((1, GROUP), f32), shape((3 * tokens, HEAD_DIM), f32)),
        [vmem()] * 5,
        [],
        2 * 9 * tokens * tokens * GROUP,
    )(sums, *totals, feats)
    later = [level_hop(weight_sum, step) for step in range(1, PLANES)]
    part = call(
        pool_kernel,
        shape((2, GROUP), f32),
        [smem()] + [vmem()] * 12,
        [pltpu.VMEM((width, GROUP), bf16), pltpu.VMEM((2 * HEAD_DIM, width), f32)],
        2 * 3 * tokens * width * HEAD_DIM,
    )(lengths, sums, *later, feats, local, normed, v_own, v_near, *v_far)
    part = part + level_hop(part, 1) + level_hop(part, 2) + level_hop(part, 3)
    own = [plane_hop(part, move) for move in range(1, PLANE)]
    other = [domain_hop(part, move) for move in range(PLANE)]
    vec, loss = call(
        loss_kernel,
        (shape((1, 1, width // 8), bf16), shape((1, 1), f32)),
        [smem()] + [vmem()] * 10,
        [pltpu.VMEM((2, width), f32), pltpu.VMEM((2, width), f32)],
        2**14,
    )(positives, part, *own, *other, pool_gain, gain_other)
    return vec, loss


def solution(mesh):
    placed = (
        P("domain", "dp", "seq", None),
        P("domain", "seq", None),
        P("domain", None),
        P("domain", None),
        P("domain", "dp"),
        P(),
    )
    small = mesh.shape["seq"] == 2 * PLANES and mesh.shape["dp"] == 2
    return jax.shard_map(
        towers if small else shards,
        mesh=mesh,
        in_specs=placed,
        out_specs=(P("domain", "dp", "seq"), P("domain", "dp")),
        check_vma=False,
    )
```

```python
import functools

import jax
import jax.numpy as jnp
from jax import lax
from jax.experimental import pallas as pl
from jax.experimental.pallas import tpu as pltpu
from jax.sharding import PartitionSpec as P

HEADS = 8
HEAD_DIM = 128


logit_scale = 20.0
epsilon = 1e-06
highest = lax.Precision.HIGHEST


def carried_in(part, axis, combine, identity):
    place = lax.axis_index(axis)
    gathered = jax.tree.map(lambda a: lax.all_gather(a, axis), part)
    state = jax.tree.map(lambda a, e: jnp.zeros_like(a) + jnp.asarray(e, a.dtype), part, identity)

    def one(hop, state):
        return combine(
            state, jax.tree.map(lambda a: lax.dynamic_index_in_dim(a, hop, 0, False), gathered)
        )

    return lax.fori_loop(0, place, one, state)


def partner_2(block, axis, stride):
    count = lax.axis_size(axis)
    route = []
    for low in range(count):
        high = low | 1 << stride
        if high != low and high < count:
            route += [(low, high), (high, low)]
    return lax.ppermute(block, axis, route)


def feature_map(values):
    return jax.nn.elu(values) + 1.0


def add_pair(earlier, later):
    return (earlier[0] + later[0], earlier[1] + later[1])


def shards(history, qkv_weight, norm_gain, pool_gain, lengths, positives):
    seq_count = lax.axis_size("seq")
    seq_place = lax.axis_index("seq")
    group_place = lax.axis_index("dp")
    domain_place = lax.axis_index("domain")
    events = history[0]
    users_dev, tokens_dev, width = events.shape
    row_count = users_dev * tokens_dev
    wide = events.astype(jnp.float32)
    normed = (
        wide * lax.rsqrt(jnp.mean(wide * wide, -1, keepdims=True) + epsilon) * norm_gain[0]
    ).astype(jnp.bfloat16)
    normed = normed.reshape(row_count, width)
    rows_here = qkv_weight[0]
    projected = jnp.dot(
        normed,
        lax.all_gather(rows_here, "seq", axis=0, tiled=True),
        preferred_element_type=jnp.float32,
    )
    query_raw = projected[:, :width]
    key_raw = projected[:, width : 2 * width]
    value_raw = projected[:, 2 * width :]
    positions = seq_place * tokens_dev + jnp.arange(tokens_dev)
    valid = positions[None, :] < lengths[0][:, None]
    shape_heads = (users_dev, tokens_dev, HEADS, HEAD_DIM)
    queries = feature_map(query_raw).astype(jnp.bfloat16).reshape(shape_heads)
    key_feats = (
        jnp.where(valid.reshape(row_count)[:, None], feature_map(key_raw), 0.0)
        .astype(jnp.bfloat16)
        .reshape(shape_heads)
    )
    val_feats = value_raw.astype(jnp.bfloat16).reshape(shape_heads)
    local_state = jnp.einsum(
        "uthc,uthd->uhcd", key_feats, val_feats, preferred_element_type=jnp.float32
    )
    local_total = jnp.sum(key_feats.astype(jnp.float32), axis=1)
    state_before, total_before = carried_in(
        (local_state, local_total),
        "seq",
        add_pair,
        (jnp.zeros_like(local_state), jnp.zeros_like(local_total)),
    )
    causal = jnp.arange(tokens_dev)[:, None] >= jnp.arange(tokens_dev)[None, :]
    scores = jnp.einsum("uthc,ushc->uhts", queries, key_feats, preferred_element_type=jnp.float32)
    scores = jnp.where(causal, scores, 0.0)
    denominator = jnp.sum(scores, axis=-1) + jnp.einsum(
        "uthc,uhc->uht", queries.astype(jnp.float32), total_before, precision=highest
    )
    numerator = jnp.einsum(
        "uhts,ushc->uthc",
        scores.astype(jnp.bfloat16),
        val_feats,
        preferred_element_type=jnp.float32,
    )
    numerator = numerator + jnp.einsum(
        "uthc,uhcd->uthd",
        queries,
        state_before.astype(jnp.bfloat16),
        preferred_element_type=jnp.float32,
    )
    attended = numerator / jnp.transpose(denominator, (0, 2, 1))[..., None]
    attended = attended.reshape(users_dev, tokens_dev, width)
    partial_value = jnp.sum(jnp.where(valid[..., None], wide + attended, 0.0), axis=1)
    piece_width = width // seq_count
    gain_row = pool_gain[0]
    pooled = lax.psum(partial_value, "seq")
    factor = lax.rsqrt(jnp.mean(pooled * pooled, -1, keepdims=True) + epsilon)
    full_vec = (pooled * factor * gain_row).astype(jnp.bfloat16)
    out_vec = lax.dynamic_slice_in_dim(full_vec, seq_place * piece_width, piece_width, 1)
    group = lax.all_gather(full_vec, "dp", axis=0, tiled=True)
    other = partner_2(group, "domain", 0)
    logits = jnp.einsum("uc,vc->uv", full_vec, other, preferred_element_type=jnp.float32) * (
        logit_scale / width
    )
    users_all = other.shape[0]
    own_index = group_place * users_dev + jnp.arange(users_dev)
    targets = lax.dynamic_slice_in_dim(positives, group_place * users_dev, users_dev)
    forward_pair = targets[:, None] == jnp.arange(users_all)[None, :]
    backward_pair = positives[None, :] == own_index[:, None]
    partner = jnp.where(domain_place == 0, forward_pair, backward_pair)
    loss = jnp.log(jnp.sum(jnp.exp(logits), axis=-1)) - jnp.sum(
        jnp.where(partner, logits, 0.0), axis=-1
    )
    return (out_vec[None], loss[None])


PLANE = 4
PLANES = 4
GROUP = 256
DOT_T = (((0,), (0,)), ((), ()))


def places():
    seq_place = lax.axis_index("seq")
    return lax.div(seq_place, 2), lax.rem(seq_place, 2), lax.axis_index("dp")


def head_sums(a):
    return [
        jnp.sum(a[:, h * HEAD_DIM : (h + 1) * HEAD_DIM], axis=1, keepdims=True)
        for h in range(GROUP // HEAD_DIM)
    ]


def by_head(columns):
    rows = columns[0].shape[0]
    return jnp.concatenate([jnp.broadcast_to(c, (rows, HEAD_DIM)) for c in columns], axis=1)


def split_two(a):
    high = a.astype(jnp.bfloat16)
    return high, (a - high.astype(jnp.float32)).astype(jnp.bfloat16)


def project_kernel(lengths, own, near, across, corner, w_own, w_near, *rest):
    shifted = rest[:6]
    gain, normed, feats, totals, sums, raw, weights, sems = rest[6:]
    tokens, width = own.shape
    wide = 2 * GROUP
    z, x, u = places()
    own_long = lengths[0, 0] > tokens
    long_u = jnp.where(own_long, u, 1 - u)
    blocks = (own, near, across, corner)

    rows = width // (2 * PLANES)
    half_at = (x, 1 - x)
    copies = []
    for half, ref in enumerate((w_own, w_near)):
        at = pl.multiple_of((2 * z + half_at[half]) * rows, rows)
        copies.append((ref.at[:, pl.ds(0, wide)], at))
    for step in range(1, PLANES):
        other = lax.rem(z + PLANES - step, PLANES)
        for half in range(2):
            at = pl.multiple_of((2 * other + half_at[half]) * rows, rows)
            copies.append((shifted[2 * (step - 1) + half], at))
    for i, (ref, at) in enumerate(copies):
        pltpu.make_async_copy(ref, weights.at[pl.ds(at, rows)], sems.at[3 + i]).start()

    for slot in range(3):
        from_x = 1 if slot == 1 else 0
        from_u = 1 - long_u if slot == 2 else long_u
        pick = jnp.bitwise_xor(x, from_x) + 2 * jnp.bitwise_xor(u, from_u)
        for j, ref in enumerate(blocks):

            @pl.when(pick == j)
            def _():
                pltpu.make_async_copy(ref, raw.at[slot], sems.at[slot]).start()

    for i, (ref, at) in enumerate(copies):
        pltpu.make_async_copy(ref, weights.at[pl.ds(at, rows)], sems.at[3 + i]).wait()
    columns = pl.ds(pl.multiple_of((2 * x + u) * GROUP, GROUP), GROUP)

    def one(slot):
        values = raw[slot].astype(jnp.float32)
        scale = lax.rsqrt(jnp.mean(values * values, axis=1, keepdims=True) + epsilon)
        low = (values * scale * gain[...]).astype(jnp.bfloat16)
        normed[pl.ds(slot * tokens, tokens), :] = low
        out = jnp.dot(low, weights[...], preferred_element_type=jnp.float32)
        out = jnp.where(out > 0.0, out + 1.0, jnp.exp(jnp.minimum(out, 0.0))).astype(jnp.bfloat16)
        feats[pl.ds(slot * tokens, tokens), :] = out
        key_total = jnp.sum(out[:, GROUP:].astype(jnp.float32), axis=0, keepdims=True)
        part = raw[slot, :, columns].astype(jnp.float32)
        return key_total, jnp.sum(part, axis=0, keepdims=True)

    for slot in range(3):
        pltpu.make_async_copy(own, raw.at[slot], sems.at[slot]).wait()
    key_one, sum_one = one(0)
    key_two, sum_two = one(1)
    totals[...] = jnp.broadcast_to((key_one + key_two)[None], totals.shape)
    sums[0:1, :] = sum_one + sum_two
    sums[1:2, :] = jnp.zeros_like(sum_one)

    @pl.when(z == 0)
    def _():
        _, sum_short = one(2)
        sums[1:2, :] = sum_short


def scan_kernel(totals, feats, weight_sum, local):
    tokens = feats.shape[0] // 3
    z, _, _ = places()
    row = lax.broadcasted_iota(jnp.int32, (tokens, tokens), 0)
    col = lax.broadcasted_iota(jnp.int32, (tokens, tokens), 1)
    lower = (row >= col).astype(jnp.bfloat16)
    upper = (row <= col).astype(jnp.bfloat16)
    before = jnp.zeros((1, GROUP), jnp.float32)
    for plane in range(PLANES - 1):
        before = before + jnp.where(plane < z, totals[plane], 0.0)

    def block(slot, carry):
        part = pl.ds(slot * tokens, tokens)
        query = feats[part, :GROUP].astype(jnp.float32)
        key = feats[part, GROUP:]
        prefix = jnp.dot(lower, key, preferred_element_type=jnp.float32) + carry
        share = query / by_head(head_sums(query * prefix))
        return share, key, prefix[tokens - 1 : tokens, :]

    def suffix(share):
        high, low = split_two(share)
        return jnp.dot(upper, high, preferred_element_type=jnp.float32) + jnp.dot(
            upper, low, preferred_element_type=jnp.float32
        )

    def store(slot, key, after):
        sums_by_head = head_sums(key.astype(jnp.float32) * after)
        part = pl.ds(slot * tokens, tokens)
        local[part, :] = jnp.concatenate(
            [jnp.broadcast_to(c, (tokens, HEAD_DIM // 2)) for c in sums_by_head], axis=1
        )

    share_one, key_one, carry = block(0, before)
    share_two, key_two, _ = block(1, carry)
    after_two = suffix(share_two)
    after_one = suffix(share_one) + after_two[0:1, :]
    weight_sum[...] = jnp.broadcast_to(after_one[0:1, :][None], weight_sum.shape)
    store(0, key_one, after_one)
    store(1, key_two, after_two)

    @pl.when(z == 0)
    def _():
        share, key, _ = block(2, jnp.zeros((1, GROUP), jnp.float32))
        store(2, key, suffix(share))


def mix_kernel(later, feats, local, normed, mixed):
    tokens = feats.shape[0] // 3
    z, _, _ = places()
    after = jnp.zeros((1, GROUP), jnp.float32)
    for plane in range(1, PLANES):
        after = after + jnp.where(plane > z, later[plane], 0.0)
    lane = lax.broadcasted_iota(jnp.int32, (1, HEAD_DIM), 1)

    def mix(weight, slot, count):
        high, low = split_two(weight)
        both = jnp.where(lax.rem(lane, 64) < 32, high.astype(jnp.float32), low.astype(jnp.float32))
        part = normed[pl.ds(slot * tokens, count), :]
        out = lax.dot_general(both.astype(jnp.bfloat16), part, DOT_T, preferred_element_type=jnp.float32)
        return [out[h : h + 1, :] + out[h + 32 : h + 33, :] for h in (0, 64)]

    def store(row, values):
        for plane in range(PLANES):
            mixed[plane, row : row + 1, :] = values[:, plane * GROUP : (plane + 1) * GROUP]

    key = feats[0 : 2 * tokens, GROUP:].astype(jnp.float32)
    extra = jnp.concatenate(
        [jnp.broadcast_to(c, (2 * tokens, HEAD_DIM // 2)) for c in head_sums(key * after)], axis=1
    )
    for row, values in enumerate(mix(local[0 : 2 * tokens, :] + extra, 0, 2 * tokens)):
        store(row, values)
    mixed[:, 2:, :] = jnp.zeros((PLANES, 2, GROUP), jnp.float32)

    @pl.when(z == 0)
    def _():
        for row, values in enumerate(mix(local[2 * tokens :, :], 2, tokens)):
            store(2 + row, values)


def pool_kernel(lengths, tokens, sums, mixed, v_own, v_near, gain, part, values):
    rows = v_own.shape[0]
    _, x, u = places()
    long_u = jnp.where(lengths[0, 0] > tokens, u, 1 - u)
    for half, ref in ((x, v_own), (1 - x, v_near)):
        values[pl.ds(pl.multiple_of(half * rows, rows), rows), :] = ref[...]
    total = (mixed[0] + mixed[1]) + (mixed[2] + mixed[3])
    high, low = split_two(jnp.concatenate([total, total], axis=0))
    out = jnp.dot(high, values[...], preferred_element_type=jnp.float32) + jnp.dot(
        low, values[...], preferred_element_type=jnp.float32
    )
    half = HEAD_DIM
    long_row = jnp.concatenate([out[0:1, :half], out[1:2, half:]], axis=1) + sums[0:1, :]
    short_row = jnp.concatenate([out[2:3, :half], out[3:4, half:]], axis=1) + sums[1:2, :]
    first = jnp.where(long_u == 0, long_row, short_row)
    second = jnp.where(long_u == 0, short_row, long_row)
    columns = pl.ds(pl.multiple_of((2 * x + u) * GROUP, GROUP), GROUP)
    own_gain = gain[:, columns]
    block = jnp.concatenate([first, second, own_gain, own_gain], axis=0)
    part[...] = jnp.broadcast_to(block[None], part.shape)


def loss_kernel(positives, parts, vec, loss, mine, theirs):
    z, x, u = places()
    domain = lax.axis_index("domain")
    width = mine.shape[1]
    piece = vec.shape[2]

    def collect(place, dest):
        total = jnp.zeros((2, 1), jnp.float32)
        for group in range(PLANE):
            blocks = [parts[2 * (PLANE * plane + group) + place] for plane in range(PLANES)]
            values = (blocks[0][:2] + blocks[1][:2]) + (blocks[2][:2] + blocks[3][:2])
            total = total + jnp.sum(values * values, axis=1, keepdims=True)
            dest[:, group * GROUP : (group + 1) * GROUP] = values * blocks[0][2:3]
        factor = lax.rsqrt(total / width + epsilon)
        return (dest[...] * factor).astype(jnp.bfloat16).astype(jnp.float32)

    own = collect(domain, mine)
    other = collect(1 - domain, theirs)
    mine[...] = own
    start = pl.multiple_of((2 * z + x) * piece, piece)
    out = mine[:, pl.ds(start, piece)]
    vec[0] = jnp.where(u == 0, out[0:1], out[1:2]).astype(jnp.bfloat16)
    this = jnp.where(u == 0, own[0:1], own[1:2])
    logits = jnp.sum(this * other, axis=1, keepdims=True) * (logit_scale / width)
    top = jnp.max(logits, axis=0, keepdims=True)
    spread = jnp.log(jnp.sum(jnp.exp(logits - top), axis=0, keepdims=True)) + top
    forward = jnp.where(u == 0, positives[0], positives[1])
    backward = jnp.where(positives[0] == u, 0, 1)
    partner = jnp.where(domain == 0, forward, backward)
    rows = lax.broadcasted_iota(jnp.int32, (2, 1), 0)
    loss[...] = spread - jnp.sum(jnp.where(rows == partner, logits, 0.0), axis=0, keepdims=True)


def vmem():
    return pl.BlockSpec(memory_space=pltpu.VMEM)


def anywhere():
    return pl.BlockSpec(memory_space=pl.ANY)


def smem():
    return pl.BlockSpec(memory_space=pltpu.SMEM)


def call(kernel, outs, in_specs, scratch, flops):
    return pl.pallas_call(
        kernel,
        out_shape=outs,
        in_specs=in_specs,
        out_specs=jax.tree.map(lambda _: vmem(), outs),
        scratch_shapes=scratch,
        compiler_params=pltpu.CompilerParams(vmem_limit_bytes=40 * 1024 * 1024),
        cost_estimate=pl.CostEstimate(flops=flops, bytes_accessed=2**21, transcendentals=0),
    )


def towers(history, qkv_weight, norm_gain, pool_gain, lengths, positives):
    events = history[0, 0]
    tokens, width = events.shape
    weight = qkv_weight[0]
    rows = weight.shape[0]
    f32, bf16 = jnp.float32, jnp.bfloat16
    shape = jax.ShapeDtypeStruct
    z, x, u = places()
    group = 2 * x + u
    here = PLANE * PLANES

    def plane_hop(a, move):
        return lax.ppermute(a, ("seq", "dp"), [(i, i ^ move) for i in range(here)])

    def level_hop(a, step):
        return lax.ppermute(a, ("seq", "dp"), [(i, (i + PLANE * step) % here) for i in range(here)])

    def swap(a, axes, groups=None):
        return lax.all_to_all(a, axes, 0, 0, axis_index_groups=groups, tiled=True)

    levels = [[2 * plane + half for plane in range(PLANES)] for half in range(2)]

    def columns(which):
        return jnp.concatenate(
            [lax.dynamic_slice(weight, (0, part * width + which * GROUP), (rows, GROUP)) for part in range(3)],
            axis=1,
        )

    near = plane_hop(events, 2)
    across = plane_hop(events, 1)
    corner = plane_hop(events, 3)
    w_own = columns(group)
    w_near = plane_hop(columns(jnp.bitwise_xor(group, 2)), 2)
    shifted = []
    for step in range(1, PLANES):
        shifted.append(level_hop(w_own[:, : 2 * GROUP], step))
        shifted.append(level_hop(w_near[:, : 2 * GROUP], step))
    v_own, v_near = w_own[:, 2 * GROUP :], w_near[:, 2 * GROUP :]

    normed, feats, totals, sums = call(
        project_kernel,
        (
            shape((3 * tokens, width), bf16),
            shape((3 * tokens, 2 * GROUP), bf16),
            shape((PLANES, 1, GROUP), f32),
            shape((2, GROUP), f32),
        ),
        [smem()] + [anywhere()] * 12 + [vmem()],
        [
            pltpu.VMEM((3, tokens, width), bf16),
            pltpu.VMEM((width, 2 * GROUP), bf16),
            pltpu.SemaphoreType.DMA((3 + 2 * PLANES,)),
        ],
        2 * 3 * tokens * width * 2 * GROUP,
    )(lengths, events, near, across, corner, w_own, w_near, *shifted, norm_gain)
    totals = swap(totals, "seq", levels)
    weight_sum, local = call(
        scan_kernel,
        (shape((PLANES, 1, GROUP), f32), shape((3 * tokens, HEAD_DIM), f32)),
        [vmem()] * 2,
        [],
        2 * 9 * tokens * tokens * GROUP,
    )(totals, feats)
    later = swap(weight_sum, "seq", levels)
    mixed = call(
        mix_kernel,
        shape((PLANES, 4, GROUP), f32),
        [vmem()] * 4,
        [],
        2 * 3 * tokens * width * HEAD_DIM,
    )(later, feats, local, normed)
    mixed = swap(mixed, "seq", levels)
    part = call(
        lambda lengths, *refs: pool_kernel(lengths, tokens, *refs),
        shape((2 * here, 4, GROUP), f32),
        [smem()] + [vmem()] * 5,
        [pltpu.VMEM((GROUP, GROUP), bf16)],
        2 * 8 * GROUP * GROUP,
    )(lengths, sums, mixed, v_own, v_near, pool_gain)
    parts = swap(part, ("seq", "dp", "domain"))
    vec, loss = call(
        loss_kernel,
        (shape((1, 1, width // 8), bf16), shape((1, 1), f32)),
        [smem(), vmem()],
        [pltpu.VMEM((2, width), f32), pltpu.VMEM((2, width), f32)],
        2**14,
    )(positives, parts)
    return vec, loss


def solution(mesh):
    placed = (
        P("domain", "dp", "seq", None),
        P("domain", "seq", None),
        P("domain", None),
        P("domain", None),
        P("domain", "dp"),
        P(),
    )
    small = mesh.shape["seq"] == 2 * PLANES and mesh.shape["dp"] == 2
    return jax.shard_map(
        towers if small else shards,
        mesh=mesh,
        in_specs=placed,
        out_specs=(P("domain", "dp", "seq"), P("domain", "dp")),
        check_vma=False,
    )
```

```python
import functools

import jax
import jax.numpy as jnp
from jax import lax
from jax.experimental import pallas as pl
from jax.experimental.pallas import tpu as pltpu
from jax.sharding import PartitionSpec as P

HEADS = 8
HEAD_DIM = 128


logit_scale = 20.0
epsilon = 1e-06
highest = lax.Precision.HIGHEST


def carried_in(part, axis, combine, identity):
    place = lax.axis_index(axis)
    gathered = jax.tree.map(lambda a: lax.all_gather(a, axis), part)
    state = jax.tree.map(lambda a, e: jnp.zeros_like(a) + jnp.asarray(e, a.dtype), part, identity)

    def one(hop, state):
        return combine(
            state, jax.tree.map(lambda a: lax.dynamic_index_in_dim(a, hop, 0, False), gathered)
        )

    return lax.fori_loop(0, place, one, state)


def partner_2(block, axis, stride):
    count = lax.axis_size(axis)
    route = []
    for low in range(count):
        high = low | 1 << stride
        if high != low and high < count:
            route += [(low, high), (high, low)]
    return lax.ppermute(block, axis, route)


def feature_map(values):
    return jax.nn.elu(values) + 1.0


def add_pair(earlier, later):
    return (earlier[0] + later[0], earlier[1] + later[1])


def shards(history, qkv_weight, norm_gain, pool_gain, lengths, positives):
    seq_count = lax.axis_size("seq")
    seq_place = lax.axis_index("seq")
    group_place = lax.axis_index("dp")
    domain_place = lax.axis_index("domain")
    events = history[0]
    users_dev, tokens_dev, width = events.shape
    row_count = users_dev * tokens_dev
    wide = events.astype(jnp.float32)
    normed = (
        wide * lax.rsqrt(jnp.mean(wide * wide, -1, keepdims=True) + epsilon) * norm_gain[0]
    ).astype(jnp.bfloat16)
    normed = normed.reshape(row_count, width)
    rows_here = qkv_weight[0]
    projected = jnp.dot(
        normed,
        lax.all_gather(rows_here, "seq", axis=0, tiled=True),
        preferred_element_type=jnp.float32,
    )
    query_raw = projected[:, :width]
    key_raw = projected[:, width : 2 * width]
    value_raw = projected[:, 2 * width :]
    positions = seq_place * tokens_dev + jnp.arange(tokens_dev)
    valid = positions[None, :] < lengths[0][:, None]
    shape_heads = (users_dev, tokens_dev, HEADS, HEAD_DIM)
    queries = feature_map(query_raw).astype(jnp.bfloat16).reshape(shape_heads)
    key_feats = (
        jnp.where(valid.reshape(row_count)[:, None], feature_map(key_raw), 0.0)
        .astype(jnp.bfloat16)
        .reshape(shape_heads)
    )
    val_feats = value_raw.astype(jnp.bfloat16).reshape(shape_heads)
    local_state = jnp.einsum(
        "uthc,uthd->uhcd", key_feats, val_feats, preferred_element_type=jnp.float32
    )
    local_total = jnp.sum(key_feats.astype(jnp.float32), axis=1)
    state_before, total_before = carried_in(
        (local_state, local_total),
        "seq",
        add_pair,
        (jnp.zeros_like(local_state), jnp.zeros_like(local_total)),
    )
    causal = jnp.arange(tokens_dev)[:, None] >= jnp.arange(tokens_dev)[None, :]
    scores = jnp.einsum("uthc,ushc->uhts", queries, key_feats, preferred_element_type=jnp.float32)
    scores = jnp.where(causal, scores, 0.0)
    denominator = jnp.sum(scores, axis=-1) + jnp.einsum(
        "uthc,uhc->uht", queries.astype(jnp.float32), total_before, precision=highest
    )
    numerator = jnp.einsum(
        "uhts,ushc->uthc",
        scores.astype(jnp.bfloat16),
        val_feats,
        preferred_element_type=jnp.float32,
    )
    numerator = numerator + jnp.einsum(
        "uthc,uhcd->uthd",
        queries,
        state_before.astype(jnp.bfloat16),
        preferred_element_type=jnp.float32,
    )
    attended = numerator / jnp.transpose(denominator, (0, 2, 1))[..., None]
    attended = attended.reshape(users_dev, tokens_dev, width)
    partial_value = jnp.sum(jnp.where(valid[..., None], wide + attended, 0.0), axis=1)
    piece_width = width // seq_count
    gain_row = pool_gain[0]
    pooled = lax.psum(partial_value, "seq")
    factor = lax.rsqrt(jnp.mean(pooled * pooled, -1, keepdims=True) + epsilon)
    full_vec = (pooled * factor * gain_row).astype(jnp.bfloat16)
    out_vec = lax.dynamic_slice_in_dim(full_vec, seq_place * piece_width, piece_width, 1)
    group = lax.all_gather(full_vec, "dp", axis=0, tiled=True)
    other = partner_2(group, "domain", 0)
    logits = jnp.einsum("uc,vc->uv", full_vec, other, preferred_element_type=jnp.float32) * (
        logit_scale / width
    )
    users_all = other.shape[0]
    own_index = group_place * users_dev + jnp.arange(users_dev)
    targets = lax.dynamic_slice_in_dim(positives, group_place * users_dev, users_dev)
    forward_pair = targets[:, None] == jnp.arange(users_all)[None, :]
    backward_pair = positives[None, :] == own_index[:, None]
    partner = jnp.where(domain_place == 0, forward_pair, backward_pair)
    loss = jnp.log(jnp.sum(jnp.exp(logits), axis=-1)) - jnp.sum(
        jnp.where(partner, logits, 0.0), axis=-1
    )
    return (out_vec[None], loss[None])


PLANE = 4
PLANES = 4
GROUP = 256
DOT_T = (((0,), (0,)), ((), ()))


def places():
    seq_place = lax.axis_index("seq")
    return lax.div(seq_place, 2), lax.rem(seq_place, 2), lax.axis_index("dp")


def head_sums(a):
    return [
        jnp.sum(a[:, h * HEAD_DIM : (h + 1) * HEAD_DIM], axis=1, keepdims=True)
        for h in range(GROUP // HEAD_DIM)
    ]


def by_head(columns):
    rows = columns[0].shape[0]
    return jnp.concatenate([jnp.broadcast_to(c, (rows, HEAD_DIM)) for c in columns], axis=1)


def split_two(a):
    high = a.astype(jnp.bfloat16)
    return high, (a - high.astype(jnp.float32)).astype(jnp.bfloat16)


def norm_kernel(lengths, own, near, across, corner_a, corner_b, gain, normed, sums, raw, sems):
    tokens = own.shape[0]
    half = corner_a.shape[0]
    z, x, u = places()
    long_u = jnp.where(lengths[0, 0] > tokens, u, 1 - u)

    def fetch(slot, pick):
        for j, ref in enumerate((own, near, across)):

            @pl.when(pick == j)
            def _():
                pltpu.make_async_copy(ref.at[pl.ds(0, half)], raw.at[slot, pl.ds(0, half)], sems.at[slot, 0]).start()
                pltpu.make_async_copy(ref.at[pl.ds(half, half)], raw.at[slot, pl.ds(half, half)], sems.at[slot, 1]).start()

        @pl.when(pick == 3)
        def _():
            pltpu.make_async_copy(corner_a, raw.at[slot, pl.ds(0, half)], sems.at[slot, 0]).start()
            pltpu.make_async_copy(corner_b, raw.at[slot, pl.ds(half, half)], sems.at[slot, 1]).start()

    for slot in range(3):
        from_x = 1 if slot == 1 else 0
        from_u = 1 - long_u if slot == 2 else long_u
        fetch(slot, jnp.bitwise_xor(x, from_x) + 2 * jnp.bitwise_xor(u, from_u))
    columns = pl.ds(pl.multiple_of((2 * x + u) * GROUP, GROUP), GROUP)

    def one(slot):
        values = raw[slot].astype(jnp.float32)
        scale = lax.rsqrt(jnp.mean(values * values, axis=1, keepdims=True) + epsilon)
        normed[pl.ds(slot * tokens, tokens), :] = (values * scale * gain[...]).astype(jnp.bfloat16)
        return jnp.sum(raw[slot, :, columns].astype(jnp.float32), axis=0, keepdims=True)

    for slot in range(3):
        for part in range(2):
            at = pl.ds(part * half, half)
            pltpu.make_async_copy(own.at[at], raw.at[slot, at], sems.at[slot, part]).wait()
    sums[0:1, :] = one(0) + one(1)
    sums[1:2, :] = jnp.zeros((1, GROUP), jnp.float32)

    @pl.when(z == 0)
    def _():
        sums[1:2, :] = one(2)


def gather_rows(z, x, parts, dest):
    rows = parts[0].shape[0] // 2
    for j, ref in enumerate(parts):
        plane = jnp.bitwise_xor(z, j)
        for half, place in enumerate((x, 1 - x)):
            start = pl.multiple_of((2 * plane + place) * rows, rows)
            dest[pl.ds(start, rows), :] = ref[pl.ds(half * rows, rows), :]


def project_kernel(normed, own, one_away, two_own, two_near, next_plane, far, feats, totals, weights):
    tokens = normed.shape[0] // 3
    rows = two_own.shape[0]
    z, x, _ = places()

    def put(plane, place, values):
        weights[pl.ds(pl.multiple_of((2 * plane + place) * rows, rows), rows), :] = values

    def put_both(plane, ref):
        put(plane, x, ref[:rows, :])
        put(plane, 1 - x, ref[rows:, :])

    put_both(z, own)
    put_both(jnp.bitwise_xor(z, 1), one_away)
    put(jnp.bitwise_xor(z, 2), x, two_own[...])
    put(jnp.bitwise_xor(z, 2), 1 - x, two_near[...])
    inner = jnp.logical_or(z == 1, z == 2)

    @pl.when(inner)
    def _():
        put_both(3 - z, next_plane)

    @pl.when(jnp.logical_not(inner))
    def _():
        put_both(3 - z, far)

    def one(slot, count):
        part = pl.ds(slot * tokens, count)
        out = jnp.dot(normed[part, :], weights[...], preferred_element_type=jnp.float32)
        out = jnp.where(out > 0.0, out + 1.0, jnp.exp(jnp.minimum(out, 0.0))).astype(jnp.bfloat16)
        feats[part, :] = out
        return jnp.sum(out[:, GROUP:].astype(jnp.float32), axis=0, keepdims=True)

    totals[...] = one(0, tokens) + one(1, tokens)

    @pl.when(z == 0)
    def _():
        one(2, tokens)


def scan_kernel(before_1, before_2, before_3, feats, weight_sum, local):
    tokens = feats.shape[0] // 3
    z, _, _ = places()
    row = lax.broadcasted_iota(jnp.int32, (tokens, tokens), 0)
    col = lax.broadcasted_iota(jnp.int32, (tokens, tokens), 1)
    lower = (row >= col).astype(jnp.bfloat16)
    upper = (row <= col).astype(jnp.bfloat16)
    before = before_1[...] + before_2[...] + before_3[...]

    def block(slot, carry):
        part = pl.ds(slot * tokens, tokens)
        query = feats[part, :GROUP].astype(jnp.float32)
        key = feats[part, GROUP:]
        prefix = jnp.dot(lower, key, preferred_element_type=jnp.float32) + carry
        share = query / by_head(head_sums(query * prefix))
        return share, key, prefix[tokens - 1 : tokens, :]

    def suffix(share):
        high, low = split_two(share)
        return jnp.dot(upper, high, preferred_element_type=jnp.float32) + jnp.dot(
            upper, low, preferred_element_type=jnp.float32
        )

    def store(slot, key, after):
        sums_by_head = head_sums(key.astype(jnp.float32) * after)
        part = pl.ds(slot * tokens, tokens)
        local[part, :] = jnp.concatenate(
            [jnp.broadcast_to(c, (tokens, HEAD_DIM // 2)) for c in sums_by_head], axis=1
        )

    share_one, key_one, carry = block(0, before)
    share_two, key_two, _ = block(1, carry)
    after_two = suffix(share_two)
    after_one = suffix(share_one) + after_two[0:1, :]
    weight_sum[...] = after_one[0:1, :]
    store(0, key_one, after_one)
    store(1, key_two, after_two)

    @pl.when(z == 0)
    def _():
        share, key, _ = block(2, jnp.zeros((1, GROUP), jnp.float32))
        store(2, key, suffix(share))


def pool_kernel(
    lengths, later_1, later_2, later_3, sums, feats, local, normed, v_own, v_1, v_2, v_3, gain, part, values, mixed
):
    tokens = feats.shape[0] // 3
    width = normed.shape[1]
    z, x, u = places()
    long_u = jnp.where(lengths[0, 0] > tokens, u, 1 - u)
    gather_rows(z, x, (v_own, v_1, v_2, v_3), values)
    after = later_1[...] + later_2[...] + later_3[...]
    lane = lax.broadcasted_iota(jnp.int32, (1, HEAD_DIM), 1)

    def mix(weight, slot, count):
        high, low = split_two(weight)
        both = jnp.where(lax.rem(lane, 64) < 32, high.astype(jnp.float32), low.astype(jnp.float32))
        rows = normed[pl.ds(slot * tokens, count), :]
        return lax.dot_general(both.astype(jnp.bfloat16), rows, DOT_T, preferred_element_type=jnp.float32)

    key = feats[0 : 2 * tokens, GROUP:].astype(jnp.float32)
    extra = jnp.concatenate(
        [jnp.broadcast_to(c, (2 * tokens, HEAD_DIM // 2)) for c in head_sums(key * after)], axis=1
    )
    mixed[0:HEAD_DIM, :] = mix(local[0 : 2 * tokens, :] + extra, 0, 2 * tokens)
    mixed[HEAD_DIM:, :] = jnp.zeros((HEAD_DIM, width), jnp.float32)

    @pl.when(z == 0)
    def _():
        mixed[HEAD_DIM:, :] = mix(local[2 * tokens :, :], 2, tokens)

    picked = [mixed[h : h + 1, :] + mixed[h + 32 : h + 33, :] for h in (0, 64, 128, 192)]
    high, low = split_two(jnp.concatenate(picked + picked, axis=0))
    out = jnp.dot(high, values[...], preferred_element_type=jnp.float32) + jnp.dot(
        low, values[...], preferred_element_type=jnp.float32
    )
    half = HEAD_DIM
    long_row = jnp.concatenate([out[0:1, :half], out[1:2, half:]], axis=1) + sums[0:1, :]
    short_row = jnp.concatenate([out[2:3, :half], out[3:4, half:]], axis=1) + sums[1:2, :]
    first = jnp.where(long_u == 0, long_row, short_row)
    second = jnp.where(long_u == 0, short_row, long_row)
    own_gain = gain[:, pl.ds(pl.multiple_of((2 * x + u) * GROUP, GROUP), GROUP)]
    block = jnp.concatenate([first, second, own_gain, own_gain], axis=0)
    part[...] = jnp.broadcast_to(block[None], part.shape)


def loss_kernel(positives, parts, vec, loss, mine, theirs):
    z, x, u = places()
    domain = lax.axis_index("domain")
    width = mine.shape[1]
    piece = vec.shape[2]

    def collect(place, dest):
        total = jnp.zeros((2, 1), jnp.float32)
        for group in range(PLANE):
            blocks = [parts[2 * (PLANE * plane + group) + place] for plane in range(PLANES)]
            values = (blocks[0][:2] + blocks[1][:2]) + (blocks[2][:2] + blocks[3][:2])
            total = total + jnp.sum(values * values, axis=1, keepdims=True)
            dest[:, group * GROUP : (group + 1) * GROUP] = values * blocks[0][2:3]
        factor = lax.rsqrt(total / width + epsilon)
        return (dest[...] * factor).astype(jnp.bfloat16).astype(jnp.float32)

    own = collect(domain, mine)
    other = collect(1 - domain, theirs)
    mine[...] = own
    start = pl.multiple_of((2 * z + x) * piece, piece)
    out = mine[:, pl.ds(start, piece)]
    vec[0] = jnp.where(u == 0, out[0:1], out[1:2]).astype(jnp.bfloat16)
    this = jnp.where(u == 0, own[0:1], own[1:2])
    logits = jnp.sum(this * other, axis=1, keepdims=True) * (logit_scale / width)
    top = jnp.max(logits, axis=0, keepdims=True)
    spread = jnp.log(jnp.sum(jnp.exp(logits - top), axis=0, keepdims=True)) + top
    forward = jnp.where(u == 0, positives[0], positives[1])
    backward = jnp.where(positives[0] == u, 0, 1)
    partner = jnp.where(domain == 0, forward, backward)
    rows = lax.broadcasted_iota(jnp.int32, (2, 1), 0)
    loss[...] = spread - jnp.sum(jnp.where(rows == partner, logits, 0.0), axis=0, keepdims=True)


def vmem():
    return pl.BlockSpec(memory_space=pltpu.VMEM)


def anywhere():
    return pl.BlockSpec(memory_space=pl.ANY)


def smem():
    return pl.BlockSpec(memory_space=pltpu.SMEM)


def call(kernel, outs, in_specs, scratch, flops):
    return pl.pallas_call(
        kernel,
        out_shape=outs,
        in_specs=in_specs,
        out_specs=jax.tree.map(lambda _: vmem(), outs),
        scratch_shapes=scratch,
        compiler_params=pltpu.CompilerParams(vmem_limit_bytes=40 * 1024 * 1024),
        cost_estimate=pl.CostEstimate(flops=flops, bytes_accessed=2**21, transcendentals=0),
    )


def towers(history, qkv_weight, norm_gain, pool_gain, lengths, positives):
    events = history[0, 0]
    tokens, width = events.shape
    weight = qkv_weight[0]
    rows = weight.shape[0]
    f32, bf16 = jnp.float32, jnp.bfloat16
    shape = jax.ShapeDtypeStruct
    z, x, u = places()
    group = 2 * x + u
    here = PLANE * PLANES

    def hop(a, target):
        pairs = [(i, target(i // PLANE) * PLANE + i % PLANE) for i in range(here) if target(i // PLANE) is not None]
        return lax.ppermute(a, ("seq", "dp"), pairs)

    def plane_hop(a, move):
        return lax.ppermute(a, ("seq", "dp"), [(i, i ^ move) for i in range(here)])

    def columns(which):
        return jnp.concatenate(
            [lax.dynamic_slice(weight, (0, part * width + which * GROUP), (rows, GROUP)) for part in range(3)],
            axis=1,
        )

    def upward(a):
        return [hop(a, lambda p: p + step if p + step < PLANES else None) for step in (3, 2, 1)]

    def downward(a):
        return [hop(a, lambda p: p - step if p >= step else None) for step in (3, 2, 1)]

    wide = 2 * GROUP
    events, w_sent = lax.optimization_barrier((events, columns(jnp.bitwise_xor(group, 2))))
    w_near = plane_hop(w_sent, 2)
    w_own = columns(group)
    qk_own, qk_near = w_own[:, :wide], w_near[:, :wide]
    two_own = hop(qk_own, lambda p: p ^ 2)
    across = plane_hop(events, 1)
    near = plane_hop(events, 2)
    two_near = hop(qk_near, lambda p: p ^ 2)
    qk = jnp.concatenate([qk_own, qk_near], axis=0)
    one_away = hop(qk, lambda p: p ^ 1)
    next_plane = hop(qk, lambda p: 3 - p if p in (1, 2) else None)
    corner_a = plane_hop(across[: tokens // 2], 2)
    corner_b = plane_hop(near[tokens // 2 :], 1)
    far = hop(jnp.concatenate([two_own, two_near], axis=0), lambda p: {1: 0, 2: 3}.get(p))
    v_own = jnp.concatenate([w_own[:, wide:], w_near[:, wide:]], axis=0)
    v_far = [hop(v_own, lambda p: p ^ j) for j in (1, 2, 3)]

    normed, sums = call(
        norm_kernel,
        (shape((3 * tokens, width), bf16), shape((2, GROUP), f32)),
        [smem()] + [anywhere()] * 5 + [vmem()],
        [pltpu.VMEM((3, tokens, width), bf16), pltpu.SemaphoreType.DMA((3, 2))],
        2 * 3 * tokens * width,
    )(lengths, events, near, across, corner_a, corner_b, norm_gain)
    feats, totals = call(
        project_kernel,
        (shape((3 * tokens, wide), bf16), shape((1, GROUP), f32)),
        [vmem()] * 7,
        [pltpu.VMEM((width, wide), bf16)],
        2 * 3 * tokens * width * wide,
    )(normed, qk, one_away, two_own, two_near, next_plane, far)
    weight_sum, local = call(
        scan_kernel,
        (shape((1, GROUP), f32), shape((3 * tokens, HEAD_DIM), f32)),
        [vmem()] * 4,
        [],
        2 * 9 * tokens * tokens * GROUP,
    )(*upward(totals), feats)
    part = call(
        pool_kernel,
        shape((2 * here, 4, GROUP), f32),
        [smem()] + [vmem()] * 12,
        [pltpu.VMEM((width, GROUP), bf16), pltpu.VMEM((2 * HEAD_DIM, width), f32)],
        2 * 3 * tokens * width * HEAD_DIM,
    )(lengths, *downward(weight_sum), sums, feats, local, normed, v_own, *v_far, pool_gain)
    parts = lax.all_to_all(part, ("seq", "dp", "domain"), 0, 0, tiled=True)
    vec, loss = call(
        loss_kernel,
        (shape((1, 1, width // 8), bf16), shape((1, 1), f32)),
        [smem(), vmem()],
        [pltpu.VMEM((2, width), f32), pltpu.VMEM((2, width), f32)],
        2**14,
    )(positives, parts)
    return vec, loss


def solution(mesh):
    placed = (
        P("domain", "dp", "seq", None),
        P("domain", "seq", None),
        P("domain", None),
        P("domain", None),
        P("domain", "dp"),
        P(),
    )
    small = mesh.shape["seq"] == 2 * PLANES and mesh.shape["dp"] == 2
    return jax.shard_map(
        towers if small else shards,
        mesh=mesh,
        in_specs=placed,
        out_specs=(P("domain", "dp", "seq"), P("domain", "dp")),
        check_vma=False,
    )
```

```python
import functools

import jax
import jax.numpy as jnp
from jax import lax
from jax.experimental import pallas as pl
from jax.experimental.pallas import tpu as pltpu
from jax.sharding import PartitionSpec as P

HEADS = 8
HEAD_DIM = 128


logit_scale = 20.0
epsilon = 1e-06
highest = lax.Precision.HIGHEST


def carried_in(part, axis, combine, identity):
    place = lax.axis_index(axis)
    gathered = jax.tree.map(lambda a: lax.all_gather(a, axis), part)
    state = jax.tree.map(lambda a, e: jnp.zeros_like(a) + jnp.asarray(e, a.dtype), part, identity)

    def one(hop, state):
        return combine(
            state, jax.tree.map(lambda a: lax.dynamic_index_in_dim(a, hop, 0, False), gathered)
        )

    return lax.fori_loop(0, place, one, state)


def partner_2(block, axis, stride):
    count = lax.axis_size(axis)
    route = []
    for low in range(count):
        high = low | 1 << stride
        if high != low and high < count:
            route += [(low, high), (high, low)]
    return lax.ppermute(block, axis, route)


def feature_map(values):
    return jax.nn.elu(values) + 1.0


def add_pair(earlier, later):
    return (earlier[0] + later[0], earlier[1] + later[1])


def shards(history, qkv_weight, norm_gain, pool_gain, lengths, positives):
    seq_count = lax.axis_size("seq")
    seq_place = lax.axis_index("seq")
    group_place = lax.axis_index("dp")
    domain_place = lax.axis_index("domain")
    events = history[0]
    users_dev, tokens_dev, width = events.shape
    row_count = users_dev * tokens_dev
    wide = events.astype(jnp.float32)
    normed = (
        wide * lax.rsqrt(jnp.mean(wide * wide, -1, keepdims=True) + epsilon) * norm_gain[0]
    ).astype(jnp.bfloat16)
    normed = normed.reshape(row_count, width)
    rows_here = qkv_weight[0]
    projected = jnp.dot(
        normed,
        lax.all_gather(rows_here, "seq", axis=0, tiled=True),
        preferred_element_type=jnp.float32,
    )
    query_raw = projected[:, :width]
    key_raw = projected[:, width : 2 * width]
    value_raw = projected[:, 2 * width :]
    positions = seq_place * tokens_dev + jnp.arange(tokens_dev)
    valid = positions[None, :] < lengths[0][:, None]
    shape_heads = (users_dev, tokens_dev, HEADS, HEAD_DIM)
    queries = feature_map(query_raw).astype(jnp.bfloat16).reshape(shape_heads)
    key_feats = (
        jnp.where(valid.reshape(row_count)[:, None], feature_map(key_raw), 0.0)
        .astype(jnp.bfloat16)
        .reshape(shape_heads)
    )
    val_feats = value_raw.astype(jnp.bfloat16).reshape(shape_heads)
    local_state = jnp.einsum(
        "uthc,uthd->uhcd", key_feats, val_feats, preferred_element_type=jnp.float32
    )
    local_total = jnp.sum(key_feats.astype(jnp.float32), axis=1)
    state_before, total_before = carried_in(
        (local_state, local_total),
        "seq",
        add_pair,
        (jnp.zeros_like(local_state), jnp.zeros_like(local_total)),
    )
    causal = jnp.arange(tokens_dev)[:, None] >= jnp.arange(tokens_dev)[None, :]
    scores = jnp.einsum("uthc,ushc->uhts", queries, key_feats, preferred_element_type=jnp.float32)
    scores = jnp.where(causal, scores, 0.0)
    denominator = jnp.sum(scores, axis=-1) + jnp.einsum(
        "uthc,uhc->uht", queries.astype(jnp.float32), total_before, precision=highest
    )
    numerator = jnp.einsum(
        "uhts,ushc->uthc",
        scores.astype(jnp.bfloat16),
        val_feats,
        preferred_element_type=jnp.float32,
    )
    numerator = numerator + jnp.einsum(
        "uthc,uhcd->uthd",
        queries,
        state_before.astype(jnp.bfloat16),
        preferred_element_type=jnp.float32,
    )
    attended = numerator / jnp.transpose(denominator, (0, 2, 1))[..., None]
    attended = attended.reshape(users_dev, tokens_dev, width)
    partial_value = jnp.sum(jnp.where(valid[..., None], wide + attended, 0.0), axis=1)
    piece_width = width // seq_count
    gain_row = pool_gain[0]
    pooled = lax.psum(partial_value, "seq")
    factor = lax.rsqrt(jnp.mean(pooled * pooled, -1, keepdims=True) + epsilon)
    full_vec = (pooled * factor * gain_row).astype(jnp.bfloat16)
    out_vec = lax.dynamic_slice_in_dim(full_vec, seq_place * piece_width, piece_width, 1)
    group = lax.all_gather(full_vec, "dp", axis=0, tiled=True)
    other = partner_2(group, "domain", 0)
    logits = jnp.einsum("uc,vc->uv", full_vec, other, preferred_element_type=jnp.float32) * (
        logit_scale / width
    )
    users_all = other.shape[0]
    own_index = group_place * users_dev + jnp.arange(users_dev)
    targets = lax.dynamic_slice_in_dim(positives, group_place * users_dev, users_dev)
    forward_pair = targets[:, None] == jnp.arange(users_all)[None, :]
    backward_pair = positives[None, :] == own_index[:, None]
    partner = jnp.where(domain_place == 0, forward_pair, backward_pair)
    loss = jnp.log(jnp.sum(jnp.exp(logits), axis=-1)) - jnp.sum(
        jnp.where(partner, logits, 0.0), axis=-1
    )
    return (out_vec[None], loss[None])


PLANE = 4
PLANES = 4
GROUP = 256
DOT_T = (((0,), (0,)), ((), ()))


def places():
    seq_place = lax.axis_index("seq")
    return lax.div(seq_place, 2), lax.rem(seq_place, 2), lax.axis_index("dp")


def head_sums(a):
    return [
        jnp.sum(a[:, h * HEAD_DIM : (h + 1) * HEAD_DIM], axis=1, keepdims=True)
        for h in range(GROUP // HEAD_DIM)
    ]


def by_head(columns):
    rows = columns[0].shape[0]
    return jnp.concatenate([jnp.broadcast_to(c, (rows, HEAD_DIM)) for c in columns], axis=1)


def split_two(a):
    high = a.astype(jnp.bfloat16)
    return high, (a - high.astype(jnp.float32)).astype(jnp.bfloat16)


def pack_kernel(weight, qk_own, v_own, qk_sent, v_sent, sems):
    _, x, u = places()
    width = weight.shape[1] // 3
    copies = []
    for move, qk, v in ((2, qk_sent, v_sent), (0, qk_own, v_own)):
        group = jnp.bitwise_xor(2 * x + u, move)
        for part, (ref, at) in enumerate(((qk, 0), (qk, GROUP), (v, 0))):
            start = pl.multiple_of(part * width + group * GROUP, GROUP)
            copies.append(
                pltpu.make_async_copy(
                    weight.at[:, pl.ds(start, GROUP)], ref.at[:, pl.ds(at, GROUP)], sems.at[len(copies)]
                )
            )
    for copy in copies:
        copy.start()
    for copy in copies:
        copy.wait()


def relay_kernel(events, after, out, sem):
    del after
    copy = pltpu.make_async_copy(events, out, sem)
    copy.start()
    copy.wait()


def norm_kernel(lengths, own, near, across, corner_a, corner_b, gain, normed, sums, raw, sems):
    tokens = own.shape[0]
    half = corner_a.shape[0]
    z, x, u = places()
    long_u = jnp.where(lengths[0, 0] > tokens, u, 1 - u)

    def fetch(slot, pick):
        for j, ref in enumerate((own, near, across)):

            @pl.when(pick == j)
            def _():
                pltpu.make_async_copy(ref.at[pl.ds(0, half)], raw.at[slot, pl.ds(0, half)], sems.at[slot, 0]).start()
                pltpu.make_async_copy(ref.at[pl.ds(half, half)], raw.at[slot, pl.ds(half, half)], sems.at[slot, 1]).start()

        @pl.when(pick == 3)
        def _():
            pltpu.make_async_copy(corner_a, raw.at[slot, pl.ds(0, half)], sems.at[slot, 0]).start()
            pltpu.make_async_copy(corner_b, raw.at[slot, pl.ds(half, half)], sems.at[slot, 1]).start()

    for slot in range(3):
        from_x = 1 if slot == 1 else 0
        from_u = 1 - long_u if slot == 2 else long_u
        fetch(slot, jnp.bitwise_xor(x, from_x) + 2 * jnp.bitwise_xor(u, from_u))
    columns = pl.ds(pl.multiple_of((2 * x + u) * GROUP, GROUP), GROUP)

    def one(slot):
        values = raw[slot].astype(jnp.float32)
        scale = lax.rsqrt(jnp.mean(values * values, axis=1, keepdims=True) + epsilon)
        normed[pl.ds(slot * tokens, tokens), :] = (values * scale * gain[...]).astype(jnp.bfloat16)
        return jnp.sum(raw[slot, :, columns].astype(jnp.float32), axis=0, keepdims=True)

    for slot in range(3):
        for part in range(2):
            at = pl.ds(part * half, half)
            pltpu.make_async_copy(own.at[at], raw.at[slot, at], sems.at[slot, part]).wait()
    sums[0:1, :] = one(0) + one(1)
    sums[1:2, :] = jnp.zeros((1, GROUP), jnp.float32)

    @pl.when(z == 0)
    def _():
        sums[1:2, :] = one(2)


def project_kernel(normed, own, one_away, two_own, two_near, next_plane, far, feats, totals, weights):
    tokens = normed.shape[0] // 3
    rows = two_own.shape[0]
    z, x, _ = places()

    def put(plane, place, values):
        weights[pl.ds(pl.multiple_of((2 * plane + place) * rows, rows), rows), :] = values

    def put_both(plane, ref):
        put(plane, x, ref[:rows, :])
        put(plane, 1 - x, ref[rows:, :])

    put_both(z, own)
    put_both(jnp.bitwise_xor(z, 1), one_away)
    put(jnp.bitwise_xor(z, 2), x, two_own[...])
    put(jnp.bitwise_xor(z, 2), 1 - x, two_near[...])
    inner = jnp.logical_or(z == 1, z == 2)

    @pl.when(inner)
    def _():
        put_both(3 - z, next_plane)

    @pl.when(jnp.logical_not(inner))
    def _():
        put_both(3 - z, far)

    def one(slot, count):
        part = pl.ds(slot * tokens, count)
        out = jnp.dot(normed[part, :], weights[...], preferred_element_type=jnp.float32)
        out = jnp.where(out > 0.0, out + 1.0, jnp.exp(jnp.minimum(out, 0.0))).astype(jnp.bfloat16)
        feats[part, :] = out
        return jnp.sum(out[:, GROUP:].astype(jnp.float32), axis=0, keepdims=True)

    totals[...] = one(0, tokens) + one(1, tokens)

    @pl.when(z == 0)
    def _():
        one(2, tokens)


def scan_kernel(total_1, total_2, total_3, feats, weight_sum, local):
    tokens = feats.shape[0] // 3
    z, _, _ = places()
    row = lax.broadcasted_iota(jnp.int32, (tokens, tokens), 0)
    col = lax.broadcasted_iota(jnp.int32, (tokens, tokens), 1)
    lower = (row >= col).astype(jnp.bfloat16)
    upper = (row <= col).astype(jnp.bfloat16)
    before = jnp.zeros((1, GROUP), jnp.float32)
    for j, ref in enumerate((total_1, total_2, total_3), 1):
        before = before + jnp.where(jnp.bitwise_xor(z, j) < z, ref[...], 0.0)

    def block(slot, carry):
        part = pl.ds(slot * tokens, tokens)
        query = feats[part, :GROUP].astype(jnp.float32)
        key = feats[part, GROUP:]
        prefix = jnp.dot(lower, key, preferred_element_type=jnp.float32) + carry
        share = query / by_head(head_sums(query * prefix))
        return share, key, prefix[tokens - 1 : tokens, :]

    def suffix(share):
        high, low = split_two(share)
        return jnp.dot(upper, high, preferred_element_type=jnp.float32) + jnp.dot(
            upper, low, preferred_element_type=jnp.float32
        )

    def store(slot, key, after):
        sums_by_head = head_sums(key.astype(jnp.float32) * after)
        part = pl.ds(slot * tokens, tokens)
        local[part, :] = jnp.concatenate(
            [jnp.broadcast_to(c, (tokens, HEAD_DIM // 2)) for c in sums_by_head], axis=1
        )

    share_one, key_one, carry = block(0, before)
    share_two, key_two, _ = block(1, carry)
    after_two = suffix(share_two)
    after_one = suffix(share_one) + after_two[0:1, :]
    weight_sum[...] = after_one[0:1, :]
    store(0, key_one, after_one)
    store(1, key_two, after_two)

    @pl.when(z == 0)
    def _():
        share, key, _ = block(2, jnp.zeros((1, GROUP), jnp.float32))
        store(2, key, suffix(share))


def mix_kernel(sum_1, sum_2, sum_3, feats, local, normed, to_0, to_1, to_2, to_3, mixed):
    tokens = feats.shape[0] // 3
    z, _, _ = places()
    after = jnp.zeros((1, GROUP), jnp.float32)
    for j, ref in enumerate((sum_1, sum_2, sum_3), 1):
        after = after + jnp.where(jnp.bitwise_xor(z, j) > z, ref[...], 0.0)
    lane = lax.broadcasted_iota(jnp.int32, (1, HEAD_DIM), 1)

    def mix(weight, slot, count):
        high, low = split_two(weight)
        both = jnp.where(lax.rem(lane, 64) < 32, high.astype(jnp.float32), low.astype(jnp.float32))
        rows = normed[pl.ds(slot * tokens, count), :]
        out = lax.dot_general(both.astype(jnp.bfloat16), rows, DOT_T, preferred_element_type=jnp.float32)
        return [out[h : h + 1, :] + out[h + 32 : h + 33, :] for h in (0, 64)]

    key = feats[0 : 2 * tokens, GROUP:].astype(jnp.float32)
    extra = jnp.concatenate(
        [jnp.broadcast_to(c, (2 * tokens, HEAD_DIM // 2)) for c in head_sums(key * after)], axis=1
    )
    mixed[0:2, :] = jnp.concatenate(mix(local[0 : 2 * tokens, :] + extra, 0, 2 * tokens), axis=0)
    mixed[2:4, :] = jnp.zeros((2, mixed.shape[1]), jnp.float32)

    @pl.when(z == 0)
    def _():
        mixed[2:4, :] = jnp.concatenate(mix(local[2 * tokens :, :], 2, tokens), axis=0)

    for j, ref in enumerate((to_0, to_1, to_2, to_3)):
        start = pl.multiple_of(jnp.bitwise_xor(z, j) * GROUP, GROUP)
        ref[...] = mixed[:, pl.ds(start, GROUP)]


def pool_kernel(lengths, tokens, sums, from_0, from_1, from_2, from_3, v_own, v_near, gain, part, values):
    rows = v_own.shape[0]
    _, x, u = places()
    long_u = jnp.where(lengths[0, 0] > tokens, u, 1 - u)
    for half, ref in ((x, v_own), (1 - x, v_near)):
        values[pl.ds(pl.multiple_of(half * rows, rows), rows), :] = ref[...]
    total = (from_0[...] + from_1[...]) + (from_2[...] + from_3[...])
    high, low = split_two(jnp.concatenate([total, total], axis=0))
    out = jnp.dot(high, values[...], preferred_element_type=jnp.float32) + jnp.dot(
        low, values[...], preferred_element_type=jnp.float32
    )
    half = HEAD_DIM
    long_row = jnp.concatenate([out[0:1, :half], out[1:2, half:]], axis=1) + sums[0:1, :]
    short_row = jnp.concatenate([out[2:3, :half], out[3:4, half:]], axis=1) + sums[1:2, :]
    first = jnp.where(long_u == 0, long_row, short_row)
    second = jnp.where(long_u == 0, short_row, long_row)
    own_gain = gain[:, pl.ds(pl.multiple_of((2 * x + u) * GROUP, GROUP), GROUP)]
    block = jnp.concatenate([first, second, own_gain, own_gain], axis=0)
    part[...] = jnp.broadcast_to(block[None], part.shape)


def loss_kernel(positives, parts, vec, loss, mine, theirs):
    z, x, u = places()
    domain = lax.axis_index("domain")
    width = mine.shape[1]
    piece = vec.shape[2]

    def collect(place, dest):
        total = jnp.zeros((2, 1), jnp.float32)
        for group in range(PLANE):
            blocks = [parts[2 * (PLANE * plane + group) + place] for plane in range(PLANES)]
            values = (blocks[0][:2] + blocks[1][:2]) + (blocks[2][:2] + blocks[3][:2])
            total = total + jnp.sum(values * values, axis=1, keepdims=True)
            dest[:, group * GROUP : (group + 1) * GROUP] = values * blocks[0][2:3]
        factor = lax.rsqrt(total / width + epsilon)
        return (dest[...] * factor).astype(jnp.bfloat16).astype(jnp.float32)

    own = collect(domain, mine)
    other = collect(1 - domain, theirs)
    mine[...] = own
    start = pl.multiple_of((2 * z + x) * piece, piece)
    out = mine[:, pl.ds(start, piece)]
    vec[0] = jnp.where(u == 0, out[0:1], out[1:2]).astype(jnp.bfloat16)
    this = jnp.where(u == 0, own[0:1], own[1:2])
    logits = jnp.sum(this * other, axis=1, keepdims=True) * (logit_scale / width)
    top = jnp.max(logits, axis=0, keepdims=True)
    spread = jnp.log(jnp.sum(jnp.exp(logits - top), axis=0, keepdims=True)) + top
    forward = jnp.where(u == 0, positives[0], positives[1])
    backward = jnp.where(positives[0] == u, 0, 1)
    partner = jnp.where(domain == 0, forward, backward)
    rows = lax.broadcasted_iota(jnp.int32, (2, 1), 0)
    loss[...] = spread - jnp.sum(jnp.where(rows == partner, logits, 0.0), axis=0, keepdims=True)


def vmem():
    return pl.BlockSpec(memory_space=pltpu.VMEM)


def anywhere():
    return pl.BlockSpec(memory_space=pl.ANY)


def hbm():
    return pl.BlockSpec(memory_space=pltpu.HBM)


def smem():
    return pl.BlockSpec(memory_space=pltpu.SMEM)


def call(kernel, outs, in_specs, scratch, flops):
    return pl.pallas_call(
        kernel,
        out_shape=outs,
        in_specs=in_specs,
        out_specs=jax.tree.map(lambda _: vmem(), outs),
        scratch_shapes=scratch,
        compiler_params=pltpu.CompilerParams(vmem_limit_bytes=40 * 1024 * 1024),
        cost_estimate=pl.CostEstimate(flops=flops, bytes_accessed=2**21, transcendentals=0),
    )


def towers(history, qkv_weight, norm_gain, pool_gain, lengths, positives):
    events = history[0, 0]
    tokens, width = events.shape
    weight = qkv_weight[0]
    rows = weight.shape[0]
    f32, bf16 = jnp.float32, jnp.bfloat16
    shape = jax.ShapeDtypeStruct
    here = PLANE * PLANES

    def hop(a, target):
        pairs = [(i, target(i // PLANE) * PLANE + i % PLANE) for i in range(here) if target(i // PLANE) is not None]
        return lax.ppermute(a, ("seq", "dp"), pairs)

    def plane_hop(a, move):
        return lax.ppermute(a, ("seq", "dp"), [(i, i ^ move) for i in range(here)])

    def each(a):
        return [hop(a, lambda p: p ^ j) for j in range(1, PLANES)]

    wide = 2 * GROUP

    qk_own, v_own, qk_sent, v_sent = call(
        pack_kernel,
        (shape((rows, wide), bf16), shape((rows, GROUP), bf16)) * 2,
        [hbm()],
        [pltpu.SemaphoreType.DMA((6,))],
        0,
    )(weight)
    qk_near = plane_hop(qk_sent, 2)
    across = plane_hop(events, 1)
    two_own = hop(qk_own, lambda p: p ^ 2)
    own = call(
        relay_kernel, shape((tokens, width), bf16), [hbm(), anywhere()], [pltpu.SemaphoreType.DMA(())], 0
    )(events, qk_near)
    near = plane_hop(own, 2)
    two_near = hop(qk_near, lambda p: p ^ 2)
    qk = jnp.concatenate([qk_own, qk_near], axis=0)
    one_away = hop(qk, lambda p: p ^ 1)
    next_plane = hop(qk, lambda p: 3 - p if p in (1, 2) else None)
    corner_a = plane_hop(across[: tokens // 2], 2)
    corner_b = plane_hop(near[tokens // 2 :], 1)
    far = hop(jnp.concatenate([two_own, two_near], axis=0), lambda p: {1: 0, 2: 3}.get(p))
    v_near = plane_hop(v_sent, 2)

    normed, sums = call(
        norm_kernel,
        (shape((3 * tokens, width), bf16), shape((2, GROUP), f32)),
        [smem()] + [anywhere()] * 5 + [vmem()],
        [pltpu.VMEM((3, tokens, width), bf16), pltpu.SemaphoreType.DMA((3, 2))],
        2 * 3 * tokens * width,
    )(lengths, own, near, across, corner_a, corner_b, norm_gain)
    feats, totals = call(
        project_kernel,
        (shape((3 * tokens, wide), bf16), shape((1, GROUP), f32)),
        [vmem()] * 7,
        [pltpu.VMEM((width, wide), bf16)],
        2 * 3 * tokens * width * wide,
    )(normed, qk, one_away, two_own, two_near, next_plane, far)
    weight_sum, local = call(
        scan_kernel,
        (shape((1, GROUP), f32), shape((3 * tokens, HEAD_DIM), f32)),
        [vmem()] * 4,
        [],
        2 * 9 * tokens * tokens * GROUP,
    )(*each(totals), feats)
    mixed = call(
        mix_kernel,
        tuple(shape((4, GROUP), f32) for _ in range(PLANES)),
        [vmem()] * 6,
        [pltpu.VMEM((4, width), f32)],
        2 * 3 * tokens * width * HEAD_DIM,
    )(*each(weight_sum), feats, local, normed)
    moved = [hop(mixed[j], lambda p: p ^ j) for j in range(1, PLANES)]
    part = call(
        lambda lengths, *refs: pool_kernel(lengths, tokens, *refs),
        shape((2 * here, 4, GROUP), f32),
        [smem()] + [vmem()] * 8,
        [pltpu.VMEM((GROUP, GROUP), bf16)],
        2 * 8 * GROUP * GROUP,
    )(lengths, sums, mixed[0], *moved, v_own, v_near, pool_gain)
    parts = lax.all_to_all(part, ("seq", "dp", "domain"), 0, 0, tiled=True)
    vec, loss = call(
        loss_kernel,
        (shape((1, 1, width // 8), bf16), shape((1, 1), f32)),
        [smem(), vmem()],
        [pltpu.VMEM((2, width), f32), pltpu.VMEM((2, width), f32)],
        2**14,
    )(positives, parts)
    return vec, loss


def solution(mesh):
    placed = (
        P("domain", "dp", "seq", None),
        P("domain", "seq", None),
        P("domain", None),
        P("domain", None),
        P("domain", "dp"),
        P(),
    )
    small = mesh.shape["seq"] == 2 * PLANES and mesh.shape["dp"] == 2
    return jax.shard_map(
        towers if small else shards,
        mesh=mesh,
        in_specs=placed,
        out_specs=(P("domain", "dp", "seq"), P("domain", "dp")),
        check_vma=False,
    )
```

```python
import functools

import jax
import jax.numpy as jnp
from jax import lax
from jax.experimental import pallas as pl
from jax.experimental.pallas import tpu as pltpu
from jax.sharding import PartitionSpec as P

HEADS = 8
HEAD_DIM = 128


logit_scale = 20.0
epsilon = 1e-06
highest = lax.Precision.HIGHEST


def carried_in(part, axis, combine, identity):
    place = lax.axis_index(axis)
    gathered = jax.tree.map(lambda a: lax.all_gather(a, axis), part)
    state = jax.tree.map(lambda a, e: jnp.zeros_like(a) + jnp.asarray(e, a.dtype), part, identity)

    def one(hop, state):
        return combine(
            state, jax.tree.map(lambda a: lax.dynamic_index_in_dim(a, hop, 0, False), gathered)
        )

    return lax.fori_loop(0, place, one, state)


def partner_2(block, axis, stride):
    count = lax.axis_size(axis)
    route = []
    for low in range(count):
        high = low | 1 << stride
        if high != low and high < count:
            route += [(low, high), (high, low)]
    return lax.ppermute(block, axis, route)


def feature_map(values):
    return jax.nn.elu(values) + 1.0


def add_pair(earlier, later):
    return (earlier[0] + later[0], earlier[1] + later[1])


def shards(history, qkv_weight, norm_gain, pool_gain, lengths, positives):
    seq_count = lax.axis_size("seq")
    seq_place = lax.axis_index("seq")
    group_place = lax.axis_index("dp")
    domain_place = lax.axis_index("domain")
    events = history[0]
    users_dev, tokens_dev, width = events.shape
    row_count = users_dev * tokens_dev
    wide = events.astype(jnp.float32)
    normed = (
        wide * lax.rsqrt(jnp.mean(wide * wide, -1, keepdims=True) + epsilon) * norm_gain[0]
    ).astype(jnp.bfloat16)
    normed = normed.reshape(row_count, width)
    rows_here = qkv_weight[0]
    projected = jnp.dot(
        normed,
        lax.all_gather(rows_here, "seq", axis=0, tiled=True),
        preferred_element_type=jnp.float32,
    )
    query_raw = projected[:, :width]
    key_raw = projected[:, width : 2 * width]
    value_raw = projected[:, 2 * width :]
    positions = seq_place * tokens_dev + jnp.arange(tokens_dev)
    valid = positions[None, :] < lengths[0][:, None]
    shape_heads = (users_dev, tokens_dev, HEADS, HEAD_DIM)
    queries = feature_map(query_raw).astype(jnp.bfloat16).reshape(shape_heads)
    key_feats = (
        jnp.where(valid.reshape(row_count)[:, None], feature_map(key_raw), 0.0)
        .astype(jnp.bfloat16)
        .reshape(shape_heads)
    )
    val_feats = value_raw.astype(jnp.bfloat16).reshape(shape_heads)
    local_state = jnp.einsum(
        "uthc,uthd->uhcd", key_feats, val_feats, preferred_element_type=jnp.float32
    )
    local_total = jnp.sum(key_feats.astype(jnp.float32), axis=1)
    state_before, total_before = carried_in(
        (local_state, local_total),
        "seq",
        add_pair,
        (jnp.zeros_like(local_state), jnp.zeros_like(local_total)),
    )
    causal = jnp.arange(tokens_dev)[:, None] >= jnp.arange(tokens_dev)[None, :]
    scores = jnp.einsum("uthc,ushc->uhts", queries, key_feats, preferred_element_type=jnp.float32)
    scores = jnp.where(causal, scores, 0.0)
    denominator = jnp.sum(scores, axis=-1) + jnp.einsum(
        "uthc,uhc->uht", queries.astype(jnp.float32), total_before, precision=highest
    )
    numerator = jnp.einsum(
        "uhts,ushc->uthc",
        scores.astype(jnp.bfloat16),
        val_feats,
        preferred_element_type=jnp.float32,
    )
    numerator = numerator + jnp.einsum(
        "uthc,uhcd->uthd",
        queries,
        state_before.astype(jnp.bfloat16),
        preferred_element_type=jnp.float32,
    )
    attended = numerator / jnp.transpose(denominator, (0, 2, 1))[..., None]
    attended = attended.reshape(users_dev, tokens_dev, width)
    partial_value = jnp.sum(jnp.where(valid[..., None], wide + attended, 0.0), axis=1)
    piece_width = width // seq_count
    gain_row = pool_gain[0]
    pooled = lax.psum(partial_value, "seq")
    factor = lax.rsqrt(jnp.mean(pooled * pooled, -1, keepdims=True) + epsilon)
    full_vec = (pooled * factor * gain_row).astype(jnp.bfloat16)
    out_vec = lax.dynamic_slice_in_dim(full_vec, seq_place * piece_width, piece_width, 1)
    group = lax.all_gather(full_vec, "dp", axis=0, tiled=True)
    other = partner_2(group, "domain", 0)
    logits = jnp.einsum("uc,vc->uv", full_vec, other, preferred_element_type=jnp.float32) * (
        logit_scale / width
    )
    users_all = other.shape[0]
    own_index = group_place * users_dev + jnp.arange(users_dev)
    targets = lax.dynamic_slice_in_dim(positives, group_place * users_dev, users_dev)
    forward_pair = targets[:, None] == jnp.arange(users_all)[None, :]
    backward_pair = positives[None, :] == own_index[:, None]
    partner = jnp.where(domain_place == 0, forward_pair, backward_pair)
    loss = jnp.log(jnp.sum(jnp.exp(logits), axis=-1)) - jnp.sum(
        jnp.where(partner, logits, 0.0), axis=-1
    )
    return (out_vec[None], loss[None])


PLANE = 4
PLANES = 4
GROUP = 256
DOT_T = (((0,), (0,)), ((), ()))
MESSAGE = GROUP + 16


def places():
    seq_place = lax.axis_index("seq")
    return lax.div(seq_place, 2), lax.rem(seq_place, 2), lax.axis_index("dp")


def head_sums(a):
    return [
        jnp.sum(a[:, h * HEAD_DIM : (h + 1) * HEAD_DIM], axis=1, keepdims=True)
        for h in range(GROUP // HEAD_DIM)
    ]


def by_head(columns):
    rows = columns[0].shape[0]
    return jnp.concatenate([jnp.broadcast_to(c, (rows, HEAD_DIM)) for c in columns], axis=1)


def split_two(a):
    high = a.astype(jnp.bfloat16)
    return high, (a - high.astype(jnp.float32)).astype(jnp.bfloat16)


def pack_kernel(weight, out, sems):
    _, _, u = places()
    width = weight.shape[1] // 3
    copies = []
    for place in range(out.shape[0]):
        group = 2 * (place % 2) + u
        for part in range(3):
            start = pl.multiple_of(part * width + group * GROUP, GROUP)
            copies.append(
                pltpu.make_async_copy(
                    weight.at[:, pl.ds(start, GROUP)],
                    out.at[place, :, pl.ds(part * GROUP, GROUP)],
                    sems.at[len(copies)],
                )
            )
    for copy in copies:
        copy.start()
    for copy in copies:
        copy.wait()


def norm_kernel(lengths, own, near, across, corner, gain, normed, sums, raw, sems):
    tokens = own.shape[0]
    z, x, u = places()
    long_u = jnp.where(lengths[0, 0] > tokens, u, 1 - u)
    for slot in range(3):
        from_x = 1 if slot == 1 else 0
        from_u = 1 - long_u if slot == 2 else long_u
        pick = jnp.bitwise_xor(x, from_x) + 2 * jnp.bitwise_xor(u, from_u)
        for j, ref in enumerate((own, near, across, corner)):

            @pl.when(pick == j)
            def _():
                pltpu.make_async_copy(ref, raw.at[slot], sems.at[slot]).start()

    columns = pl.ds(pl.multiple_of((2 * x + u) * GROUP, GROUP), GROUP)

    def one(slot):
        values = raw[slot].astype(jnp.float32)
        scale = lax.rsqrt(jnp.mean(values * values, axis=1, keepdims=True) + epsilon)
        normed[pl.ds(slot * tokens, tokens), :] = (values * scale * gain[...]).astype(jnp.bfloat16)
        return jnp.sum(raw[slot, :, columns].astype(jnp.float32), axis=0, keepdims=True)

    for slot in range(3):
        pltpu.make_async_copy(own, raw.at[slot], sems.at[slot]).wait()
    sums[0:1, :] = one(0) + one(1)
    sums[1:2, :] = jnp.zeros((1, GROUP), jnp.float32)

    @pl.when(z == 0)
    def _():
        sums[1:2, :] = one(2)


def project_kernel(normed, weights, feats, message):
    tokens = normed.shape[0] // 3
    z, _, _ = places()
    wide = 2 * GROUP

    def one(slot, count):
        part = pl.ds(slot * tokens, count)
        out = jnp.dot(normed[part, :], weights[...], preferred_element_type=jnp.float32)
        raw = out[:, :wide]
        low = jnp.where(raw > 0.0, raw + 1.0, jnp.exp(jnp.minimum(raw, 0.0))).astype(jnp.bfloat16)
        feats[part, :wide] = low
        feats[part, wide:] = out[:, wide:].astype(jnp.bfloat16)
        return jnp.sum(low[:, GROUP:].astype(jnp.float32), axis=0, keepdims=True)

    high, low = split_two(one(0, tokens) + one(1, tokens))
    for h in range(GROUP // HEAD_DIM):
        at = h * HEAD_DIM
        key = feats[0 : 2 * tokens, GROUP + at : GROUP + at + HEAD_DIM]
        value = feats[0 : 2 * tokens, wide + at : wide + at + HEAD_DIM]
        state = lax.dot_general(key, value, DOT_T, preferred_element_type=jnp.float32)
        message[at : at + HEAD_DIM, :] = state.astype(jnp.bfloat16)
    total_rows = [high[:, :HEAD_DIM], high[:, HEAD_DIM:], low[:, :HEAD_DIM], low[:, HEAD_DIM:]]
    message[GROUP:, :] = jnp.concatenate(total_rows * 4, axis=0)

    @pl.when(z == 0)
    def _():
        one(2, tokens)


def pool_kernel(lengths, state_1, state_2, state_3, feats, sums, gain, part, short):
    tokens = feats.shape[0] // 3
    z, x, u = places()
    long_u = jnp.where(lengths[0, 0] > tokens, u, 1 - u)
    row = lax.broadcasted_iota(jnp.int32, (tokens, tokens), 0)
    col = lax.broadcasted_iota(jnp.int32, (tokens, tokens), 1)
    lower = (row >= col).astype(jnp.bfloat16)
    upper = (row <= col).astype(jnp.bfloat16)
    states = [(jnp.bitwise_xor(z, j) < z, ref) for j, ref in enumerate((state_1, state_2, state_3), 1)]
    before = jnp.zeros((1, GROUP), jnp.float32)
    for earlier, ref in states:
        rows = ref[GROUP : GROUP + 16, :].astype(jnp.float32)
        total = jnp.concatenate([rows[0:1] + rows[2:3], rows[1:2] + rows[3:4]], axis=1)
        before = before + jnp.where(earlier, total, 0.0)

    def block(slot, carry):
        at = pl.ds(slot * tokens, tokens)
        query = feats[at, :GROUP].astype(jnp.float32)
        key = feats[at, GROUP : 2 * GROUP]
        prefix = jnp.dot(lower, key, preferred_element_type=jnp.float32) + carry
        share = query / by_head(head_sums(query * prefix))
        return share, key, prefix[tokens - 1 : tokens, :]

    def suffix(share):
        high, low = split_two(share)
        return jnp.dot(upper, high, preferred_element_type=jnp.float32) + jnp.dot(
            upper, low, preferred_element_type=jnp.float32
        )

    def pooled(slot, key, after):
        weight = by_head(head_sums(key.astype(jnp.float32) * after))
        value = feats[pl.ds(slot * tokens, tokens), 2 * GROUP :].astype(jnp.float32)
        return jnp.sum(weight * value, axis=0, keepdims=True)

    share_one, key_one, carry = block(0, before)
    share_two, key_two, _ = block(1, carry)
    after_two = suffix(share_two)
    after_one = suffix(share_one) + after_two[0:1, :]
    long_row = pooled(0, key_one, after_one) + pooled(1, key_two, after_two) + sums[0:1, :]
    weight = after_one[0:1, :]
    for earlier, ref in states:
        high, low = split_two(jnp.where(earlier, weight, 0.0))
        products = []
        for h in range(GROUP // HEAD_DIM):
            at = h * HEAD_DIM
            both = jnp.concatenate([high[:, at : at + HEAD_DIM]] * 8 + [low[:, at : at + HEAD_DIM]] * 8, axis=0)
            out = jnp.dot(both, ref[at : at + HEAD_DIM, :], preferred_element_type=jnp.float32)
            products.append(out[0:1] + out[8:9])
        long_row = long_row + jnp.concatenate(products, axis=1)

    short[...] = sums[1:2, :]

    @pl.when(z == 0)
    def _():
        share, key, _ = block(2, jnp.zeros((1, GROUP), jnp.float32))
        short[...] = sums[1:2, :] + pooled(2, key, suffix(share))

    short_row = short[...]
    first = jnp.where(long_u == 0, long_row, short_row)
    second = jnp.where(long_u == 0, short_row, long_row)
    own_gain = gain[:, pl.ds(pl.multiple_of((2 * x + u) * GROUP, GROUP), GROUP)]
    rows = jnp.concatenate([first, second, own_gain, own_gain], axis=0)
    part[...] = jnp.broadcast_to(rows[None], part.shape)


def loss_kernel(positives, parts, vec, loss, mine, theirs):
    z, x, u = places()
    domain = lax.axis_index("domain")
    width = mine.shape[1]
    piece = vec.shape[2]

    def collect(place, dest):
        total = jnp.zeros((2, 1), jnp.float32)
        for group in range(PLANE):
            blocks = [parts[2 * (PLANE * plane + group) + place] for plane in range(PLANES)]
            values = (blocks[0][:2] + blocks[1][:2]) + (blocks[2][:2] + blocks[3][:2])
            total = total + jnp.sum(values * values, axis=1, keepdims=True)
            dest[:, group * GROUP : (group + 1) * GROUP] = values * blocks[0][2:3]
        factor = lax.rsqrt(total / width + epsilon)
        return (dest[...] * factor).astype(jnp.bfloat16).astype(jnp.float32)

    own = collect(domain, mine)
    other = collect(1 - domain, theirs)
    mine[...] = own
    start = pl.multiple_of((2 * z + x) * piece, piece)
    out = mine[:, pl.ds(start, piece)]
    vec[0] = jnp.where(u == 0, out[0:1], out[1:2]).astype(jnp.bfloat16)
    this = jnp.where(u == 0, own[0:1], own[1:2])
    logits = jnp.sum(this * other, axis=1, keepdims=True) * (logit_scale / width)
    top = jnp.max(logits, axis=0, keepdims=True)
    spread = jnp.log(jnp.sum(jnp.exp(logits - top), axis=0, keepdims=True)) + top
    forward = jnp.where(u == 0, positives[0], positives[1])
    backward = jnp.where(positives[0] == u, 0, 1)
    partner = jnp.where(domain == 0, forward, backward)
    rows = lax.broadcasted_iota(jnp.int32, (2, 1), 0)
    loss[...] = spread - jnp.sum(jnp.where(rows == partner, logits, 0.0), axis=0, keepdims=True)


def vmem():
    return pl.BlockSpec(memory_space=pltpu.VMEM)


def anywhere():
    return pl.BlockSpec(memory_space=pl.ANY)


def hbm():
    return pl.BlockSpec(memory_space=pltpu.HBM)


def smem():
    return pl.BlockSpec(memory_space=pltpu.SMEM)


def call(kernel, outs, in_specs, scratch, flops):
    return pl.pallas_call(
        kernel,
        out_shape=outs,
        in_specs=in_specs,
        out_specs=jax.tree.map(lambda _: vmem(), outs),
        scratch_shapes=scratch,
        compiler_params=pltpu.CompilerParams(vmem_limit_bytes=40 * 1024 * 1024),
        cost_estimate=pl.CostEstimate(flops=flops, bytes_accessed=2**21, transcendentals=0),
    )


def towers(history, qkv_weight, norm_gain, pool_gain, lengths, positives):
    events = history[0, 0]
    tokens, width = events.shape
    weight = qkv_weight[0]
    rows = weight.shape[0]
    f32, bf16 = jnp.float32, jnp.bfloat16
    shape = jax.ShapeDtypeStruct
    here = PLANE * PLANES

    def hop(a, target):
        pairs = [(i, target(i // PLANE) * PLANE + i % PLANE) for i in range(here) if target(i // PLANE) is not None]
        return lax.ppermute(a, ("seq", "dp"), pairs)

    def plane_hop(a, move):
        return lax.ppermute(a, ("seq", "dp"), [(i, i ^ move) for i in range(here)])

    def each(a):
        return [hop(a, lambda p: p ^ j) for j in range(1, PLANES)]

    wide = 3 * GROUP
    sent = call(
        pack_kernel, shape((2 * PLANES, rows, wide), bf16), [hbm()], [pltpu.SemaphoreType.DMA((6 * PLANES,))], 0
    )(weight)
    weights = lax.all_to_all(sent, "seq", 0, 0, tiled=True).reshape(width, wide)
    near = plane_hop(events, 2)
    across = plane_hop(events, 1)
    corner = plane_hop(events, 3)

    normed, sums = call(
        norm_kernel,
        (shape((3 * tokens, width), bf16), shape((2, GROUP), f32)),
        [smem()] + [anywhere()] * 4 + [vmem()],
        [pltpu.VMEM((3, tokens, width), bf16), pltpu.SemaphoreType.DMA((3,))],
        2 * 3 * tokens * width,
    )(lengths, events, near, across, corner, norm_gain)
    feats, message = call(
        project_kernel,
        (shape((3 * tokens, wide), bf16), shape((MESSAGE, HEAD_DIM), bf16)),
        [vmem()] * 2,
        [],
        2 * 3 * tokens * width * wide,
    )(normed, weights)
    part = call(
        pool_kernel,
        shape((2 * here, 4, GROUP), f32),
        [smem()] + [vmem()] * 6,
        [pltpu.VMEM((1, GROUP), f32)],
        2 * 9 * tokens * tokens * GROUP,
    )(lengths, *each(message), feats, sums, pool_gain)
    parts = lax.all_to_all(part, ("seq", "dp", "domain"), 0, 0, tiled=True)
    vec, loss = call(
        loss_kernel,
        (shape((1, 1, width // 8), bf16), shape((1, 1), f32)),
        [smem(), vmem()],
        [pltpu.VMEM((2, width), f32), pltpu.VMEM((2, width), f32)],
        2**14,
    )(positives, parts)
    return vec, loss


def solution(mesh):
    placed = (
        P("domain", "dp", "seq", None),
        P("domain", "seq", None),
        P("domain", None),
        P("domain", None),
        P("domain", "dp"),
        P(),
    )
    small = mesh.shape["seq"] == 2 * PLANES and mesh.shape["dp"] == 2
    return jax.shard_map(
        towers if small else shards,
        mesh=mesh,
        in_specs=placed,
        out_specs=(P("domain", "dp", "seq"), P("domain", "dp")),
        check_vma=False,
    )
```

```python
import functools

import jax
import jax.numpy as jnp
from jax import lax
from jax.experimental import pallas as pl
from jax.experimental.pallas import tpu as pltpu
from jax.sharding import PartitionSpec as P

HEADS = 8
HEAD_DIM = 128


logit_scale = 20.0
epsilon = 1e-06
highest = lax.Precision.HIGHEST


def carried_in(part, axis, combine, identity):
    place = lax.axis_index(axis)
    gathered = jax.tree.map(lambda a: lax.all_gather(a, axis), part)
    state = jax.tree.map(lambda a, e: jnp.zeros_like(a) + jnp.asarray(e, a.dtype), part, identity)

    def one(hop, state):
        return combine(
            state, jax.tree.map(lambda a: lax.dynamic_index_in_dim(a, hop, 0, False), gathered)
        )

    return lax.fori_loop(0, place, one, state)


def partner_2(block, axis, stride):
    count = lax.axis_size(axis)
    route = []
    for low in range(count):
        high = low | 1 << stride
        if high != low and high < count:
            route += [(low, high), (high, low)]
    return lax.ppermute(block, axis, route)


def feature_map(values):
    return jax.nn.elu(values) + 1.0


def add_pair(earlier, later):
    return (earlier[0] + later[0], earlier[1] + later[1])


def shards(history, qkv_weight, norm_gain, pool_gain, lengths, positives):
    seq_count = lax.axis_size("seq")
    seq_place = lax.axis_index("seq")
    group_place = lax.axis_index("dp")
    domain_place = lax.axis_index("domain")
    events = history[0]
    users_dev, tokens_dev, width = events.shape
    row_count = users_dev * tokens_dev
    wide = events.astype(jnp.float32)
    normed = (
        wide * lax.rsqrt(jnp.mean(wide * wide, -1, keepdims=True) + epsilon) * norm_gain[0]
    ).astype(jnp.bfloat16)
    normed = normed.reshape(row_count, width)
    rows_here = qkv_weight[0]
    projected = jnp.dot(
        normed,
        lax.all_gather(rows_here, "seq", axis=0, tiled=True),
        preferred_element_type=jnp.float32,
    )
    query_raw = projected[:, :width]
    key_raw = projected[:, width : 2 * width]
    value_raw = projected[:, 2 * width :]
    positions = seq_place * tokens_dev + jnp.arange(tokens_dev)
    valid = positions[None, :] < lengths[0][:, None]
    shape_heads = (users_dev, tokens_dev, HEADS, HEAD_DIM)
    queries = feature_map(query_raw).astype(jnp.bfloat16).reshape(shape_heads)
    key_feats = (
        jnp.where(valid.reshape(row_count)[:, None], feature_map(key_raw), 0.0)
        .astype(jnp.bfloat16)
        .reshape(shape_heads)
    )
    val_feats = value_raw.astype(jnp.bfloat16).reshape(shape_heads)
    local_state = jnp.einsum(
        "uthc,uthd->uhcd", key_feats, val_feats, preferred_element_type=jnp.float32
    )
    local_total = jnp.sum(key_feats.astype(jnp.float32), axis=1)
    state_before, total_before = carried_in(
        (local_state, local_total),
        "seq",
        add_pair,
        (jnp.zeros_like(local_state), jnp.zeros_like(local_total)),
    )
    causal = jnp.arange(tokens_dev)[:, None] >= jnp.arange(tokens_dev)[None, :]
    scores = jnp.einsum("uthc,ushc->uhts", queries, key_feats, preferred_element_type=jnp.float32)
    scores = jnp.where(causal, scores, 0.0)
    denominator = jnp.sum(scores, axis=-1) + jnp.einsum(
        "uthc,uhc->uht", queries.astype(jnp.float32), total_before, precision=highest
    )
    numerator = jnp.einsum(
        "uhts,ushc->uthc",
        scores.astype(jnp.bfloat16),
        val_feats,
        preferred_element_type=jnp.float32,
    )
    numerator = numerator + jnp.einsum(
        "uthc,uhcd->uthd",
        queries,
        state_before.astype(jnp.bfloat16),
        preferred_element_type=jnp.float32,
    )
    attended = numerator / jnp.transpose(denominator, (0, 2, 1))[..., None]
    attended = attended.reshape(users_dev, tokens_dev, width)
    partial_value = jnp.sum(jnp.where(valid[..., None], wide + attended, 0.0), axis=1)
    piece_width = width // seq_count
    gain_row = pool_gain[0]
    pooled = lax.psum(partial_value, "seq")
    factor = lax.rsqrt(jnp.mean(pooled * pooled, -1, keepdims=True) + epsilon)
    full_vec = (pooled * factor * gain_row).astype(jnp.bfloat16)
    out_vec = lax.dynamic_slice_in_dim(full_vec, seq_place * piece_width, piece_width, 1)
    group = lax.all_gather(full_vec, "dp", axis=0, tiled=True)
    other = partner_2(group, "domain", 0)
    logits = jnp.einsum("uc,vc->uv", full_vec, other, preferred_element_type=jnp.float32) * (
        logit_scale / width
    )
    users_all = other.shape[0]
    own_index = group_place * users_dev + jnp.arange(users_dev)
    targets = lax.dynamic_slice_in_dim(positives, group_place * users_dev, users_dev)
    forward_pair = targets[:, None] == jnp.arange(users_all)[None, :]
    backward_pair = positives[None, :] == own_index[:, None]
    partner = jnp.where(domain_place == 0, forward_pair, backward_pair)
    loss = jnp.log(jnp.sum(jnp.exp(logits), axis=-1)) - jnp.sum(
        jnp.where(partner, logits, 0.0), axis=-1
    )
    return (out_vec[None], loss[None])


PLANE = 4
PLANES = 4
GROUP = 256
DOT_T = (((0,), (0,)), ((), ()))
MESSAGE = GROUP + 16


def places():
    seq_place = lax.axis_index("seq")
    return lax.div(seq_place, 2), lax.rem(seq_place, 2), lax.axis_index("dp")


def head_sums(a):
    return [
        jnp.sum(a[:, h * HEAD_DIM : (h + 1) * HEAD_DIM], axis=1, keepdims=True)
        for h in range(GROUP // HEAD_DIM)
    ]


def by_head(columns):
    rows = columns[0].shape[0]
    return jnp.concatenate([jnp.broadcast_to(c, (rows, HEAD_DIM)) for c in columns], axis=1)


def split_two(a):
    high = a.astype(jnp.bfloat16)
    return high, (a - high.astype(jnp.float32)).astype(jnp.bfloat16)


def pack_kernel(weight, own, sent, sems):
    _, x, u = places()
    width = weight.shape[1] // 3
    copies = []
    for move, out in ((2, sent), (0, own)):
        group = jnp.bitwise_xor(2 * x + u, move)
        for part in range(3):
            start = pl.multiple_of(part * width + group * GROUP, GROUP)
            copies.append(
                pltpu.make_async_copy(
                    weight.at[:, pl.ds(start, GROUP)], out.at[:, pl.ds(part * GROUP, GROUP)], sems.at[len(copies)]
                )
            )
    for copy in copies:
        copy.start()
    for copy in copies:
        copy.wait()


def relay_kernel(events, w_own, w_near, out, both, sem):
    rows = w_own.shape[0]
    copy = pltpu.make_async_copy(events, out, sem)
    copy.start()
    both[:rows, :] = w_own[...]
    both[rows:, :] = w_near[...]
    copy.wait()


def norm_kernel(lengths, own, near, across, corner_a, corner_b, gain, normed, sums, raw, sems):
    tokens = own.shape[0]
    half = corner_a.shape[0]
    z, x, u = places()
    long_u = jnp.where(lengths[0, 0] > tokens, u, 1 - u)

    def fetch(slot, pick):
        for j, ref in enumerate((own, near, across)):

            @pl.when(pick == j)
            def _():
                pltpu.make_async_copy(ref.at[pl.ds(0, half)], raw.at[slot, pl.ds(0, half)], sems.at[slot, 0]).start()
                pltpu.make_async_copy(ref.at[pl.ds(half, half)], raw.at[slot, pl.ds(half, half)], sems.at[slot, 1]).start()

        @pl.when(pick == 3)
        def _():
            pltpu.make_async_copy(corner_a, raw.at[slot, pl.ds(0, half)], sems.at[slot, 0]).start()
            pltpu.make_async_copy(corner_b, raw.at[slot, pl.ds(half, half)], sems.at[slot, 1]).start()

    for slot in range(3):
        from_x = 1 if slot == 1 else 0
        from_u = 1 - long_u if slot == 2 else long_u
        fetch(slot, jnp.bitwise_xor(x, from_x) + 2 * jnp.bitwise_xor(u, from_u))
    columns = pl.ds(pl.multiple_of((2 * x + u) * GROUP, GROUP), GROUP)

    def one(slot):
        values = raw[slot].astype(jnp.float32)
        scale = lax.rsqrt(jnp.mean(values * values, axis=1, keepdims=True) + epsilon)
        normed[pl.ds(slot * tokens, tokens), :] = (values * scale * gain[...]).astype(jnp.bfloat16)
        return jnp.sum(raw[slot, :, columns].astype(jnp.float32), axis=0, keepdims=True)

    for slot in range(3):
        for part in range(2):
            at = pl.ds(part * half, half)
            pltpu.make_async_copy(own.at[at], raw.at[slot, at], sems.at[slot, part]).wait()
    sums[0:1, :] = one(0) + one(1)
    sums[1:2, :] = jnp.zeros((1, GROUP), jnp.float32)

    @pl.when(z == 0)
    def _():
        sums[1:2, :] = one(2)


def project_kernel(normed, both, one, two_own, two_near, next_both, far_own, far_near, feats, message, weights):
    tokens = normed.shape[0] // 3
    rows = two_own.shape[0]
    z, x, _ = places()

    def put(plane, own, near):
        for place, values in ((x, own), (1 - x, near)):
            weights[pl.ds(pl.multiple_of((2 * plane + place) * rows, rows), rows), :] = values

    put(z, both[:rows, :], both[rows:, :])
    put(jnp.bitwise_xor(z, 1), one[:rows, :], one[rows:, :])
    put(jnp.bitwise_xor(z, 2), two_own[...], two_near[...])
    inner = jnp.logical_or(z == 1, z == 2)

    @pl.when(inner)
    def _():
        put(3 - z, next_both[:rows, :], next_both[rows:, :])

    @pl.when(jnp.logical_not(inner))
    def _():
        put(3 - z, far_own[...], far_near[...])

    wide = 2 * GROUP

    def one(slot, count):
        part = pl.ds(slot * tokens, count)
        out = jnp.dot(normed[part, :], weights[...], preferred_element_type=jnp.float32)
        raw = out[:, :wide]
        low = jnp.where(raw > 0.0, raw + 1.0, jnp.exp(jnp.minimum(raw, 0.0))).astype(jnp.bfloat16)
        feats[part, :wide] = low
        feats[part, wide:] = out[:, wide:].astype(jnp.bfloat16)
        return jnp.sum(low[:, GROUP:].astype(jnp.float32), axis=0, keepdims=True)

    high, low = split_two(one(0, tokens) + one(1, tokens))
    for h in range(GROUP // HEAD_DIM):
        at = h * HEAD_DIM
        key = feats[0 : 2 * tokens, GROUP + at : GROUP + at + HEAD_DIM]
        value = feats[0 : 2 * tokens, wide + at : wide + at + HEAD_DIM]
        state = lax.dot_general(key, value, DOT_T, preferred_element_type=jnp.float32)
        message[at : at + HEAD_DIM, :] = state.astype(jnp.bfloat16)
    total_rows = [high[:, :HEAD_DIM], high[:, HEAD_DIM:], low[:, :HEAD_DIM], low[:, HEAD_DIM:]]
    message[GROUP:, :] = jnp.concatenate(total_rows * 4, axis=0)

    @pl.when(z == 0)
    def _():
        one(2, tokens)


def pool_kernel(lengths, state_1, state_2, state_3, feats, sums, gain, part, short):
    tokens = feats.shape[0] // 3
    z, x, u = places()
    long_u = jnp.where(lengths[0, 0] > tokens, u, 1 - u)
    row = lax.broadcasted_iota(jnp.int32, (tokens, tokens), 0)
    col = lax.broadcasted_iota(jnp.int32, (tokens, tokens), 1)
    lower = (row >= col).astype(jnp.bfloat16)
    upper = (row <= col).astype(jnp.bfloat16)
    states = [(jnp.bitwise_xor(z, j) < z, ref) for j, ref in enumerate((state_1, state_2, state_3), 1)]
    before = jnp.zeros((1, GROUP), jnp.float32)
    for earlier, ref in states:
        rows = ref[GROUP : GROUP + 16, :].astype(jnp.float32)
        total = jnp.concatenate([rows[0:1] + rows[2:3], rows[1:2] + rows[3:4]], axis=1)
        before = before + jnp.where(earlier, total, 0.0)

    def block(slot, carry):
        at = pl.ds(slot * tokens, tokens)
        query = feats[at, :GROUP].astype(jnp.float32)
        key = feats[at, GROUP : 2 * GROUP]
        prefix = jnp.dot(lower, key, preferred_element_type=jnp.float32) + carry
        share = query / by_head(head_sums(query * prefix))
        return share, key, prefix[tokens - 1 : tokens, :]

    def suffix(share):
        high, low = split_two(share)
        return jnp.dot(upper, high, preferred_element_type=jnp.float32) + jnp.dot(
            upper, low, preferred_element_type=jnp.float32
        )

    def pooled(slot, key, after):
        weight = by_head(head_sums(key.astype(jnp.float32) * after))
        value = feats[pl.ds(slot * tokens, tokens), 2 * GROUP :].astype(jnp.float32)
        return jnp.sum(weight * value, axis=0, keepdims=True)

    share_one, key_one, carry = block(0, before)
    share_two, key_two, _ = block(1, carry)
    after_two = suffix(share_two)
    after_one = suffix(share_one) + after_two[0:1, :]
    long_row = pooled(0, key_one, after_one) + pooled(1, key_two, after_two) + sums[0:1, :]
    weight = after_one[0:1, :]
    for earlier, ref in states:
        high, low = split_two(jnp.where(earlier, weight, 0.0))
        products = []
        for h in range(GROUP // HEAD_DIM):
            at = h * HEAD_DIM
            both = jnp.concatenate([high[:, at : at + HEAD_DIM]] * 8 + [low[:, at : at + HEAD_DIM]] * 8, axis=0)
            out = jnp.dot(both, ref[at : at + HEAD_DIM, :], preferred_element_type=jnp.float32)
            products.append(out[0:1] + out[8:9])
        long_row = long_row + jnp.concatenate(products, axis=1)

    short[...] = sums[1:2, :]

    @pl.when(z == 0)
    def _():
        share, key, _ = block(2, jnp.zeros((1, GROUP), jnp.float32))
        short[...] = sums[1:2, :] + pooled(2, key, suffix(share))

    short_row = short[...]
    first = jnp.where(long_u == 0, long_row, short_row)
    second = jnp.where(long_u == 0, short_row, long_row)
    own_gain = gain[:, pl.ds(pl.multiple_of((2 * x + u) * GROUP, GROUP), GROUP)]
    rows = jnp.concatenate([first, second, own_gain, own_gain], axis=0)
    part[...] = jnp.broadcast_to(rows[None], part.shape)


def loss_kernel(positives, parts, vec, loss, mine, theirs):
    z, x, u = places()
    domain = lax.axis_index("domain")
    width = mine.shape[1]
    piece = vec.shape[2]

    def collect(place, dest):
        total = jnp.zeros((2, 1), jnp.float32)
        for group in range(PLANE):
            blocks = [parts[2 * (PLANE * plane + group) + place] for plane in range(PLANES)]
            values = (blocks[0][:2] + blocks[1][:2]) + (blocks[2][:2] + blocks[3][:2])
            total = total + jnp.sum(values * values, axis=1, keepdims=True)
            dest[:, group * GROUP : (group + 1) * GROUP] = values * blocks[0][2:3]
        factor = lax.rsqrt(total / width + epsilon)
        return (dest[...] * factor).astype(jnp.bfloat16).astype(jnp.float32)

    own = collect(domain, mine)
    other = collect(1 - domain, theirs)
    mine[...] = own
    start = pl.multiple_of((2 * z + x) * piece, piece)
    out = mine[:, pl.ds(start, piece)]
    vec[0] = jnp.where(u == 0, out[0:1], out[1:2]).astype(jnp.bfloat16)
    this = jnp.where(u == 0, own[0:1], own[1:2])
    logits = jnp.sum(this * other, axis=1, keepdims=True) * (logit_scale / width)
    top = jnp.max(logits, axis=0, keepdims=True)
    spread = jnp.log(jnp.sum(jnp.exp(logits - top), axis=0, keepdims=True)) + top
    forward = jnp.where(u == 0, positives[0], positives[1])
    backward = jnp.where(positives[0] == u, 0, 1)
    partner = jnp.where(domain == 0, forward, backward)
    rows = lax.broadcasted_iota(jnp.int32, (2, 1), 0)
    loss[...] = spread - jnp.sum(jnp.where(rows == partner, logits, 0.0), axis=0, keepdims=True)


def vmem():
    return pl.BlockSpec(memory_space=pltpu.VMEM)


def anywhere():
    return pl.BlockSpec(memory_space=pl.ANY)


def hbm():
    return pl.BlockSpec(memory_space=pltpu.HBM)


def smem():
    return pl.BlockSpec(memory_space=pltpu.SMEM)


def call(kernel, outs, in_specs, scratch, flops):
    return pl.pallas_call(
        kernel,
        out_shape=outs,
        in_specs=in_specs,
        out_specs=jax.tree.map(lambda _: vmem(), outs),
        scratch_shapes=scratch,
        compiler_params=pltpu.CompilerParams(vmem_limit_bytes=40 * 1024 * 1024),
        cost_estimate=pl.CostEstimate(flops=flops, bytes_accessed=2**21, transcendentals=0),
    )


def towers(history, qkv_weight, norm_gain, pool_gain, lengths, positives):
    events = history[0, 0]
    tokens, width = events.shape
    weight = qkv_weight[0]
    rows = weight.shape[0]
    f32, bf16 = jnp.float32, jnp.bfloat16
    shape = jax.ShapeDtypeStruct
    here = PLANE * PLANES

    def hop(a, target):
        pairs = [(i, target(i // PLANE) * PLANE + i % PLANE) for i in range(here) if target(i // PLANE) is not None]
        return lax.ppermute(a, ("seq", "dp"), pairs)

    def plane_hop(a, move):
        return lax.ppermute(a, ("seq", "dp"), [(i, i ^ move) for i in range(here)])

    def each(a):
        return [hop(a, lambda p: p ^ j) for j in range(1, PLANES)]

    wide = 3 * GROUP
    w_own, w_sent = call(
        pack_kernel, (shape((rows, wide), bf16),) * 2, [hbm()], [pltpu.SemaphoreType.DMA((6,))], 0
    )(weight)
    w_near = plane_hop(w_sent, 2)
    across = plane_hop(events, 1)
    two_own = hop(w_own, lambda p: p ^ 2)
    own, both = call(
        relay_kernel,
        (shape((tokens, width), bf16), shape((2 * rows, wide), bf16)),
        [hbm(), vmem(), vmem()],
        [pltpu.SemaphoreType.DMA(())],
        0,
    )(events, w_own, w_near)
    two_near = hop(w_near, lambda p: p ^ 2)
    next_both = hop(both, lambda p: 3 - p if p in (1, 2) else None)
    one = hop(both, lambda p: p ^ 1)
    near = plane_hop(own, 2)
    far_own = hop(two_own, lambda p: {1: 0, 2: 3}.get(p))
    far_near = hop(two_near, lambda p: {1: 0, 2: 3}.get(p))
    corner_a = plane_hop(across[: tokens // 2], 2)
    corner_b = plane_hop(near[tokens // 2 :], 1)

    normed, sums = call(
        norm_kernel,
        (shape((3 * tokens, width), bf16), shape((2, GROUP), f32)),
        [smem()] + [anywhere()] * 5 + [vmem()],
        [pltpu.VMEM((3, tokens, width), bf16), pltpu.SemaphoreType.DMA((3, 2))],
        2 * 3 * tokens * width,
    )(lengths, own, near, across, corner_a, corner_b, norm_gain)
    feats, message = call(
        project_kernel,
        (shape((3 * tokens, wide), bf16), shape((MESSAGE, HEAD_DIM), bf16)),
        [vmem()] * 8,
        [pltpu.VMEM((width, wide), bf16)],
        2 * 3 * tokens * width * wide,
    )(normed, both, one, two_own, two_near, next_both, far_own, far_near)
    part = call(
        pool_kernel,
        shape((2 * here, 4, GROUP), f32),
        [smem()] + [vmem()] * 6,
        [pltpu.VMEM((1, GROUP), f32)],
        2 * 9 * tokens * tokens * GROUP,
    )(lengths, *each(message), feats, sums, pool_gain)
    parts = lax.all_to_all(part, ("seq", "dp", "domain"), 0, 0, tiled=True)
    vec, loss = call(
        loss_kernel,
        (shape((1, 1, width // 8), bf16), shape((1, 1), f32)),
        [smem(), vmem()],
        [pltpu.VMEM((2, width), f32), pltpu.VMEM((2, width), f32)],
        2**14,
    )(positives, parts)
    return vec, loss


def solution(mesh):
    placed = (
        P("domain", "dp", "seq", None),
        P("domain", "seq", None),
        P("domain", None),
        P("domain", None),
        P("domain", "dp"),
        P(),
    )
    small = mesh.shape["seq"] == 2 * PLANES and mesh.shape["dp"] == 2
    return jax.shard_map(
        towers if small else shards,
        mesh=mesh,
        in_specs=placed,
        out_specs=(P("domain", "dp", "seq"), P("domain", "dp")),
        check_vma=False,
    )
```

```python
import functools

import jax
import jax.numpy as jnp
from jax import lax
from jax.experimental import pallas as pl
from jax.experimental.pallas import tpu as pltpu
from jax.sharding import PartitionSpec as P

HEADS = 8
HEAD_DIM = 128


logit_scale = 20.0
epsilon = 1e-06
highest = lax.Precision.HIGHEST


def carried_in(part, axis, combine, identity):
    place = lax.axis_index(axis)
    gathered = jax.tree.map(lambda a: lax.all_gather(a, axis), part)
    state = jax.tree.map(lambda a, e: jnp.zeros_like(a) + jnp.asarray(e, a.dtype), part, identity)

    def one(hop, state):
        return combine(
            state, jax.tree.map(lambda a: lax.dynamic_index_in_dim(a, hop, 0, False), gathered)
        )

    return lax.fori_loop(0, place, one, state)


def partner_2(block, axis, stride):
    count = lax.axis_size(axis)
    route = []
    for low in range(count):
        high = low | 1 << stride
        if high != low and high < count:
            route += [(low, high), (high, low)]
    return lax.ppermute(block, axis, route)


def feature_map(values):
    return jax.nn.elu(values) + 1.0


def add_pair(earlier, later):
    return (earlier[0] + later[0], earlier[1] + later[1])


def shards(history, qkv_weight, norm_gain, pool_gain, lengths, positives):
    seq_count = lax.axis_size("seq")
    seq_place = lax.axis_index("seq")
    group_place = lax.axis_index("dp")
    domain_place = lax.axis_index("domain")
    events = history[0]
    users_dev, tokens_dev, width = events.shape
    row_count = users_dev * tokens_dev
    wide = events.astype(jnp.float32)
    normed = (
        wide * lax.rsqrt(jnp.mean(wide * wide, -1, keepdims=True) + epsilon) * norm_gain[0]
    ).astype(jnp.bfloat16)
    normed = normed.reshape(row_count, width)
    rows_here = qkv_weight[0]
    projected = jnp.dot(
        normed,
        lax.all_gather(rows_here, "seq", axis=0, tiled=True),
        preferred_element_type=jnp.float32,
    )
    query_raw = projected[:, :width]
    key_raw = projected[:, width : 2 * width]
    value_raw = projected[:, 2 * width :]
    positions = seq_place * tokens_dev + jnp.arange(tokens_dev)
    valid = positions[None, :] < lengths[0][:, None]
    shape_heads = (users_dev, tokens_dev, HEADS, HEAD_DIM)
    queries = feature_map(query_raw).astype(jnp.bfloat16).reshape(shape_heads)
    key_feats = (
        jnp.where(valid.reshape(row_count)[:, None], feature_map(key_raw), 0.0)
        .astype(jnp.bfloat16)
        .reshape(shape_heads)
    )
    val_feats = value_raw.astype(jnp.bfloat16).reshape(shape_heads)
    local_state = jnp.einsum(
        "uthc,uthd->uhcd", key_feats, val_feats, preferred_element_type=jnp.float32
    )
    local_total = jnp.sum(key_feats.astype(jnp.float32), axis=1)
    state_before, total_before = carried_in(
        (local_state, local_total),
        "seq",
        add_pair,
        (jnp.zeros_like(local_state), jnp.zeros_like(local_total)),
    )
    causal = jnp.arange(tokens_dev)[:, None] >= jnp.arange(tokens_dev)[None, :]
    scores = jnp.einsum("uthc,ushc->uhts", queries, key_feats, preferred_element_type=jnp.float32)
    scores = jnp.where(causal, scores, 0.0)
    denominator = jnp.sum(scores, axis=-1) + jnp.einsum(
        "uthc,uhc->uht", queries.astype(jnp.float32), total_before, precision=highest
    )
    numerator = jnp.einsum(
        "uhts,ushc->uthc",
        scores.astype(jnp.bfloat16),
        val_feats,
        preferred_element_type=jnp.float32,
    )
    numerator = numerator + jnp.einsum(
        "uthc,uhcd->uthd",
        queries,
        state_before.astype(jnp.bfloat16),
        preferred_element_type=jnp.float32,
    )
    attended = numerator / jnp.transpose(denominator, (0, 2, 1))[..., None]
    attended = attended.reshape(users_dev, tokens_dev, width)
    partial_value = jnp.sum(jnp.where(valid[..., None], wide + attended, 0.0), axis=1)
    piece_width = width // seq_count
    gain_row = pool_gain[0]
    pooled = lax.psum(partial_value, "seq")
    factor = lax.rsqrt(jnp.mean(pooled * pooled, -1, keepdims=True) + epsilon)
    full_vec = (pooled * factor * gain_row).astype(jnp.bfloat16)
    out_vec = lax.dynamic_slice_in_dim(full_vec, seq_place * piece_width, piece_width, 1)
    group = lax.all_gather(full_vec, "dp", axis=0, tiled=True)
    other = partner_2(group, "domain", 0)
    logits = jnp.einsum("uc,vc->uv", full_vec, other, preferred_element_type=jnp.float32) * (
        logit_scale / width
    )
    users_all = other.shape[0]
    own_index = group_place * users_dev + jnp.arange(users_dev)
    targets = lax.dynamic_slice_in_dim(positives, group_place * users_dev, users_dev)
    forward_pair = targets[:, None] == jnp.arange(users_all)[None, :]
    backward_pair = positives[None, :] == own_index[:, None]
    partner = jnp.where(domain_place == 0, forward_pair, backward_pair)
    loss = jnp.log(jnp.sum(jnp.exp(logits), axis=-1)) - jnp.sum(
        jnp.where(partner, logits, 0.0), axis=-1
    )
    return (out_vec[None], loss[None])


PLANE = 4
PLANES = 4
GROUP = 256
DOT_T = (((0,), (0,)), ((), ()))
MESSAGE = GROUP + 16


def places():
    seq_place = lax.axis_index("seq")
    return lax.div(seq_place, 2), lax.rem(seq_place, 2), lax.axis_index("dp")


def head_sums(a):
    return [
        jnp.sum(a[:, h * HEAD_DIM : (h + 1) * HEAD_DIM], axis=1, keepdims=True)
        for h in range(GROUP // HEAD_DIM)
    ]


def by_head(columns):
    rows = columns[0].shape[0]
    return jnp.concatenate([jnp.broadcast_to(c, (rows, HEAD_DIM)) for c in columns], axis=1)


def split_two(a):
    high = a.astype(jnp.bfloat16)
    return high, (a - high.astype(jnp.float32)).astype(jnp.bfloat16)


def pack_kernel(weight, own, sent, sems):
    _, x, u = places()
    width = weight.shape[1] // 3
    copies = []
    for move, out in ((2, sent), (0, own)):
        group = jnp.bitwise_xor(2 * x + u, move)
        for part in range(3):
            start = pl.multiple_of(part * width + group * GROUP, GROUP)
            copies.append(
                pltpu.make_async_copy(
                    weight.at[:, pl.ds(start, GROUP)], out.at[:, pl.ds(part * GROUP, GROUP)], sems.at[len(copies)]
                )
            )
    for copy in copies:
        copy.start()
    for copy in copies:
        copy.wait()


def gate_kernel(values, after, out):
    del after
    out[...] = values[...]


def normalise(values, gain):
    wide = values.astype(jnp.float32)
    scale = lax.rsqrt(jnp.mean(wide * wide, axis=1, keepdims=True) + epsilon)
    return (wide * scale * gain).astype(jnp.bfloat16)


def features(normed, weights):
    out = jnp.dot(normed, weights, preferred_element_type=jnp.float32)
    raw = out[:, : 2 * GROUP]
    low = jnp.where(raw > 0.0, raw + 1.0, jnp.exp(jnp.minimum(raw, 0.0))).astype(jnp.bfloat16)
    return low[:, :GROUP], low[:, GROUP:], out[:, 2 * GROUP :].astype(jnp.bfloat16)


def norm_kernel(lengths, own, near, across, corner, gain, normed, sums, short, raw, sems):
    tokens = own.shape[0]
    _, x, u = places()
    long_u = jnp.where(lengths[0, 0] > tokens, u, 1 - u)
    for slot in range(3):
        from_x = 1 if slot == 1 else 0
        from_u = 1 - long_u if slot == 2 else long_u
        pick = jnp.bitwise_xor(x, from_x) + 2 * jnp.bitwise_xor(u, from_u)
        dest = short if slot == 2 else raw.at[slot]
        for j, ref in enumerate((own, near, across, corner)):

            @pl.when(pick == j)
            def _():
                pltpu.make_async_copy(ref, dest, sems.at[slot]).start()

    columns = pl.ds(pl.multiple_of((2 * x + u) * GROUP, GROUP), GROUP)
    total = jnp.zeros((1, GROUP), jnp.float32)
    for slot in range(2):
        pltpu.make_async_copy(own, raw.at[slot], sems.at[slot]).wait()
        normed[pl.ds(slot * tokens, tokens), :] = normalise(raw[slot], gain[...])
        total = total + jnp.sum(raw[slot, :, columns].astype(jnp.float32), axis=0, keepdims=True)
    sums[...] = total
    pltpu.make_async_copy(own, short, sems.at[2]).wait()


def project_kernel(normed, both, one, two_own, two_near, next_both, far_own, far_near, feats, message, weights):
    tokens = normed.shape[0]
    rows = two_own.shape[0]
    z, x, _ = places()

    def put(plane, own, near):
        for place, values in ((x, own), (1 - x, near)):
            weights[pl.ds(pl.multiple_of((2 * plane + place) * rows, rows), rows), :] = values

    put(z, both[:rows, :], both[rows:, :])
    put(jnp.bitwise_xor(z, 1), one[:rows, :], one[rows:, :])
    put(jnp.bitwise_xor(z, 2), two_own[...], two_near[...])
    inner = jnp.logical_or(z == 1, z == 2)

    @pl.when(inner)
    def _():
        put(3 - z, next_both[:rows, :], next_both[rows:, :])

    @pl.when(jnp.logical_not(inner))
    def _():
        put(3 - z, far_own[...], far_near[...])

    half = tokens // 2
    total = jnp.zeros((1, GROUP), jnp.float32)
    for part in range(2):
        at = pl.ds(part * half, half)
        query, key, value = features(normed[at, :], weights[...])
        feats[at, :GROUP] = query
        feats[at, GROUP : 2 * GROUP] = key
        feats[at, 2 * GROUP :] = value
        total = total + jnp.sum(key.astype(jnp.float32), axis=0, keepdims=True)
    high, low = split_two(total)
    for h in range(GROUP // HEAD_DIM):
        at = h * HEAD_DIM
        key = feats[:, GROUP + at : GROUP + at + HEAD_DIM]
        value = feats[:, 2 * GROUP + at : 2 * GROUP + at + HEAD_DIM]
        state = lax.dot_general(key, value, DOT_T, preferred_element_type=jnp.float32)
        message[at : at + HEAD_DIM, :] = state.astype(jnp.bfloat16)
    total_rows = [high[:, :HEAD_DIM], high[:, HEAD_DIM:], low[:, :HEAD_DIM], low[:, HEAD_DIM:]]
    message[GROUP:, :] = jnp.concatenate(total_rows * 4, axis=0)


def triangle(tokens, upper):
    row = lax.broadcasted_iota(jnp.int32, (tokens, tokens), 0)
    col = lax.broadcasted_iota(jnp.int32, (tokens, tokens), 1)
    return (row <= col if upper else row >= col).astype(jnp.bfloat16)


def shares(query, key, carry):
    prefix = jnp.dot(triangle(key.shape[0], False), key, preferred_element_type=jnp.float32) + carry
    wide = query.astype(jnp.float32)
    return wide / by_head(head_sums(wide * prefix)), prefix[key.shape[0] - 1 :, :]


def suffix(share):
    upper = triangle(share.shape[0], True)
    high, low = split_two(share)
    return jnp.dot(upper, high, preferred_element_type=jnp.float32) + jnp.dot(
        upper, low, preferred_element_type=jnp.float32
    )


def weighted(key, value, after):
    weight = by_head(head_sums(key.astype(jnp.float32) * after))
    return jnp.sum(weight * value.astype(jnp.float32), axis=0, keepdims=True)


def short_kernel(raw, weights, gain, out):
    z, x, u = places()
    out[...] = jnp.zeros(out.shape, jnp.float32)

    @pl.when(z == 0)
    def _():
        query, key, value = features(normalise(raw[...], gain[...]), weights[...])
        share, _ = shares(query, key, jnp.zeros((1, GROUP), jnp.float32))
        columns = pl.ds(pl.multiple_of((2 * x + u) * GROUP, GROUP), GROUP)
        own = jnp.sum(raw[:, columns].astype(jnp.float32), axis=0, keepdims=True)
        out[...] = own + weighted(key, value, suffix(share))


def pool_kernel(lengths, state_1, state_2, state_3, feats, sums, short, gain, part):
    tokens = feats.shape[0] // 2
    z, x, u = places()
    long_u = jnp.where(lengths[0, 0] > tokens, u, 1 - u)
    states = [(jnp.bitwise_xor(z, j) < z, ref) for j, ref in enumerate((state_1, state_2, state_3), 1)]
    before = jnp.zeros((1, GROUP), jnp.float32)
    for earlier, ref in states:
        rows = ref[GROUP : GROUP + 16, :].astype(jnp.float32)
        total = jnp.concatenate([rows[0:1] + rows[2:3], rows[1:2] + rows[3:4]], axis=1)
        before = before + jnp.where(earlier, total, 0.0)

    def block(slot):
        at = pl.ds(slot * tokens, tokens)
        return feats[at, :GROUP], feats[at, GROUP : 2 * GROUP], feats[at, 2 * GROUP :]

    query_one, key_one, value_one = block(0)
    query_two, key_two, value_two = block(1)
    share_one, carry = shares(query_one, key_one, before)
    share_two, _ = shares(query_two, key_two, carry)
    after_two = suffix(share_two)
    after_one = suffix(share_one) + after_two[0:1, :]
    long_row = weighted(key_one, value_one, after_one) + weighted(key_two, value_two, after_two) + sums[...]
    weight = after_one[0:1, :]
    for earlier, ref in states:
        high, low = split_two(jnp.where(earlier, weight, 0.0))
        products = []
        for h in range(GROUP // HEAD_DIM):
            at = h * HEAD_DIM
            both = jnp.concatenate([high[:, at : at + HEAD_DIM]] * 8 + [low[:, at : at + HEAD_DIM]] * 8, axis=0)
            out = jnp.dot(both, ref[at : at + HEAD_DIM, :], preferred_element_type=jnp.float32)
            products.append(out[0:1] + out[8:9])
        long_row = long_row + jnp.concatenate(products, axis=1)

    short_row = short[...]
    first = jnp.where(long_u == 0, long_row, short_row)
    second = jnp.where(long_u == 0, short_row, long_row)
    own_gain = gain[:, pl.ds(pl.multiple_of((2 * x + u) * GROUP, GROUP), GROUP)]
    rows = jnp.concatenate([first, second, own_gain, own_gain], axis=0)
    part[...] = jnp.broadcast_to(rows[None], part.shape)


def loss_kernel(positives, parts, vec, loss, mine, theirs):
    z, x, u = places()
    domain = lax.axis_index("domain")
    width = mine.shape[1]
    piece = vec.shape[2]

    def collect(place, dest):
        total = jnp.zeros((2, 1), jnp.float32)
        for group in range(PLANE):
            blocks = [parts[2 * (PLANE * plane + group) + place] for plane in range(PLANES)]
            values = (blocks[0][:2] + blocks[1][:2]) + (blocks[2][:2] + blocks[3][:2])
            total = total + jnp.sum(values * values, axis=1, keepdims=True)
            dest[:, group * GROUP : (group + 1) * GROUP] = values * blocks[0][2:3]
        factor = lax.rsqrt(total / width + epsilon)
        return (dest[...] * factor).astype(jnp.bfloat16).astype(jnp.float32)

    own = collect(domain, mine)
    other = collect(1 - domain, theirs)
    mine[...] = own
    start = pl.multiple_of((2 * z + x) * piece, piece)
    out = mine[:, pl.ds(start, piece)]
    vec[0] = jnp.where(u == 0, out[0:1], out[1:2]).astype(jnp.bfloat16)
    this = jnp.where(u == 0, own[0:1], own[1:2])
    logits = jnp.sum(this * other, axis=1, keepdims=True) * (logit_scale / width)
    top = jnp.max(logits, axis=0, keepdims=True)
    spread = jnp.log(jnp.sum(jnp.exp(logits - top), axis=0, keepdims=True)) + top
    forward = jnp.where(u == 0, positives[0], positives[1])
    backward = jnp.where(positives[0] == u, 0, 1)
    partner = jnp.where(domain == 0, forward, backward)
    rows = lax.broadcasted_iota(jnp.int32, (2, 1), 0)
    loss[...] = spread - jnp.sum(jnp.where(rows == partner, logits, 0.0), axis=0, keepdims=True)


def vmem():
    return pl.BlockSpec(memory_space=pltpu.VMEM)


def anywhere():
    return pl.BlockSpec(memory_space=pl.ANY)


def hbm():
    return pl.BlockSpec(memory_space=pltpu.HBM)


def smem():
    return pl.BlockSpec(memory_space=pltpu.SMEM)


def call(kernel, outs, in_specs, scratch, flops):
    return pl.pallas_call(
        kernel,
        out_shape=outs,
        in_specs=in_specs,
        out_specs=jax.tree.map(lambda _: vmem(), outs),
        scratch_shapes=scratch,
        compiler_params=pltpu.CompilerParams(vmem_limit_bytes=40 * 1024 * 1024),
        cost_estimate=pl.CostEstimate(flops=flops, bytes_accessed=2**21, transcendentals=0),
    )


def towers(history, qkv_weight, norm_gain, pool_gain, lengths, positives):
    events = history[0, 0]
    tokens, width = events.shape
    weight = qkv_weight[0]
    rows = weight.shape[0]
    f32, bf16 = jnp.float32, jnp.bfloat16
    shape = jax.ShapeDtypeStruct
    here = PLANE * PLANES

    def hop(a, target):
        pairs = [(i, target(i // PLANE) * PLANE + i % PLANE) for i in range(here) if target(i // PLANE) is not None]
        return lax.ppermute(a, ("seq", "dp"), pairs)

    def plane_hop(a, move):
        return lax.ppermute(a, ("seq", "dp"), [(i, i ^ move) for i in range(here)])

    def each(a):
        return [hop(a, lambda p: p ^ j) for j in range(1, PLANES)]

    wide = 3 * GROUP
    w_own, w_sent = call(
        pack_kernel, (shape((rows, wide), bf16),) * 2, [hbm()], [pltpu.SemaphoreType.DMA((6,))], 0
    )(weight)
    near = plane_hop(events, 2)
    across = plane_hop(events, 1)
    corner = plane_hop(events, 3)
    w_near = plane_hop(w_sent, 2)
    two_own = hop(w_own, lambda p: p ^ 2)
    two_near = hop(w_near, lambda p: p ^ 2)
    both = jnp.concatenate([w_own, w_near], axis=0)
    one_own = hop(w_own, lambda p: p ^ 1)
    one_near = hop(w_near, lambda p: p ^ 1)
    one = jnp.concatenate([one_own, one_near], axis=0)
    next_both = hop(both, lambda p: 3 - p if p in (1, 2) else None)
    far_own = hop(two_own, lambda p: {1: 0, 2: 3}.get(p))
    far_near = hop(two_near, lambda p: {1: 0, 2: 3}.get(p))

    normed, sums, raw_short = call(
        norm_kernel,
        (shape((2 * tokens, width), bf16), shape((1, GROUP), f32), shape((tokens, width), bf16)),
        [smem()] + [anywhere()] * 4 + [vmem()],
        [pltpu.VMEM((2, tokens, width), bf16), pltpu.SemaphoreType.DMA((3,))],
        2 * 3 * tokens * width,
    )(lengths, events, near, across, corner, norm_gain)
    feats, message, weights = call(
        project_kernel,
        (shape((2 * tokens, wide), bf16), shape((MESSAGE, HEAD_DIM), bf16), shape((width, wide), bf16)),
        [vmem()] * 8,
        [],
        2 * 2 * tokens * width * wide,
    )(normed, both, one, two_own, two_near, next_both, far_own, far_near)
    short = call(
        short_kernel, shape((1, GROUP), f32), [vmem()] * 3, [], 2 * tokens * width * wide
    )(raw_short, weights, norm_gain)
    part = call(
        pool_kernel,
        shape((2 * here, 4, GROUP), f32),
        [smem()] + [vmem()] * 7,
        [],
        2 * 9 * tokens * tokens * GROUP,
    )(lengths, *each(message), feats, sums, short, pool_gain)
    parts = lax.all_to_all(part, ("seq", "dp", "domain"), 0, 0, tiled=True)
    vec, loss = call(
        loss_kernel,
        (shape((1, 1, width // 8), bf16), shape((1, 1), f32)),
        [smem(), vmem()],
        [pltpu.VMEM((2, width), f32), pltpu.VMEM((2, width), f32)],
        2**14,
    )(positives, parts)
    return vec, loss


def solution(mesh):
    placed = (
        P("domain", "dp", "seq", None),
        P("domain", "seq", None),
        P("domain", None),
        P("domain", None),
        P("domain", "dp"),
        P(),
    )
    small = mesh.shape["seq"] == 2 * PLANES and mesh.shape["dp"] == 2
    return jax.shard_map(
        towers if small else shards,
        mesh=mesh,
        in_specs=placed,
        out_specs=(P("domain", "dp", "seq"), P("domain", "dp")),
        check_vma=False,
    )
```

```python
import functools

import jax
import jax.numpy as jnp
from jax import lax
from jax.experimental import pallas as pl
from jax.experimental.pallas import tpu as pltpu
from jax.sharding import PartitionSpec as P

HEADS = 8
HEAD_DIM = 128


logit_scale = 20.0
epsilon = 1e-06
highest = lax.Precision.HIGHEST


def carried_in(part, axis, combine, identity):
    place = lax.axis_index(axis)
    gathered = jax.tree.map(lambda a: lax.all_gather(a, axis), part)
    state = jax.tree.map(lambda a, e: jnp.zeros_like(a) + jnp.asarray(e, a.dtype), part, identity)

    def one(hop, state):
        return combine(
            state, jax.tree.map(lambda a: lax.dynamic_index_in_dim(a, hop, 0, False), gathered)
        )

    return lax.fori_loop(0, place, one, state)


def partner_2(block, axis, stride):
    count = lax.axis_size(axis)
    route = []
    for low in range(count):
        high = low | 1 << stride
        if high != low and high < count:
            route += [(low, high), (high, low)]
    return lax.ppermute(block, axis, route)


def feature_map(values):
    return jax.nn.elu(values) + 1.0


def add_pair(earlier, later):
    return (earlier[0] + later[0], earlier[1] + later[1])


def shards(history, qkv_weight, norm_gain, pool_gain, lengths, positives):
    seq_count = lax.axis_size("seq")
    seq_place = lax.axis_index("seq")
    group_place = lax.axis_index("dp")
    domain_place = lax.axis_index("domain")
    events = history[0]
    users_dev, tokens_dev, width = events.shape
    row_count = users_dev * tokens_dev
    wide = events.astype(jnp.float32)
    normed = (
        wide * lax.rsqrt(jnp.mean(wide * wide, -1, keepdims=True) + epsilon) * norm_gain[0]
    ).astype(jnp.bfloat16)
    normed = normed.reshape(row_count, width)
    rows_here = qkv_weight[0]
    projected = jnp.dot(
        normed,
        lax.all_gather(rows_here, "seq", axis=0, tiled=True),
        preferred_element_type=jnp.float32,
    )
    query_raw = projected[:, :width]
    key_raw = projected[:, width : 2 * width]
    value_raw = projected[:, 2 * width :]
    positions = seq_place * tokens_dev + jnp.arange(tokens_dev)
    valid = positions[None, :] < lengths[0][:, None]
    shape_heads = (users_dev, tokens_dev, HEADS, HEAD_DIM)
    queries = feature_map(query_raw).astype(jnp.bfloat16).reshape(shape_heads)
    key_feats = (
        jnp.where(valid.reshape(row_count)[:, None], feature_map(key_raw), 0.0)
        .astype(jnp.bfloat16)
        .reshape(shape_heads)
    )
    val_feats = value_raw.astype(jnp.bfloat16).reshape(shape_heads)
    local_state = jnp.einsum(
        "uthc,uthd->uhcd", key_feats, val_feats, preferred_element_type=jnp.float32
    )
    local_total = jnp.sum(key_feats.astype(jnp.float32), axis=1)
    state_before, total_before = carried_in(
        (local_state, local_total),
        "seq",
        add_pair,
        (jnp.zeros_like(local_state), jnp.zeros_like(local_total)),
    )
    causal = jnp.arange(tokens_dev)[:, None] >= jnp.arange(tokens_dev)[None, :]
    scores = jnp.einsum("uthc,ushc->uhts", queries, key_feats, preferred_element_type=jnp.float32)
    scores = jnp.where(causal, scores, 0.0)
    denominator = jnp.sum(scores, axis=-1) + jnp.einsum(
        "uthc,uhc->uht", queries.astype(jnp.float32), total_before, precision=highest
    )
    numerator = jnp.einsum(
        "uhts,ushc->uthc",
        scores.astype(jnp.bfloat16),
        val_feats,
        preferred_element_type=jnp.float32,
    )
    numerator = numerator + jnp.einsum(
        "uthc,uhcd->uthd",
        queries,
        state_before.astype(jnp.bfloat16),
        preferred_element_type=jnp.float32,
    )
    attended = numerator / jnp.transpose(denominator, (0, 2, 1))[..., None]
    attended = attended.reshape(users_dev, tokens_dev, width)
    partial_value = jnp.sum(jnp.where(valid[..., None], wide + attended, 0.0), axis=1)
    piece_width = width // seq_count
    gain_row = pool_gain[0]
    pooled = lax.psum(partial_value, "seq")
    factor = lax.rsqrt(jnp.mean(pooled * pooled, -1, keepdims=True) + epsilon)
    full_vec = (pooled * factor * gain_row).astype(jnp.bfloat16)
    out_vec = lax.dynamic_slice_in_dim(full_vec, seq_place * piece_width, piece_width, 1)
    group = lax.all_gather(full_vec, "dp", axis=0, tiled=True)
    other = partner_2(group, "domain", 0)
    logits = jnp.einsum("uc,vc->uv", full_vec, other, preferred_element_type=jnp.float32) * (
        logit_scale / width
    )
    users_all = other.shape[0]
    own_index = group_place * users_dev + jnp.arange(users_dev)
    targets = lax.dynamic_slice_in_dim(positives, group_place * users_dev, users_dev)
    forward_pair = targets[:, None] == jnp.arange(users_all)[None, :]
    backward_pair = positives[None, :] == own_index[:, None]
    partner = jnp.where(domain_place == 0, forward_pair, backward_pair)
    loss = jnp.log(jnp.sum(jnp.exp(logits), axis=-1)) - jnp.sum(
        jnp.where(partner, logits, 0.0), axis=-1
    )
    return (out_vec[None], loss[None])


PLANE = 4
PLANES = 4
GROUP = 256
DOT_T = (((0,), (0,)), ((), ()))
MESSAGE = GROUP + 16


def places():
    seq_place = lax.axis_index("seq")
    return lax.div(seq_place, 2), lax.rem(seq_place, 2), lax.axis_index("dp")


def head_sums(a):
    return [
        jnp.sum(a[:, h * HEAD_DIM : (h + 1) * HEAD_DIM], axis=1, keepdims=True)
        for h in range(GROUP // HEAD_DIM)
    ]


def by_head(columns):
    rows = columns[0].shape[0]
    return jnp.concatenate([jnp.broadcast_to(c, (rows, HEAD_DIM)) for c in columns], axis=1)


def split_two(a):
    high = a.astype(jnp.bfloat16)
    return high, (a - high.astype(jnp.float32)).astype(jnp.bfloat16)


def pack_kernel(weight, own, sent, sems):
    _, x, u = places()
    width = weight.shape[1] // 3
    copies = []
    for move, out in ((2, sent), (0, own)):
        group = jnp.bitwise_xor(2 * x + u, move)
        for part in range(3):
            start = pl.multiple_of(part * width + group * GROUP, GROUP)
            copies.append(
                pltpu.make_async_copy(
                    weight.at[:, pl.ds(start, GROUP)], out.at[:, pl.ds(part * GROUP, GROUP)], sems.at[len(copies)]
                )
            )
    for copy in copies:
        copy.start()
    for copy in copies:
        copy.wait()


def gate_kernel(values, *rest):
    rest[-1][...] = values[...]


def normalise(values, gain):
    wide = values.astype(jnp.float32)
    scale = lax.rsqrt(jnp.mean(wide * wide, axis=1, keepdims=True) + epsilon)
    return (wide * scale * gain).astype(jnp.bfloat16)


def features(normed, weights):
    out = jnp.dot(normed, weights, preferred_element_type=jnp.float32)
    raw = out[:, : 2 * GROUP]
    low = jnp.where(raw > 0.0, raw + 1.0, jnp.exp(jnp.minimum(raw, 0.0))).astype(jnp.bfloat16)
    return low[:, :GROUP], low[:, GROUP:], out[:, 2 * GROUP :].astype(jnp.bfloat16)


def norm_kernel(lengths, own, near, across, corner, gain, normed, sums, short, raw, sems):
    tokens = own.shape[0]
    _, x, u = places()
    long_u = jnp.where(lengths[0, 0] > tokens, u, 1 - u)
    for slot in range(3):
        from_x = 1 if slot == 1 else 0
        from_u = 1 - long_u if slot == 2 else long_u
        pick = jnp.bitwise_xor(x, from_x) + 2 * jnp.bitwise_xor(u, from_u)
        dest = short if slot == 2 else raw.at[slot]
        for j, ref in enumerate((own, near, across, corner)):

            @pl.when(pick == j)
            def _():
                pltpu.make_async_copy(ref, dest, sems.at[slot]).start()

    columns = pl.ds(pl.multiple_of((2 * x + u) * GROUP, GROUP), GROUP)
    total = jnp.zeros((1, GROUP), jnp.float32)
    for slot in range(2):
        pltpu.make_async_copy(own, raw.at[slot], sems.at[slot]).wait()
        normed[pl.ds(slot * tokens, tokens), :] = normalise(raw[slot], gain[...])
        total = total + jnp.sum(raw[slot, :, columns].astype(jnp.float32), axis=0, keepdims=True)
    sums[...] = total
    pltpu.make_async_copy(own, short, sems.at[2]).wait()


def project_kernel(normed, *refs):
    own, near, one_own, one_near, next_own, next_near, then_own, then_near, far_own, far_near, last_own, last_near = refs[:12]
    feats, message, weights = refs[12:]
    tokens = normed.shape[0]
    rows = own.shape[0]
    z, x, _ = places()

    def put(plane, here, there):
        for place, ref in ((x, here), (1 - x, there)):
            weights[pl.ds(pl.multiple_of((2 * plane + place) * rows, rows), rows), :] = ref[...]

    put(z, own, near)
    put(jnp.bitwise_xor(z, 1), one_own, one_near)
    inner = jnp.logical_or(z == 1, z == 2)

    @pl.when(inner)
    def _():
        put(3 - z, next_own, next_near)
        put(jnp.bitwise_xor(z, 2), far_own, far_near)

    @pl.when(jnp.logical_not(inner))
    def _():
        put(jnp.bitwise_xor(z, 2), then_own, then_near)
        put(3 - z, last_own, last_near)

    half = tokens // 2
    total = jnp.zeros((1, GROUP), jnp.float32)
    for part in range(2):
        at = pl.ds(part * half, half)
        query, key, value = features(normed[at, :], weights[...])
        feats[at, :GROUP] = query
        feats[at, GROUP : 2 * GROUP] = key
        feats[at, 2 * GROUP :] = value
        total = total + jnp.sum(key.astype(jnp.float32), axis=0, keepdims=True)
    high, low = split_two(total)
    for h in range(GROUP // HEAD_DIM):
        at = h * HEAD_DIM
        key = feats[:, GROUP + at : GROUP + at + HEAD_DIM]
        value = feats[:, 2 * GROUP + at : 2 * GROUP + at + HEAD_DIM]
        state = lax.dot_general(key, value, DOT_T, preferred_element_type=jnp.float32)
        message[at : at + HEAD_DIM, :] = state.astype(jnp.bfloat16)
    total_rows = [high[:, :HEAD_DIM], high[:, HEAD_DIM:], low[:, :HEAD_DIM], low[:, HEAD_DIM:]]
    message[GROUP:, :] = jnp.concatenate(total_rows * 4, axis=0)


def triangle(tokens, upper):
    row = lax.broadcasted_iota(jnp.int32, (tokens, tokens), 0)
    col = lax.broadcasted_iota(jnp.int32, (tokens, tokens), 1)
    return (row <= col if upper else row >= col).astype(jnp.bfloat16)


def shares(query, key, carry):
    prefix = jnp.dot(triangle(key.shape[0], False), key, preferred_element_type=jnp.float32) + carry
    wide = query.astype(jnp.float32)
    return wide / by_head(head_sums(wide * prefix)), prefix[key.shape[0] - 1 :, :]


def suffix(share):
    upper = triangle(share.shape[0], True)
    high, low = split_two(share)
    return jnp.dot(upper, high, preferred_element_type=jnp.float32) + jnp.dot(
        upper, low, preferred_element_type=jnp.float32
    )


def weighted(key, value, after):
    weight = by_head(head_sums(key.astype(jnp.float32) * after))
    return jnp.sum(weight * value.astype(jnp.float32), axis=0, keepdims=True)


def short_kernel(raw, weights, gain, out):
    z, x, u = places()
    out[...] = jnp.zeros(out.shape, jnp.float32)

    @pl.when(z == 0)
    def _():
        query, key, value = features(normalise(raw[...], gain[...]), weights[...])
        share, _ = shares(query, key, jnp.zeros((1, GROUP), jnp.float32))
        columns = pl.ds(pl.multiple_of((2 * x + u) * GROUP, GROUP), GROUP)
        own = jnp.sum(raw[:, columns].astype(jnp.float32), axis=0, keepdims=True)
        out[...] = own + weighted(key, value, suffix(share))


def pool_kernel(lengths, state_1, state_2, state_3, feats, sums, short, gain, part):
    tokens = feats.shape[0] // 2
    z, x, u = places()
    long_u = jnp.where(lengths[0, 0] > tokens, u, 1 - u)
    states = [(jnp.bitwise_xor(z, j) < z, ref) for j, ref in enumerate((state_1, state_2, state_3), 1)]
    before = jnp.zeros((1, GROUP), jnp.float32)
    for earlier, ref in states:
        rows = ref[GROUP : GROUP + 16, :].astype(jnp.float32)
        total = jnp.concatenate([rows[0:1] + rows[2:3], rows[1:2] + rows[3:4]], axis=1)
        before = before + jnp.where(earlier, total, 0.0)

    def block(slot):
        at = pl.ds(slot * tokens, tokens)
        return feats[at, :GROUP], feats[at, GROUP : 2 * GROUP], feats[at, 2 * GROUP :]

    query_one, key_one, value_one = block(0)
    query_two, key_two, value_two = block(1)
    share_one, carry = shares(query_one, key_one, before)
    share_two, _ = shares(query_two, key_two, carry)
    after_two = suffix(share_two)
    after_one = suffix(share_one) + after_two[0:1, :]
    long_row = weighted(key_one, value_one, after_one) + weighted(key_two, value_two, after_two) + sums[...]
    weight = after_one[0:1, :]
    for earlier, ref in states:
        high, low = split_two(jnp.where(earlier, weight, 0.0))
        products = []
        for h in range(GROUP // HEAD_DIM):
            at = h * HEAD_DIM
            both = jnp.concatenate([high[:, at : at + HEAD_DIM]] * 8 + [low[:, at : at + HEAD_DIM]] * 8, axis=0)
            out = jnp.dot(both, ref[at : at + HEAD_DIM, :], preferred_element_type=jnp.float32)
            products.append(out[0:1] + out[8:9])
        long_row = long_row + jnp.concatenate(products, axis=1)

    short_row = short[...]
    first = jnp.where(long_u == 0, long_row, short_row)
    second = jnp.where(long_u == 0, short_row, long_row)
    own_gain = gain[:, pl.ds(pl.multiple_of((2 * x + u) * GROUP, GROUP), GROUP)]
    rows = jnp.concatenate([first, second, own_gain, own_gain], axis=0)
    part[...] = jnp.broadcast_to(rows[None], part.shape)


def loss_kernel(positives, parts, vec, loss, mine, theirs):
    z, x, u = places()
    domain = lax.axis_index("domain")
    width = mine.shape[1]
    piece = vec.shape[2]

    def collect(place, dest):
        total = jnp.zeros((2, 1), jnp.float32)
        for group in range(PLANE):
            blocks = [parts[2 * (PLANE * plane + group) + place] for plane in range(PLANES)]
            values = (blocks[0][:2] + blocks[1][:2]) + (blocks[2][:2] + blocks[3][:2])
            total = total + jnp.sum(values * values, axis=1, keepdims=True)
            dest[:, group * GROUP : (group + 1) * GROUP] = values * blocks[0][2:3]
        factor = lax.rsqrt(total / width + epsilon)
        return (dest[...] * factor).astype(jnp.bfloat16).astype(jnp.float32)

    own = collect(domain, mine)
    other = collect(1 - domain, theirs)
    mine[...] = own
    start = pl.multiple_of((2 * z + x) * piece, piece)
    out = mine[:, pl.ds(start, piece)]
    vec[0] = jnp.where(u == 0, out[0:1], out[1:2]).astype(jnp.bfloat16)
    this = jnp.where(u == 0, own[0:1], own[1:2])
    logits = jnp.sum(this * other, axis=1, keepdims=True) * (logit_scale / width)
    top = jnp.max(logits, axis=0, keepdims=True)
    spread = jnp.log(jnp.sum(jnp.exp(logits - top), axis=0, keepdims=True)) + top
    forward = jnp.where(u == 0, positives[0], positives[1])
    backward = jnp.where(positives[0] == u, 0, 1)
    partner = jnp.where(domain == 0, forward, backward)
    rows = lax.broadcasted_iota(jnp.int32, (2, 1), 0)
    loss[...] = spread - jnp.sum(jnp.where(rows == partner, logits, 0.0), axis=0, keepdims=True)


def vmem():
    return pl.BlockSpec(memory_space=pltpu.VMEM)


def anywhere():
    return pl.BlockSpec(memory_space=pl.ANY)


def hbm():
    return pl.BlockSpec(memory_space=pltpu.HBM)


def smem():
    return pl.BlockSpec(memory_space=pltpu.SMEM)


def call(kernel, outs, in_specs, scratch, flops):
    return pl.pallas_call(
        kernel,
        out_shape=outs,
        in_specs=in_specs,
        out_specs=jax.tree.map(lambda _: vmem(), outs),
        scratch_shapes=scratch,
        compiler_params=pltpu.CompilerParams(vmem_limit_bytes=40 * 1024 * 1024),
        cost_estimate=pl.CostEstimate(flops=flops, bytes_accessed=2**21, transcendentals=0),
    )


def towers(history, qkv_weight, norm_gain, pool_gain, lengths, positives):
    events = history[0, 0]
    tokens, width = events.shape
    weight = qkv_weight[0]
    rows = weight.shape[0]
    f32, bf16 = jnp.float32, jnp.bfloat16
    shape = jax.ShapeDtypeStruct
    here = PLANE * PLANES

    def hop(a, target):
        pairs = [(i, target(i // PLANE) * PLANE + i % PLANE) for i in range(here) if target(i // PLANE) is not None]
        return lax.ppermute(a, ("seq", "dp"), pairs)

    def plane_hop(a, move):
        return lax.ppermute(a, ("seq", "dp"), [(i, i ^ move) for i in range(here)])

    def each(a):
        return [hop(a, lambda p: p ^ j) for j in range(1, PLANES)]

    wide = 3 * GROUP
    w_own, w_sent = call(
        pack_kernel, (shape((rows, wide), bf16),) * 2, [hbm()], [pltpu.SemaphoreType.DMA((6,))], 0
    )(weight)

    def between(p):
        return 3 - p if p in (1, 2) else None

    def outward(p):
        return {1: 0, 2: 3}.get(p)

    near = plane_hop(events, 2)
    across = plane_hop(events, 1)
    w_near = plane_hop(w_sent, 2)
    corner = plane_hop(call(gate_kernel, shape((tokens, width), bf16), [vmem()] + [anywhere()] * 1, [], 0)(events, w_near), 3)
    next_own = hop(w_own, between)
    then_own = hop(next_own, outward)
    one_near = hop(call(gate_kernel, shape((rows, wide), bf16), [vmem()] + [anywhere()] * 1, [], 0)(w_near, then_own), lambda p: p ^ 1)
    far_near = hop(one_near, between)
    last_near = hop(call(gate_kernel, shape((rows, wide), bf16), [vmem()] + [anywhere()] * 1, [], 0)(far_near, corner), outward)
    one_own = hop(w_own, lambda p: p ^ 1)
    far_own = hop(one_own, between)
    last_own = hop(far_own, outward)
    next_near = hop(call(gate_kernel, shape((rows, wide), bf16), [vmem()] + [anywhere()] * 1, [], 0)(w_near, far_own), between)
    then_near = hop(next_near, outward)

    normed, sums, raw_short = call(
        norm_kernel,
        (shape((2 * tokens, width), bf16), shape((1, GROUP), f32), shape((tokens, width), bf16)),
        [smem()] + [anywhere()] * 4 + [vmem()],
        [pltpu.VMEM((2, tokens, width), bf16), pltpu.SemaphoreType.DMA((3,))],
        2 * 3 * tokens * width,
    )(lengths, events, near, across, corner, norm_gain)
    feats, message, weights = call(
        project_kernel,
        (shape((2 * tokens, wide), bf16), shape((MESSAGE, HEAD_DIM), bf16), shape((width, wide), bf16)),
        [vmem()] * 13,
        [],
        2 * 2 * tokens * width * wide,
    )(normed, w_own, w_near, one_own, one_near, next_own, next_near, then_own, then_near, far_own, far_near, last_own, last_near)
    short = call(
        short_kernel, shape((1, GROUP), f32), [vmem()] * 3, [], 2 * tokens * width * wide
    )(raw_short, weights, norm_gain)
    part = call(
        pool_kernel,
        shape((2 * here, 4, GROUP), f32),
        [smem()] + [vmem()] * 7,
        [],
        2 * 9 * tokens * tokens * GROUP,
    )(lengths, *each(message), feats, sums, short, pool_gain)
    parts = lax.all_to_all(part, ("seq", "dp", "domain"), 0, 0, tiled=True)
    vec, loss = call(
        loss_kernel,
        (shape((1, 1, width // 8), bf16), shape((1, 1), f32)),
        [smem(), vmem()],
        [pltpu.VMEM((2, width), f32), pltpu.VMEM((2, width), f32)],
        2**14,
    )(positives, parts)
    return vec, loss


def solution(mesh):
    placed = (
        P("domain", "dp", "seq", None),
        P("domain", "seq", None),
        P("domain", None),
        P("domain", None),
        P("domain", "dp"),
        P(),
    )
    small = mesh.shape["seq"] == 2 * PLANES and mesh.shape["dp"] == 2
    return jax.shard_map(
        towers if small else shards,
        mesh=mesh,
        in_specs=placed,
        out_specs=(P("domain", "dp", "seq"), P("domain", "dp")),
        check_vma=False,
    )
```

```python
import functools

import jax
import jax.numpy as jnp
from jax import lax
from jax.experimental import pallas as pl
from jax.experimental.pallas import tpu as pltpu
from jax.sharding import PartitionSpec as P

HEADS = 8
HEAD_DIM = 128


logit_scale = 20.0
epsilon = 1e-06
highest = lax.Precision.HIGHEST


def carried_in(part, axis, combine, identity):
    place = lax.axis_index(axis)
    gathered = jax.tree.map(lambda a: lax.all_gather(a, axis), part)
    state = jax.tree.map(lambda a, e: jnp.zeros_like(a) + jnp.asarray(e, a.dtype), part, identity)

    def one(hop, state):
        return combine(
            state, jax.tree.map(lambda a: lax.dynamic_index_in_dim(a, hop, 0, False), gathered)
        )

    return lax.fori_loop(0, place, one, state)


def partner_2(block, axis, stride):
    count = lax.axis_size(axis)
    route = []
    for low in range(count):
        high = low | 1 << stride
        if high != low and high < count:
            route += [(low, high), (high, low)]
    return lax.ppermute(block, axis, route)


def feature_map(values):
    return jax.nn.elu(values) + 1.0


def add_pair(earlier, later):
    return (earlier[0] + later[0], earlier[1] + later[1])


def shards(history, qkv_weight, norm_gain, pool_gain, lengths, positives):
    seq_count = lax.axis_size("seq")
    seq_place = lax.axis_index("seq")
    group_place = lax.axis_index("dp")
    domain_place = lax.axis_index("domain")
    events = history[0]
    users_dev, tokens_dev, width = events.shape
    row_count = users_dev * tokens_dev
    wide = events.astype(jnp.float32)
    normed = (
        wide * lax.rsqrt(jnp.mean(wide * wide, -1, keepdims=True) + epsilon) * norm_gain[0]
    ).astype(jnp.bfloat16)
    normed = normed.reshape(row_count, width)
    rows_here = qkv_weight[0]
    projected = jnp.dot(
        normed,
        lax.all_gather(rows_here, "seq", axis=0, tiled=True),
        preferred_element_type=jnp.float32,
    )
    query_raw = projected[:, :width]
    key_raw = projected[:, width : 2 * width]
    value_raw = projected[:, 2 * width :]
    positions = seq_place * tokens_dev + jnp.arange(tokens_dev)
    valid = positions[None, :] < lengths[0][:, None]
    shape_heads = (users_dev, tokens_dev, HEADS, HEAD_DIM)
    queries = feature_map(query_raw).astype(jnp.bfloat16).reshape(shape_heads)
    key_feats = (
        jnp.where(valid.reshape(row_count)[:, None], feature_map(key_raw), 0.0)
        .astype(jnp.bfloat16)
        .reshape(shape_heads)
    )
    val_feats = value_raw.astype(jnp.bfloat16).reshape(shape_heads)
    local_state = jnp.einsum(
        "uthc,uthd->uhcd", key_feats, val_feats, preferred_element_type=jnp.float32
    )
    local_total = jnp.sum(key_feats.astype(jnp.float32), axis=1)
    state_before, total_before = carried_in(
        (local_state, local_total),
        "seq",
        add_pair,
        (jnp.zeros_like(local_state), jnp.zeros_like(local_total)),
    )
    causal = jnp.arange(tokens_dev)[:, None] >= jnp.arange(tokens_dev)[None, :]
    scores = jnp.einsum("uthc,ushc->uhts", queries, key_feats, preferred_element_type=jnp.float32)
    scores = jnp.where(causal, scores, 0.0)
    denominator = jnp.sum(scores, axis=-1) + jnp.einsum(
        "uthc,uhc->uht", queries.astype(jnp.float32), total_before, precision=highest
    )
    numerator = jnp.einsum(
        "uhts,ushc->uthc",
        scores.astype(jnp.bfloat16),
        val_feats,
        preferred_element_type=jnp.float32,
    )
    numerator = numerator + jnp.einsum(
        "uthc,uhcd->uthd",
        queries,
        state_before.astype(jnp.bfloat16),
        preferred_element_type=jnp.float32,
    )
    attended = numerator / jnp.transpose(denominator, (0, 2, 1))[..., None]
    attended = attended.reshape(users_dev, tokens_dev, width)
    partial_value = jnp.sum(jnp.where(valid[..., None], wide + attended, 0.0), axis=1)
    piece_width = width // seq_count
    gain_row = pool_gain[0]
    pooled = lax.psum(partial_value, "seq")
    factor = lax.rsqrt(jnp.mean(pooled * pooled, -1, keepdims=True) + epsilon)
    full_vec = (pooled * factor * gain_row).astype(jnp.bfloat16)
    out_vec = lax.dynamic_slice_in_dim(full_vec, seq_place * piece_width, piece_width, 1)
    group = lax.all_gather(full_vec, "dp", axis=0, tiled=True)
    other = partner_2(group, "domain", 0)
    logits = jnp.einsum("uc,vc->uv", full_vec, other, preferred_element_type=jnp.float32) * (
        logit_scale / width
    )
    users_all = other.shape[0]
    own_index = group_place * users_dev + jnp.arange(users_dev)
    targets = lax.dynamic_slice_in_dim(positives, group_place * users_dev, users_dev)
    forward_pair = targets[:, None] == jnp.arange(users_all)[None, :]
    backward_pair = positives[None, :] == own_index[:, None]
    partner = jnp.where(domain_place == 0, forward_pair, backward_pair)
    loss = jnp.log(jnp.sum(jnp.exp(logits), axis=-1)) - jnp.sum(
        jnp.where(partner, logits, 0.0), axis=-1
    )
    return (out_vec[None], loss[None])


PLANE = 4
PLANES = 4
GROUP = 256
DOT_T = (((0,), (0,)), ((), ()))
MESSAGE = GROUP + 16


def places():
    seq_place = lax.axis_index("seq")
    return lax.div(seq_place, 2), lax.rem(seq_place, 2), lax.axis_index("dp")


def head_sums(a):
    return [
        jnp.sum(a[:, h * HEAD_DIM : (h + 1) * HEAD_DIM], axis=1, keepdims=True)
        for h in range(GROUP // HEAD_DIM)
    ]


def by_head(columns):
    rows = columns[0].shape[0]
    return jnp.concatenate([jnp.broadcast_to(c, (rows, HEAD_DIM)) for c in columns], axis=1)


def split_two(a):
    high = a.astype(jnp.bfloat16)
    return high, (a - high.astype(jnp.float32)).astype(jnp.bfloat16)


def pack_kernel(weight, own, sent, sems):
    _, x, u = places()
    width = weight.shape[1] // 3
    copies = []
    for move, out in ((2, sent), (0, own)):
        group = jnp.bitwise_xor(2 * x + u, move)
        for part in range(3):
            start = pl.multiple_of(part * width + group * GROUP, GROUP)
            copies.append(
                pltpu.make_async_copy(
                    weight.at[:, pl.ds(start, GROUP)], out.at[:, pl.ds(part * GROUP, GROUP)], sems.at[len(copies)]
                )
            )
    for copy in copies:
        copy.start()
    for copy in copies:
        copy.wait()


def gate_kernel(values, *rest):
    rest[-1][...] = values[...]


def normalise(values, gain):
    wide = values.astype(jnp.float32)
    scale = lax.rsqrt(jnp.mean(wide * wide, axis=1, keepdims=True) + epsilon)
    return (wide * scale * gain).astype(jnp.bfloat16)


def features(normed, weights):
    out = jnp.dot(normed, weights, preferred_element_type=jnp.float32)
    raw = out[:, : 2 * GROUP]
    low = jnp.where(raw > 0.0, raw + 1.0, jnp.exp(jnp.minimum(raw, 0.0))).astype(jnp.bfloat16)
    return low[:, :GROUP], low[:, GROUP:], out[:, 2 * GROUP :].astype(jnp.bfloat16)


def norm_kernel(lengths, own, near, across, corner, gain, normed, sums, short, raw, sems):
    tokens = own.shape[0]
    _, x, u = places()
    long_u = jnp.where(lengths[0, 0] > tokens, u, 1 - u)
    for slot in range(3):
        from_x = 1 if slot == 1 else 0
        from_u = 1 - long_u if slot == 2 else long_u
        pick = jnp.bitwise_xor(x, from_x) + 2 * jnp.bitwise_xor(u, from_u)
        dest = short if slot == 2 else raw.at[slot]
        for j, ref in enumerate((own, near, across, corner)):

            @pl.when(pick == j)
            def _():
                pltpu.make_async_copy(ref, dest, sems.at[slot]).start()

    columns = pl.ds(pl.multiple_of((2 * x + u) * GROUP, GROUP), GROUP)
    total = jnp.zeros((1, GROUP), jnp.float32)
    for slot in range(2):
        pltpu.make_async_copy(own, raw.at[slot], sems.at[slot]).wait()
        normed[pl.ds(slot * tokens, tokens), :] = normalise(raw[slot], gain[...])
        total = total + jnp.sum(raw[slot, :, columns].astype(jnp.float32), axis=0, keepdims=True)
    sums[...] = total
    pltpu.make_async_copy(own, short, sems.at[2]).wait()


def project_kernel(normed, *refs):
    own, near, one_own, one_near, next_own, next_near, then_own, then_near, far_own, far_near, last_own, last_near = refs[:12]
    feats, message, weights = refs[12:]
    tokens = normed.shape[0]
    rows = own.shape[0]
    z, x, _ = places()

    def put(plane, here, there):
        for place, ref in ((x, here), (1 - x, there)):
            weights[pl.ds(pl.multiple_of((2 * plane + place) * rows, rows), rows), :] = ref[...]

    put(z, own, near)
    put(jnp.bitwise_xor(z, 1), one_own, one_near)
    inner = jnp.logical_or(z == 1, z == 2)

    @pl.when(inner)
    def _():
        put(3 - z, next_own, next_near)
        put(jnp.bitwise_xor(z, 2), far_own, far_near)

    @pl.when(jnp.logical_not(inner))
    def _():
        put(jnp.bitwise_xor(z, 2), then_own, then_near)
        put(3 - z, last_own, last_near)

    half = tokens // 2
    total = jnp.zeros((1, GROUP), jnp.float32)
    for part in range(2):
        at = pl.ds(part * half, half)
        query, key, value = features(normed[at, :], weights[...])
        feats[at, :GROUP] = query
        feats[at, GROUP : 2 * GROUP] = key
        feats[at, 2 * GROUP :] = value
        total = total + jnp.sum(key.astype(jnp.float32), axis=0, keepdims=True)
    high, low = split_two(total)
    for h in range(GROUP // HEAD_DIM):
        at = h * HEAD_DIM
        key = feats[:, GROUP + at : GROUP + at + HEAD_DIM]
        value = feats[:, 2 * GROUP + at : 2 * GROUP + at + HEAD_DIM]
        state = lax.dot_general(key, value, DOT_T, preferred_element_type=jnp.float32)
        message[at : at + HEAD_DIM, :] = state.astype(jnp.bfloat16)
    total_rows = [high[:, :HEAD_DIM], high[:, HEAD_DIM:], low[:, :HEAD_DIM], low[:, HEAD_DIM:]]
    message[GROUP:, :] = jnp.concatenate(total_rows * 4, axis=0)


def triangle(tokens, upper):
    row = lax.broadcasted_iota(jnp.int32, (tokens, tokens), 0)
    col = lax.broadcasted_iota(jnp.int32, (tokens, tokens), 1)
    return (row <= col if upper else row >= col).astype(jnp.bfloat16)


def shares(query, key, carry):
    prefix = jnp.dot(triangle(key.shape[0], False), key, preferred_element_type=jnp.float32) + carry
    wide = query.astype(jnp.float32)
    return wide / by_head(head_sums(wide * prefix)), prefix[key.shape[0] - 1 :, :]


def suffix(share):
    upper = triangle(share.shape[0], True)
    high, low = split_two(share)
    return jnp.dot(upper, high, preferred_element_type=jnp.float32) + jnp.dot(
        upper, low, preferred_element_type=jnp.float32
    )


def weighted(key, value, after):
    weight = by_head(head_sums(key.astype(jnp.float32) * after))
    return jnp.sum(weight * value.astype(jnp.float32), axis=0, keepdims=True)


def short_kernel(raw, weights, gain, out):
    z, x, u = places()
    out[...] = jnp.zeros(out.shape, jnp.float32)

    @pl.when(z == 0)
    def _():
        query, key, value = features(normalise(raw[...], gain[...]), weights[...])
        share, _ = shares(query, key, jnp.zeros((1, GROUP), jnp.float32))
        columns = pl.ds(pl.multiple_of((2 * x + u) * GROUP, GROUP), GROUP)
        own = jnp.sum(raw[:, columns].astype(jnp.float32), axis=0, keepdims=True)
        out[...] = own + weighted(key, value, suffix(share))


def pool_kernel(lengths, state_1, state_2, state_3, feats, sums, short, gain, part):
    tokens = feats.shape[0] // 2
    z, x, u = places()
    long_u = jnp.where(lengths[0, 0] > tokens, u, 1 - u)
    states = [(jnp.bitwise_xor(z, j) < z, ref) for j, ref in enumerate((state_1, state_2, state_3), 1)]
    before = jnp.zeros((1, GROUP), jnp.float32)
    for earlier, ref in states:
        rows = ref[GROUP : GROUP + 16, :].astype(jnp.float32)
        total = jnp.concatenate([rows[0:1] + rows[2:3], rows[1:2] + rows[3:4]], axis=1)
        before = before + jnp.where(earlier, total, 0.0)

    def block(slot):
        at = pl.ds(slot * tokens, tokens)
        return feats[at, :GROUP], feats[at, GROUP : 2 * GROUP], feats[at, 2 * GROUP :]

    query_one, key_one, value_one = block(0)
    query_two, key_two, value_two = block(1)
    share_one, carry = shares(query_one, key_one, before)
    share_two, _ = shares(query_two, key_two, carry)
    after_two = suffix(share_two)
    after_one = suffix(share_one) + after_two[0:1, :]
    long_row = weighted(key_one, value_one, after_one) + weighted(key_two, value_two, after_two) + sums[...]
    weight = after_one[0:1, :]
    for earlier, ref in states:
        high, low = split_two(jnp.where(earlier, weight, 0.0))
        products = []
        for h in range(GROUP // HEAD_DIM):
            at = h * HEAD_DIM
            both = jnp.concatenate([high[:, at : at + HEAD_DIM]] * 8 + [low[:, at : at + HEAD_DIM]] * 8, axis=0)
            out = jnp.dot(both, ref[at : at + HEAD_DIM, :], preferred_element_type=jnp.float32)
            products.append(out[0:1] + out[8:9])
        long_row = long_row + jnp.concatenate(products, axis=1)

    short_row = short[...]
    first = jnp.where(long_u == 0, long_row, short_row)
    second = jnp.where(long_u == 0, short_row, long_row)
    own_gain = gain[:, pl.ds(pl.multiple_of((2 * x + u) * GROUP, GROUP), GROUP)]
    rows = jnp.concatenate([first, second, own_gain, own_gain], axis=0)
    part[...] = jnp.broadcast_to(rows[None], part.shape)


def loss_kernel(positives, parts, vec, loss, mine, theirs):
    z, x, u = places()
    domain = lax.axis_index("domain")
    width = mine.shape[1]
    piece = vec.shape[2]

    def collect(place, dest):
        total = jnp.zeros((2, 1), jnp.float32)
        for group in range(PLANE):
            blocks = [parts[2 * (PLANE * plane + group) + place] for plane in range(PLANES)]
            values = (blocks[0][:2] + blocks[1][:2]) + (blocks[2][:2] + blocks[3][:2])
            total = total + jnp.sum(values * values, axis=1, keepdims=True)
            dest[:, group * GROUP : (group + 1) * GROUP] = values * blocks[0][2:3]
        factor = lax.rsqrt(total / width + epsilon)
        return (dest[...] * factor).astype(jnp.bfloat16).astype(jnp.float32)

    own = collect(domain, mine)
    other = collect(1 - domain, theirs)
    mine[...] = own
    start = pl.multiple_of((2 * z + x) * piece, piece)
    out = mine[:, pl.ds(start, piece)]
    vec[0] = jnp.where(u == 0, out[0:1], out[1:2]).astype(jnp.bfloat16)
    this = jnp.where(u == 0, own[0:1], own[1:2])
    logits = jnp.sum(this * other, axis=1, keepdims=True) * (logit_scale / width)
    top = jnp.max(logits, axis=0, keepdims=True)
    spread = jnp.log(jnp.sum(jnp.exp(logits - top), axis=0, keepdims=True)) + top
    forward = jnp.where(u == 0, positives[0], positives[1])
    backward = jnp.where(positives[0] == u, 0, 1)
    partner = jnp.where(domain == 0, forward, backward)
    rows = lax.broadcasted_iota(jnp.int32, (2, 1), 0)
    loss[...] = spread - jnp.sum(jnp.where(rows == partner, logits, 0.0), axis=0, keepdims=True)


def vmem():
    return pl.BlockSpec(memory_space=pltpu.VMEM)


def anywhere():
    return pl.BlockSpec(memory_space=pl.ANY)


def hbm():
    return pl.BlockSpec(memory_space=pltpu.HBM)


def smem():
    return pl.BlockSpec(memory_space=pltpu.SMEM)


def call(kernel, outs, in_specs, scratch, flops):
    return pl.pallas_call(
        kernel,
        out_shape=outs,
        in_specs=in_specs,
        out_specs=jax.tree.map(lambda _: vmem(), outs),
        scratch_shapes=scratch,
        compiler_params=pltpu.CompilerParams(vmem_limit_bytes=40 * 1024 * 1024),
        cost_estimate=pl.CostEstimate(flops=flops, bytes_accessed=2**21, transcendentals=0),
    )


def towers(history, qkv_weight, norm_gain, pool_gain, lengths, positives):
    events = history[0, 0]
    tokens, width = events.shape
    weight = qkv_weight[0]
    rows = weight.shape[0]
    f32, bf16 = jnp.float32, jnp.bfloat16
    shape = jax.ShapeDtypeStruct
    here = PLANE * PLANES

    def hop(a, target):
        pairs = [(i, target(i // PLANE) * PLANE + i % PLANE) for i in range(here) if target(i // PLANE) is not None]
        return lax.ppermute(a, ("seq", "dp"), pairs)

    def plane_hop(a, move):
        return lax.ppermute(a, ("seq", "dp"), [(i, i ^ move) for i in range(here)])

    def each(a):
        return [hop(a, lambda p: p ^ j) for j in range(1, PLANES)]

    wide = 3 * GROUP
    w_own, w_sent = call(
        pack_kernel, (shape((rows, wide), bf16),) * 2, [hbm()], [pltpu.SemaphoreType.DMA((6,))], 0
    )(weight)

    def between(p):
        return 3 - p if p in (1, 2) else p

    def outward(p):
        return p ^ 1

    near = plane_hop(events, 2)
    across = plane_hop(events, 1)
    w_near = plane_hop(w_sent, 2)
    corner = plane_hop(call(gate_kernel, shape((tokens, width), bf16), [vmem()] + [anywhere()] * 1, [], 0)(events, w_near), 3)
    next_own = hop(w_own, between)
    then_own = hop(next_own, outward)
    one_near = hop(call(gate_kernel, shape((rows, wide), bf16), [vmem()] + [anywhere()] * 1, [], 0)(w_near, then_own), lambda p: p ^ 1)
    far_near = hop(one_near, between)
    last_near = hop(call(gate_kernel, shape((rows, wide), bf16), [vmem()] + [anywhere()] * 1, [], 0)(far_near, corner), outward)
    one_own = hop(w_own, lambda p: p ^ 1)
    far_own = hop(one_own, between)
    last_own = hop(far_own, outward)
    next_near = hop(call(gate_kernel, shape((rows, wide), bf16), [vmem()] + [anywhere()] * 1, [], 0)(w_near, far_own), between)
    then_near = hop(next_near, outward)

    normed, sums, raw_short = call(
        norm_kernel,
        (shape((2 * tokens, width), bf16), shape((1, GROUP), f32), shape((tokens, width), bf16)),
        [smem()] + [anywhere()] * 4 + [vmem()],
        [pltpu.VMEM((2, tokens, width), bf16), pltpu.SemaphoreType.DMA((3,))],
        2 * 3 * tokens * width,
    )(lengths, events, near, across, corner, norm_gain)
    feats, message, weights = call(
        project_kernel,
        (shape((2 * tokens, wide), bf16), shape((MESSAGE, HEAD_DIM), bf16), shape((width, wide), bf16)),
        [vmem()] * 13,
        [],
        2 * 2 * tokens * width * wide,
    )(normed, w_own, w_near, one_own, one_near, next_own, next_near, then_own, then_near, far_own, far_near, last_own, last_near)
    short = call(
        short_kernel, shape((1, GROUP), f32), [vmem()] * 3, [], 2 * tokens * width * wide
    )(raw_short, weights, norm_gain)
    part = call(
        pool_kernel,
        shape((2 * here, 4, GROUP), f32),
        [smem()] + [vmem()] * 7,
        [],
        2 * 9 * tokens * tokens * GROUP,
    )(lengths, *each(message), feats, sums, short, pool_gain)
    parts = lax.all_to_all(part, ("seq", "dp", "domain"), 0, 0, tiled=True)
    vec, loss = call(
        loss_kernel,
        (shape((1, 1, width // 8), bf16), shape((1, 1), f32)),
        [smem(), vmem()],
        [pltpu.VMEM((2, width), f32), pltpu.VMEM((2, width), f32)],
        2**14,
    )(positives, parts)
    return vec, loss


def solution(mesh):
    placed = (
        P("domain", "dp", "seq", None),
        P("domain", "seq", None),
        P("domain", None),
        P("domain", None),
        P("domain", "dp"),
        P(),
    )
    small = mesh.shape["seq"] == 2 * PLANES and mesh.shape["dp"] == 2
    return jax.shard_map(
        towers if small else shards,
        mesh=mesh,
        in_specs=placed,
        out_specs=(P("domain", "dp", "seq"), P("domain", "dp")),
        check_vma=False,
    )
```

```python
import functools

import jax
import jax.numpy as jnp
from jax import lax
from jax.experimental import pallas as pl
from jax.experimental.pallas import tpu as pltpu
from jax.sharding import PartitionSpec as P

HEADS = 8
HEAD_DIM = 128


logit_scale = 20.0
epsilon = 1e-06
highest = lax.Precision.HIGHEST


def carried_in(part, axis, combine, identity):
    place = lax.axis_index(axis)
    gathered = jax.tree.map(lambda a: lax.all_gather(a, axis), part)
    state = jax.tree.map(lambda a, e: jnp.zeros_like(a) + jnp.asarray(e, a.dtype), part, identity)

    def one(hop, state):
        return combine(
            state, jax.tree.map(lambda a: lax.dynamic_index_in_dim(a, hop, 0, False), gathered)
        )

    return lax.fori_loop(0, place, one, state)


def partner_2(block, axis, stride):
    count = lax.axis_size(axis)
    route = []
    for low in range(count):
        high = low | 1 << stride
        if high != low and high < count:
            route += [(low, high), (high, low)]
    return lax.ppermute(block, axis, route)


def feature_map(values):
    return jax.nn.elu(values) + 1.0


def add_pair(earlier, later):
    return (earlier[0] + later[0], earlier[1] + later[1])


def shards(history, qkv_weight, norm_gain, pool_gain, lengths, positives):
    seq_count = lax.axis_size("seq")
    seq_place = lax.axis_index("seq")
    group_place = lax.axis_index("dp")
    domain_place = lax.axis_index("domain")
    events = history[0]
    users_dev, tokens_dev, width = events.shape
    row_count = users_dev * tokens_dev
    wide = events.astype(jnp.float32)
    normed = (
        wide * lax.rsqrt(jnp.mean(wide * wide, -1, keepdims=True) + epsilon) * norm_gain[0]
    ).astype(jnp.bfloat16)
    normed = normed.reshape(row_count, width)
    rows_here = qkv_weight[0]
    projected = jnp.dot(
        normed,
        lax.all_gather(rows_here, "seq", axis=0, tiled=True),
        preferred_element_type=jnp.float32,
    )
    query_raw = projected[:, :width]
    key_raw = projected[:, width : 2 * width]
    value_raw = projected[:, 2 * width :]
    positions = seq_place * tokens_dev + jnp.arange(tokens_dev)
    valid = positions[None, :] < lengths[0][:, None]
    shape_heads = (users_dev, tokens_dev, HEADS, HEAD_DIM)
    queries = feature_map(query_raw).astype(jnp.bfloat16).reshape(shape_heads)
    key_feats = (
        jnp.where(valid.reshape(row_count)[:, None], feature_map(key_raw), 0.0)
        .astype(jnp.bfloat16)
        .reshape(shape_heads)
    )
    val_feats = value_raw.astype(jnp.bfloat16).reshape(shape_heads)
    local_state = jnp.einsum(
        "uthc,uthd->uhcd", key_feats, val_feats, preferred_element_type=jnp.float32
    )
    local_total = jnp.sum(key_feats.astype(jnp.float32), axis=1)
    state_before, total_before = carried_in(
        (local_state, local_total),
        "seq",
        add_pair,
        (jnp.zeros_like(local_state), jnp.zeros_like(local_total)),
    )
    causal = jnp.arange(tokens_dev)[:, None] >= jnp.arange(tokens_dev)[None, :]
    scores = jnp.einsum("uthc,ushc->uhts", queries, key_feats, preferred_element_type=jnp.float32)
    scores = jnp.where(causal, scores, 0.0)
    denominator = jnp.sum(scores, axis=-1) + jnp.einsum(
        "uthc,uhc->uht", queries.astype(jnp.float32), total_before, precision=highest
    )
    numerator = jnp.einsum(
        "uhts,ushc->uthc",
        scores.astype(jnp.bfloat16),
        val_feats,
        preferred_element_type=jnp.float32,
    )
    numerator = numerator + jnp.einsum(
        "uthc,uhcd->uthd",
        queries,
        state_before.astype(jnp.bfloat16),
        preferred_element_type=jnp.float32,
    )
    attended = numerator / jnp.transpose(denominator, (0, 2, 1))[..., None]
    attended = attended.reshape(users_dev, tokens_dev, width)
    partial_value = jnp.sum(jnp.where(valid[..., None], wide + attended, 0.0), axis=1)
    piece_width = width // seq_count
    gain_row = pool_gain[0]
    pooled = lax.psum(partial_value, "seq")
    factor = lax.rsqrt(jnp.mean(pooled * pooled, -1, keepdims=True) + epsilon)
    full_vec = (pooled * factor * gain_row).astype(jnp.bfloat16)
    out_vec = lax.dynamic_slice_in_dim(full_vec, seq_place * piece_width, piece_width, 1)
    group = lax.all_gather(full_vec, "dp", axis=0, tiled=True)
    other = partner_2(group, "domain", 0)
    logits = jnp.einsum("uc,vc->uv", full_vec, other, preferred_element_type=jnp.float32) * (
        logit_scale / width
    )
    users_all = other.shape[0]
    own_index = group_place * users_dev + jnp.arange(users_dev)
    targets = lax.dynamic_slice_in_dim(positives, group_place * users_dev, users_dev)
    forward_pair = targets[:, None] == jnp.arange(users_all)[None, :]
    backward_pair = positives[None, :] == own_index[:, None]
    partner = jnp.where(domain_place == 0, forward_pair, backward_pair)
    loss = jnp.log(jnp.sum(jnp.exp(logits), axis=-1)) - jnp.sum(
        jnp.where(partner, logits, 0.0), axis=-1
    )
    return (out_vec[None], loss[None])


PLANE = 4
PLANES = 4
GROUP = 256
DOT_T = (((0,), (0,)), ((), ()))
MESSAGE = GROUP + 16


def places():
    seq_place = lax.axis_index("seq")
    return lax.div(seq_place, 2), lax.rem(seq_place, 2), lax.axis_index("dp")


def head_sums(a):
    return [
        jnp.sum(a[:, h * HEAD_DIM : (h + 1) * HEAD_DIM], axis=1, keepdims=True)
        for h in range(GROUP // HEAD_DIM)
    ]


def by_head(columns):
    rows = columns[0].shape[0]
    return jnp.concatenate([jnp.broadcast_to(c, (rows, HEAD_DIM)) for c in columns], axis=1)


def split_two(a):
    high = a.astype(jnp.bfloat16)
    return high, (a - high.astype(jnp.float32)).astype(jnp.bfloat16)


def pack_kernel(weight, own, sent, sems):
    _, x, u = places()
    width = weight.shape[1] // 3
    copies = []
    for move, out in ((2, sent), (0, own)):
        group = jnp.bitwise_xor(2 * x + u, move)
        for part in range(3):
            start = pl.multiple_of(part * width + group * GROUP, GROUP)
            copies.append(
                pltpu.make_async_copy(
                    weight.at[:, pl.ds(start, GROUP)], out.at[:, pl.ds(part * GROUP, GROUP)], sems.at[len(copies)]
                )
            )
    for copy in copies:
        copy.start()
    for copy in copies:
        copy.wait()


def gate_kernel(values, *rest):
    rest[-1][...] = values[...]


def normalise(values, gain):
    wide = values.astype(jnp.float32)
    scale = lax.rsqrt(jnp.mean(wide * wide, axis=1, keepdims=True) + epsilon)
    return (wide * scale * gain).astype(jnp.bfloat16)


def features(out):
    raw = out[:, : 2 * GROUP]
    low = jnp.where(raw > 0.0, raw + 1.0, jnp.exp(jnp.minimum(raw, 0.0))).astype(jnp.bfloat16)
    return low[:, :GROUP], low[:, GROUP:], out[:, 2 * GROUP :].astype(jnp.bfloat16)


def norm_kernel(lengths, own, near, across, corner, gain, normed, sums, short, raw, sems):
    tokens = own.shape[0]
    _, x, u = places()
    long_u = jnp.where(lengths[0, 0] > tokens, u, 1 - u)
    for slot in range(3):
        from_x = 1 if slot == 1 else 0
        from_u = 1 - long_u if slot == 2 else long_u
        pick = jnp.bitwise_xor(x, from_x) + 2 * jnp.bitwise_xor(u, from_u)
        dest = short if slot == 2 else raw.at[slot]
        for j, ref in enumerate((own, near, across, corner)):

            @pl.when(pick == j)
            def _():
                pltpu.make_async_copy(ref, dest, sems.at[slot]).start()

    columns = pl.ds(pl.multiple_of((2 * x + u) * GROUP, GROUP), GROUP)
    total = jnp.zeros((1, GROUP), jnp.float32)
    for slot in range(2):
        pltpu.make_async_copy(own, raw.at[slot], sems.at[slot]).wait()
        normed[pl.ds(slot * tokens, tokens), :] = normalise(raw[slot], gain[...])
        total = total + jnp.sum(raw[slot, :, columns].astype(jnp.float32), axis=0, keepdims=True)
    sums[...] = total
    pltpu.make_async_copy(own, short, sems.at[2]).wait()


def place_rows(dest, start, x, here, there):
    rows = here.shape[0]
    for place, values in ((x, here), (1 - x, there)):
        dest[pl.ds(pl.multiple_of(start + place * rows, rows), rows), :] = values


def partial_kernel(normed, own, near, one_own, one_near, two_own, two_near, partial, weights):
    z, x, _ = places()
    parts = ((own, near), (one_own, one_near), (two_own, two_near), None)
    starts = [pl.multiple_of(jnp.bitwise_xor(z, j) * GROUP, GROUP) for j in range(PLANES)]
    for start, refs in zip(starts, parts):
        if refs is None:
            weights[pl.ds(start, GROUP), :] = jnp.zeros((GROUP, weights.shape[1]), weights.dtype)
        else:
            place_rows(weights, start, x, refs[0][...], refs[1][...])
    total = None
    for start in starts[:3]:
        rows = pl.ds(start, GROUP)
        out = jnp.dot(normed[:, rows], weights[rows, :], preferred_element_type=jnp.float32)
        total = out if total is None else total + out
    partial[...] = total


def project_kernel(normed, partial, next_both, far_own, far_near, feats, message, last):
    tokens = normed.shape[0]
    rows = far_own.shape[0]
    z, x, _ = places()
    inner = jnp.logical_or(z == 1, z == 2)

    @pl.when(inner)
    def _():
        place_rows(last, 0, x, next_both[:rows, :], next_both[rows:, :])

    @pl.when(jnp.logical_not(inner))
    def _():
        place_rows(last, 0, x, far_own[...], far_near[...])

    columns = pl.ds(pl.multiple_of((3 - z) * GROUP, GROUP), GROUP)
    half = tokens // 2
    total = jnp.zeros((1, GROUP), jnp.float32)
    for part in range(2):
        at = pl.ds(part * half, half)
        out = partial[at, :] + jnp.dot(normed[at, columns], last[...], preferred_element_type=jnp.float32)
        query, key, value = features(out)
        feats[at, :GROUP] = query
        feats[at, GROUP : 2 * GROUP] = key
        feats[at, 2 * GROUP :] = value
        total = total + jnp.sum(key.astype(jnp.float32), axis=0, keepdims=True)
    high, low = split_two(total)
    for h in range(GROUP // HEAD_DIM):
        at = h * HEAD_DIM
        key = feats[:, GROUP + at : GROUP + at + HEAD_DIM]
        value = feats[:, 2 * GROUP + at : 2 * GROUP + at + HEAD_DIM]
        state = lax.dot_general(key, value, DOT_T, preferred_element_type=jnp.float32)
        message[at : at + HEAD_DIM, :] = state.astype(jnp.bfloat16)
    total_rows = [high[:, :HEAD_DIM], high[:, HEAD_DIM:], low[:, :HEAD_DIM], low[:, HEAD_DIM:]]
    message[GROUP:, :] = jnp.concatenate(total_rows * 4, axis=0)


def triangle(tokens, upper):
    row = lax.broadcasted_iota(jnp.int32, (tokens, tokens), 0)
    col = lax.broadcasted_iota(jnp.int32, (tokens, tokens), 1)
    return (row <= col if upper else row >= col).astype(jnp.bfloat16)


def shares(query, key, carry):
    prefix = jnp.dot(triangle(key.shape[0], False), key, preferred_element_type=jnp.float32) + carry
    wide = query.astype(jnp.float32)
    return wide / by_head(head_sums(wide * prefix)), prefix[key.shape[0] - 1 :, :]


def suffix(share):
    upper = triangle(share.shape[0], True)
    high, low = split_two(share)
    return jnp.dot(upper, high, preferred_element_type=jnp.float32) + jnp.dot(
        upper, low, preferred_element_type=jnp.float32
    )


def weighted(key, value, after):
    weight = by_head(head_sums(key.astype(jnp.float32) * after))
    return jnp.sum(weight * value.astype(jnp.float32), axis=0, keepdims=True)


def short_kernel(raw, weights, last, gain, out):
    z, x, u = places()
    out[...] = jnp.zeros(out.shape, jnp.float32)

    @pl.when(z == 0)
    def _():
        low = normalise(raw[...], gain[...])
        wide = jnp.dot(low, weights[...], preferred_element_type=jnp.float32)
        wide = wide + jnp.dot(low[:, 3 * GROUP :], last[...], preferred_element_type=jnp.float32)
        query, key, value = features(wide)
        share, _ = shares(query, key, jnp.zeros((1, GROUP), jnp.float32))
        columns = pl.ds(pl.multiple_of((2 * x + u) * GROUP, GROUP), GROUP)
        own = jnp.sum(raw[:, columns].astype(jnp.float32), axis=0, keepdims=True)
        out[...] = own + weighted(key, value, suffix(share))


def pool_kernel(lengths, state_1, state_2, state_3, feats, sums, short, gain, part):
    tokens = feats.shape[0] // 2
    z, x, u = places()
    long_u = jnp.where(lengths[0, 0] > tokens, u, 1 - u)
    states = [(jnp.bitwise_xor(z, j) < z, ref) for j, ref in enumerate((state_1, state_2, state_3), 1)]
    before = jnp.zeros((1, GROUP), jnp.float32)
    for earlier, ref in states:
        rows = ref[GROUP : GROUP + 16, :].astype(jnp.float32)
        total = jnp.concatenate([rows[0:1] + rows[2:3], rows[1:2] + rows[3:4]], axis=1)
        before = before + jnp.where(earlier, total, 0.0)

    def block(slot):
        at = pl.ds(slot * tokens, tokens)
        return feats[at, :GROUP], feats[at, GROUP : 2 * GROUP], feats[at, 2 * GROUP :]

    query_one, key_one, value_one = block(0)
    query_two, key_two, value_two = block(1)
    share_one, carry = shares(query_one, key_one, before)
    share_two, _ = shares(query_two, key_two, carry)
    after_two = suffix(share_two)
    after_one = suffix(share_one) + after_two[0:1, :]
    long_row = weighted(key_one, value_one, after_one) + weighted(key_two, value_two, after_two) + sums[...]
    weight = after_one[0:1, :]
    for earlier, ref in states:
        high, low = split_two(jnp.where(earlier, weight, 0.0))
        products = []
        for h in range(GROUP // HEAD_DIM):
            at = h * HEAD_DIM
            both = jnp.concatenate([high[:, at : at + HEAD_DIM]] * 8 + [low[:, at : at + HEAD_DIM]] * 8, axis=0)
            out = jnp.dot(both, ref[at : at + HEAD_DIM, :], preferred_element_type=jnp.float32)
            products.append(out[0:1] + out[8:9])
        long_row = long_row + jnp.concatenate(products, axis=1)

    short_row = short[...]
    first = jnp.where(long_u == 0, long_row, short_row)
    second = jnp.where(long_u == 0, short_row, long_row)
    own_gain = gain[:, pl.ds(pl.multiple_of((2 * x + u) * GROUP, GROUP), GROUP)]
    half = jnp.where(lax.rem(z, 2) == 0, own_gain[:, :HEAD_DIM], own_gain[:, HEAD_DIM:])
    part[...] = jnp.broadcast_to(jnp.concatenate([first, second, half], axis=1)[None], part.shape)


def loss_kernel(positives, parts, vec, loss, mine):
    z, x, u = places()
    domain = lax.axis_index("domain")
    width = mine.shape[1]
    piece = vec.shape[2]

    def collect(place):
        groups = []
        for group in range(PLANE):
            at = [parts[2 * (PLANE * plane + group) + place] for plane in range(PLANES)]
            total = (at[0][:, : 2 * GROUP] + at[1][:, : 2 * GROUP]) + (at[2][:, : 2 * GROUP] + at[3][:, : 2 * GROUP])
            gain = jnp.concatenate([at[0][:, 2 * GROUP :], at[1][:, 2 * GROUP :]], axis=1)
            groups.append((total[:, :GROUP], total[:, GROUP:], gain))
        return groups

    def reduced(terms):
        total = (terms[0] + terms[1]) + (terms[2] + terms[3])
        return jnp.sum(total, axis=1, keepdims=True)

    own = [(jnp.where(u == 0, a, b), gain) for a, b, gain in collect(domain)]
    other = collect(1 - domain)
    scaled = [a * gain for a, gain in own]
    for group in range(PLANE):
        mine[:, group * GROUP : (group + 1) * GROUP] = scaled[group]
    factor = lax.rsqrt(reduced([a * a for a, _ in own]) / width + epsilon)
    logits = []
    for user in range(2):
        norm = reduced([o[user] * o[user] for o in other])
        product = reduced([s * (o[user] * o[2]) for s, o in zip(scaled, other)])
        logits.append(product * factor * lax.rsqrt(norm / width + epsilon) * (logit_scale / width))
    start = pl.multiple_of((2 * z + x) * piece, piece)
    vec[0] = (mine[:, pl.ds(start, piece)] * factor).astype(jnp.bfloat16)
    forward = jnp.where(u == 0, positives[0], positives[1])
    backward = jnp.where(positives[0] == u, 0, 1)
    partner = jnp.where(domain == 0, forward, backward)
    top = jnp.maximum(logits[0], logits[1])
    spread = jnp.log(jnp.exp(logits[0] - top) + jnp.exp(logits[1] - top)) + top
    loss[...] = spread - jnp.where(partner == 0, logits[0], logits[1])


def vmem():
    return pl.BlockSpec(memory_space=pltpu.VMEM)


def anywhere():
    return pl.BlockSpec(memory_space=pl.ANY)


def hbm():
    return pl.BlockSpec(memory_space=pltpu.HBM)


def smem():
    return pl.BlockSpec(memory_space=pltpu.SMEM)


def call(kernel, outs, in_specs, scratch, flops):
    return pl.pallas_call(
        kernel,
        out_shape=outs,
        in_specs=in_specs,
        out_specs=jax.tree.map(lambda _: vmem(), outs),
        scratch_shapes=scratch,
        compiler_params=pltpu.CompilerParams(vmem_limit_bytes=40 * 1024 * 1024),
        cost_estimate=pl.CostEstimate(flops=flops, bytes_accessed=2**21, transcendentals=0),
    )


def towers(history, qkv_weight, norm_gain, pool_gain, lengths, positives):
    events = history[0, 0]
    tokens, width = events.shape
    weight = qkv_weight[0]
    rows = weight.shape[0]
    f32, bf16 = jnp.float32, jnp.bfloat16
    shape = jax.ShapeDtypeStruct
    here = PLANE * PLANES

    def hop(a, target):
        pairs = [(i, target(i // PLANE) * PLANE + i % PLANE) for i in range(here) if target(i // PLANE) is not None]
        return lax.ppermute(a, ("seq", "dp"), pairs)

    def plane_hop(a, move):
        return lax.ppermute(a, ("seq", "dp"), [(i, i ^ move) for i in range(here)])

    def each(a):
        return [hop(a, lambda p: p ^ j) for j in range(1, PLANES)]

    wide = 3 * GROUP
    w_own, w_sent = call(
        pack_kernel, (shape((rows, wide), bf16),) * 2, [hbm()], [pltpu.SemaphoreType.DMA((6,))], 0
    )(weight)
    two_own = hop(w_own, lambda p: p ^ 2)
    far_own = hop(two_own, lambda p: {1: 0, 2: 3}.get(p))
    w_near = plane_hop(w_sent, 2)
    two_near = hop(call(gate_kernel, shape((rows, wide), bf16), [vmem()] + [anywhere()] * 1, [], 0)(w_near, two_own), lambda p: p ^ 2)
    one_near = hop(w_near, lambda p: p ^ 1)
    far_near = hop(call(gate_kernel, shape((rows, wide), bf16), [vmem()] + [anywhere()] * 1, [], 0)(two_near, far_own), lambda p: {1: 0, 2: 3}.get(p))
    both = jnp.concatenate([w_own, w_near], axis=0)
    corner = plane_hop(events, 3)
    near = plane_hop(events, 2)
    one_own = hop(w_own, lambda p: p ^ 1)
    next_both = hop(call(gate_kernel, shape((2 * rows, wide), bf16), [vmem()] + [anywhere()] * 1, [], 0)(both, one_own), lambda p: 3 - p if p in (1, 2) else None)
    across = plane_hop(events, 1)

    normed, sums, raw_short = call(
        norm_kernel,
        (shape((2 * tokens, width), bf16), shape((1, GROUP), f32), shape((tokens, width), bf16)),
        [smem()] + [anywhere()] * 4 + [vmem()],
        [pltpu.VMEM((2, tokens, width), bf16), pltpu.SemaphoreType.DMA((3,))],
        2 * 3 * tokens * width,
    )(lengths, events, near, across, corner, norm_gain)
    partial, weights = call(
        partial_kernel,
        (shape((2 * tokens, wide), f32), shape((width, wide), bf16)),
        [vmem()] * 7,
        [],
        2 * 2 * tokens * 3 * GROUP * wide,
    )(normed, w_own, w_near, one_own, one_near, two_own, two_near)
    feats, message, last = call(
        project_kernel,
        (shape((2 * tokens, wide), bf16), shape((MESSAGE, HEAD_DIM), bf16), shape((GROUP, wide), bf16)),
        [vmem()] * 5,
        [],
        2 * 2 * tokens * GROUP * wide,
    )(normed, partial, next_both, far_own, far_near)
    short = call(
        short_kernel, shape((1, GROUP), f32), [vmem()] * 4, [], 2 * tokens * width * wide
    )(raw_short, weights, last, norm_gain)
    part = call(
        pool_kernel,
        shape((2 * here, 1, 2 * GROUP + HEAD_DIM), f32),
        [smem()] + [vmem()] * 7,
        [],
        2 * 9 * tokens * tokens * GROUP,
    )(lengths, *each(message), feats, sums, short, pool_gain)
    parts = lax.all_to_all(part, ("seq", "dp", "domain"), 0, 0, tiled=True)
    vec, loss = call(
        loss_kernel,
        (shape((1, 1, width // 8), bf16), shape((1, 1), f32)),
        [smem(), vmem()],
        [pltpu.VMEM((1, width), f32)],
        2**14,
    )(positives, parts)
    return vec, loss


def solution(mesh):
    placed = (
        P("domain", "dp", "seq", None),
        P("domain", "seq", None),
        P("domain", None),
        P("domain", None),
        P("domain", "dp"),
        P(),
    )
    small = mesh.shape["seq"] == 2 * PLANES and mesh.shape["dp"] == 2
    return jax.shard_map(
        towers if small else shards,
        mesh=mesh,
        in_specs=placed,
        out_specs=(P("domain", "dp", "seq"), P("domain", "dp")),
        check_vma=False,
    )
```

```python
import functools

import jax
import jax.numpy as jnp
from jax import lax
from jax.experimental import pallas as pl
from jax.experimental.pallas import tpu as pltpu
from jax.sharding import PartitionSpec as P

HEADS = 8
HEAD_DIM = 128


logit_scale = 20.0
epsilon = 1e-06
highest = lax.Precision.HIGHEST


def carried_in(part, axis, combine, identity):
    place = lax.axis_index(axis)
    gathered = jax.tree.map(lambda a: lax.all_gather(a, axis), part)
    state = jax.tree.map(lambda a, e: jnp.zeros_like(a) + jnp.asarray(e, a.dtype), part, identity)

    def one(hop, state):
        return combine(
            state, jax.tree.map(lambda a: lax.dynamic_index_in_dim(a, hop, 0, False), gathered)
        )

    return lax.fori_loop(0, place, one, state)


def partner_2(block, axis, stride):
    count = lax.axis_size(axis)
    route = []
    for low in range(count):
        high = low | 1 << stride
        if high != low and high < count:
            route += [(low, high), (high, low)]
    return lax.ppermute(block, axis, route)


def feature_map(values):
    return jax.nn.elu(values) + 1.0


def add_pair(earlier, later):
    return (earlier[0] + later[0], earlier[1] + later[1])


def shards(history, qkv_weight, norm_gain, pool_gain, lengths, positives):
    seq_count = lax.axis_size("seq")
    seq_place = lax.axis_index("seq")
    group_place = lax.axis_index("dp")
    domain_place = lax.axis_index("domain")
    events = history[0]
    users_dev, tokens_dev, width = events.shape
    row_count = users_dev * tokens_dev
    wide = events.astype(jnp.float32)
    normed = (
        wide * lax.rsqrt(jnp.mean(wide * wide, -1, keepdims=True) + epsilon) * norm_gain[0]
    ).astype(jnp.bfloat16)
    normed = normed.reshape(row_count, width)
    rows_here = qkv_weight[0]
    projected = jnp.dot(
        normed,
        lax.all_gather(rows_here, "seq", axis=0, tiled=True),
        preferred_element_type=jnp.float32,
    )
    query_raw = projected[:, :width]
    key_raw = projected[:, width : 2 * width]
    value_raw = projected[:, 2 * width :]
    positions = seq_place * tokens_dev + jnp.arange(tokens_dev)
    valid = positions[None, :] < lengths[0][:, None]
    shape_heads = (users_dev, tokens_dev, HEADS, HEAD_DIM)
    queries = feature_map(query_raw).astype(jnp.bfloat16).reshape(shape_heads)
    key_feats = (
        jnp.where(valid.reshape(row_count)[:, None], feature_map(key_raw), 0.0)
        .astype(jnp.bfloat16)
        .reshape(shape_heads)
    )
    val_feats = value_raw.astype(jnp.bfloat16).reshape(shape_heads)
    local_state = jnp.einsum(
        "uthc,uthd->uhcd", key_feats, val_feats, preferred_element_type=jnp.float32
    )
    local_total = jnp.sum(key_feats.astype(jnp.float32), axis=1)
    state_before, total_before = carried_in(
        (local_state, local_total),
        "seq",
        add_pair,
        (jnp.zeros_like(local_state), jnp.zeros_like(local_total)),
    )
    causal = jnp.arange(tokens_dev)[:, None] >= jnp.arange(tokens_dev)[None, :]
    scores = jnp.einsum("uthc,ushc->uhts", queries, key_feats, preferred_element_type=jnp.float32)
    scores = jnp.where(causal, scores, 0.0)
    denominator = jnp.sum(scores, axis=-1) + jnp.einsum(
        "uthc,uhc->uht", queries.astype(jnp.float32), total_before, precision=highest
    )
    numerator = jnp.einsum(
        "uhts,ushc->uthc",
        scores.astype(jnp.bfloat16),
        val_feats,
        preferred_element_type=jnp.float32,
    )
    numerator = numerator + jnp.einsum(
        "uthc,uhcd->uthd",
        queries,
        state_before.astype(jnp.bfloat16),
        preferred_element_type=jnp.float32,
    )
    attended = numerator / jnp.transpose(denominator, (0, 2, 1))[..., None]
    attended = attended.reshape(users_dev, tokens_dev, width)
    partial_value = jnp.sum(jnp.where(valid[..., None], wide + attended, 0.0), axis=1)
    piece_width = width // seq_count
    gain_row = pool_gain[0]
    pooled = lax.psum(partial_value, "seq")
    factor = lax.rsqrt(jnp.mean(pooled * pooled, -1, keepdims=True) + epsilon)
    full_vec = (pooled * factor * gain_row).astype(jnp.bfloat16)
    out_vec = lax.dynamic_slice_in_dim(full_vec, seq_place * piece_width, piece_width, 1)
    group = lax.all_gather(full_vec, "dp", axis=0, tiled=True)
    other = partner_2(group, "domain", 0)
    logits = jnp.einsum("uc,vc->uv", full_vec, other, preferred_element_type=jnp.float32) * (
        logit_scale / width
    )
    users_all = other.shape[0]
    own_index = group_place * users_dev + jnp.arange(users_dev)
    targets = lax.dynamic_slice_in_dim(positives, group_place * users_dev, users_dev)
    forward_pair = targets[:, None] == jnp.arange(users_all)[None, :]
    backward_pair = positives[None, :] == own_index[:, None]
    partner = jnp.where(domain_place == 0, forward_pair, backward_pair)
    loss = jnp.log(jnp.sum(jnp.exp(logits), axis=-1)) - jnp.sum(
        jnp.where(partner, logits, 0.0), axis=-1
    )
    return (out_vec[None], loss[None])


PLANE = 4
PLANES = 4
GROUP = 256
DOT_T = (((0,), (0,)), ((), ()))
MESSAGE = GROUP + 16


def places():
    seq_place = lax.axis_index("seq")
    return lax.div(seq_place, 2), lax.rem(seq_place, 2), lax.axis_index("dp")


def head_sums(a):
    return [
        jnp.sum(a[:, h * HEAD_DIM : (h + 1) * HEAD_DIM], axis=1, keepdims=True)
        for h in range(GROUP // HEAD_DIM)
    ]


def by_head(columns):
    rows = columns[0].shape[0]
    return jnp.concatenate([jnp.broadcast_to(c, (rows, HEAD_DIM)) for c in columns], axis=1)


def split_two(a):
    high = a.astype(jnp.bfloat16)
    return high, (a - high.astype(jnp.float32)).astype(jnp.bfloat16)


def pack_kernel(weight, own, sent, sems):
    _, x, u = places()
    width = weight.shape[1] // 3
    copies = []
    for move, out in ((2, sent), (0, own)):
        group = jnp.bitwise_xor(2 * x + u, move)
        for part in range(3):
            start = pl.multiple_of(part * width + group * GROUP, GROUP)
            copies.append(
                pltpu.make_async_copy(
                    weight.at[:, pl.ds(start, GROUP)], out.at[:, pl.ds(part * GROUP, GROUP)], sems.at[len(copies)]
                )
            )
    for copy in copies:
        copy.start()
    for copy in copies:
        copy.wait()


def gate_kernel(values, *rest):
    rest[-1][...] = values[...]


def normalise(values, gain):
    wide = values.astype(jnp.float32)
    scale = lax.rsqrt(jnp.mean(wide * wide, axis=1, keepdims=True) + epsilon)
    return (wide * scale * gain).astype(jnp.bfloat16)


def features(out):
    raw = out[:, : 2 * GROUP]
    low = jnp.where(raw > 0.0, raw + 1.0, jnp.exp(jnp.minimum(raw, 0.0))).astype(jnp.bfloat16)
    return low[:, :GROUP], low[:, GROUP:], out[:, 2 * GROUP :].astype(jnp.bfloat16)


def norm_kernel(lengths, own, near, across, corner, gain, normed, sums, short, raw, sems):
    tokens = own.shape[0]
    _, x, u = places()
    long_u = jnp.where(lengths[0, 0] > tokens, u, 1 - u)
    for slot in range(3):
        from_x = 1 if slot == 1 else 0
        from_u = 1 - long_u if slot == 2 else long_u
        pick = jnp.bitwise_xor(x, from_x) + 2 * jnp.bitwise_xor(u, from_u)
        dest = short if slot == 2 else raw.at[slot]
        for j, ref in enumerate((own, near, across, corner)):

            @pl.when(pick == j)
            def _():
                pltpu.make_async_copy(ref, dest, sems.at[slot]).start()

    columns = pl.ds(pl.multiple_of((2 * x + u) * GROUP, GROUP), GROUP)
    total = jnp.zeros((1, GROUP), jnp.float32)
    for slot in range(2):
        pltpu.make_async_copy(own, raw.at[slot], sems.at[slot]).wait()
        normed[pl.ds(slot * tokens, tokens), :] = normalise(raw[slot], gain[...])
        total = total + jnp.sum(raw[slot, :, columns].astype(jnp.float32), axis=0, keepdims=True)
    sums[...] = total
    pltpu.make_async_copy(own, short, sems.at[2]).wait()


def place_rows(dest, start, x, here, there):
    rows = here.shape[0]
    for place, values in ((x, here), (1 - x, there)):
        dest[pl.ds(pl.multiple_of(start + place * rows, rows), rows), :] = values


def partial_kernel(normed, own, near, one_own, one_near, two_own, two_near, partial, weights):
    z, x, _ = places()
    parts = ((own, near), (one_own, one_near), (two_own, two_near), None)
    starts = [pl.multiple_of(jnp.bitwise_xor(z, j) * GROUP, GROUP) for j in range(PLANES)]
    for start, refs in zip(starts, parts):
        if refs is None:
            weights[pl.ds(start, GROUP), :] = jnp.zeros((GROUP, weights.shape[1]), weights.dtype)
        else:
            place_rows(weights, start, x, refs[0][...], refs[1][...])
    total = None
    for start in starts[:3]:
        rows = pl.ds(start, GROUP)
        out = jnp.dot(normed[:, rows], weights[rows, :], preferred_element_type=jnp.float32)
        total = out if total is None else total + out
    partial[...] = total


def project_kernel(normed, partial, far_own, far_near, feats, message, last):
    tokens = normed.shape[0]
    z, x, _ = places()
    place_rows(last, 0, x, far_own[...], far_near[...])
    columns = pl.ds(pl.multiple_of((3 - z) * GROUP, GROUP), GROUP)
    half = tokens // 2
    total = jnp.zeros((1, GROUP), jnp.float32)
    for part in range(2):
        at = pl.ds(part * half, half)
        out = partial[at, :] + jnp.dot(normed[at, columns], last[...], preferred_element_type=jnp.float32)
        query, key, value = features(out)
        feats[at, :GROUP] = query
        feats[at, GROUP : 2 * GROUP] = key
        feats[at, 2 * GROUP :] = value
        total = total + jnp.sum(key.astype(jnp.float32), axis=0, keepdims=True)
    high, low = split_two(total)
    for h in range(GROUP // HEAD_DIM):
        at = h * HEAD_DIM
        key = feats[:, GROUP + at : GROUP + at + HEAD_DIM]
        value = feats[:, 2 * GROUP + at : 2 * GROUP + at + HEAD_DIM]
        state = lax.dot_general(key, value, DOT_T, preferred_element_type=jnp.float32)
        message[at : at + HEAD_DIM, :] = state.astype(jnp.bfloat16)
    total_rows = [high[:, :HEAD_DIM], high[:, HEAD_DIM:], low[:, :HEAD_DIM], low[:, HEAD_DIM:]]
    message[GROUP:, :] = jnp.concatenate(total_rows * 4, axis=0)


def triangle(tokens, upper):
    row = lax.broadcasted_iota(jnp.int32, (tokens, tokens), 0)
    col = lax.broadcasted_iota(jnp.int32, (tokens, tokens), 1)
    return (row <= col if upper else row >= col).astype(jnp.bfloat16)


def shares(query, key, carry):
    prefix = jnp.dot(triangle(key.shape[0], False), key, preferred_element_type=jnp.float32) + carry
    wide = query.astype(jnp.float32)
    return wide / by_head(head_sums(wide * prefix)), prefix[key.shape[0] - 1 :, :]


def suffix(share):
    upper = triangle(share.shape[0], True)
    high, low = split_two(share)
    return jnp.dot(upper, high, preferred_element_type=jnp.float32) + jnp.dot(
        upper, low, preferred_element_type=jnp.float32
    )


def weighted(key, value, after):
    weight = by_head(head_sums(key.astype(jnp.float32) * after))
    return jnp.sum(weight * value.astype(jnp.float32), axis=0, keepdims=True)


def short_kernel(raw, weights, last, gain, out):
    z, x, u = places()
    out[...] = jnp.zeros(out.shape, jnp.float32)

    @pl.when(z == 0)
    def _():
        low = normalise(raw[...], gain[...])
        wide = jnp.dot(low, weights[...], preferred_element_type=jnp.float32)
        wide = wide + jnp.dot(low[:, 3 * GROUP :], last[...], preferred_element_type=jnp.float32)
        query, key, value = features(wide)
        share, _ = shares(query, key, jnp.zeros((1, GROUP), jnp.float32))
        columns = pl.ds(pl.multiple_of((2 * x + u) * GROUP, GROUP), GROUP)
        own = jnp.sum(raw[:, columns].astype(jnp.float32), axis=0, keepdims=True)
        out[...] = own + weighted(key, value, suffix(share))


def pool_kernel(lengths, state_1, state_2, state_3, feats, sums, short, gain, part):
    tokens = feats.shape[0] // 2
    z, x, u = places()
    long_u = jnp.where(lengths[0, 0] > tokens, u, 1 - u)
    states = [(jnp.bitwise_xor(z, j) < z, ref) for j, ref in enumerate((state_1, state_2, state_3), 1)]
    before = jnp.zeros((1, GROUP), jnp.float32)
    for earlier, ref in states:
        rows = ref[GROUP : GROUP + 16, :].astype(jnp.float32)
        total = jnp.concatenate([rows[0:1] + rows[2:3], rows[1:2] + rows[3:4]], axis=1)
        before = before + jnp.where(earlier, total, 0.0)

    def block(slot):
        at = pl.ds(slot * tokens, tokens)
        return feats[at, :GROUP], feats[at, GROUP : 2 * GROUP], feats[at, 2 * GROUP :]

    query_one, key_one, value_one = block(0)
    query_two, key_two, value_two = block(1)
    share_one, carry = shares(query_one, key_one, before)
    share_two, _ = shares(query_two, key_two, carry)
    after_two = suffix(share_two)
    after_one = suffix(share_one) + after_two[0:1, :]
    long_row = weighted(key_one, value_one, after_one) + weighted(key_two, value_two, after_two) + sums[...]
    weight = after_one[0:1, :]
    for earlier, ref in states:
        high, low = split_two(jnp.where(earlier, weight, 0.0))
        products = []
        for h in range(GROUP // HEAD_DIM):
            at = h * HEAD_DIM
            both = jnp.concatenate([high[:, at : at + HEAD_DIM]] * 8 + [low[:, at : at + HEAD_DIM]] * 8, axis=0)
            out = jnp.dot(both, ref[at : at + HEAD_DIM, :], preferred_element_type=jnp.float32)
            products.append(out[0:1] + out[8:9])
        long_row = long_row + jnp.concatenate(products, axis=1)

    short_row = short[...]
    first = jnp.where(long_u == 0, long_row, short_row)
    second = jnp.where(long_u == 0, short_row, long_row)
    own_gain = gain[:, pl.ds(pl.multiple_of((2 * x + u) * GROUP, GROUP), GROUP)]
    half = jnp.where(lax.rem(z, 2) == 0, own_gain[:, :HEAD_DIM], own_gain[:, HEAD_DIM:])
    part[...] = jnp.broadcast_to(jnp.concatenate([first, second, half], axis=1)[None], part.shape)


def loss_kernel(positives, parts, vec, loss, mine):
    z, x, u = places()
    domain = lax.axis_index("domain")
    width = mine.shape[1]
    piece = vec.shape[2]

    def collect(place):
        groups = []
        for group in range(PLANE):
            at = [parts[2 * (PLANE * plane + group) + place] for plane in range(PLANES)]
            total = (at[0][:, : 2 * GROUP] + at[1][:, : 2 * GROUP]) + (at[2][:, : 2 * GROUP] + at[3][:, : 2 * GROUP])
            gain = jnp.concatenate([at[0][:, 2 * GROUP :], at[1][:, 2 * GROUP :]], axis=1)
            groups.append((total[:, :GROUP], total[:, GROUP:], gain))
        return groups

    def reduced(terms):
        total = (terms[0] + terms[1]) + (terms[2] + terms[3])
        return jnp.sum(total, axis=1, keepdims=True)

    own = [(jnp.where(u == 0, a, b), gain) for a, b, gain in collect(domain)]
    other = collect(1 - domain)
    scaled = [a * gain for a, gain in own]
    for group in range(PLANE):
        mine[:, group * GROUP : (group + 1) * GROUP] = scaled[group]
    factor = lax.rsqrt(reduced([a * a for a, _ in own]) / width + epsilon)
    logits = []
    for user in range(2):
        norm = reduced([o[user] * o[user] for o in other])
        product = reduced([s * (o[user] * o[2]) for s, o in zip(scaled, other)])
        logits.append(product * factor * lax.rsqrt(norm / width + epsilon) * (logit_scale / width))
    start = pl.multiple_of((2 * z + x) * piece, piece)
    vec[0] = (mine[:, pl.ds(start, piece)] * factor).astype(jnp.bfloat16)
    forward = jnp.where(u == 0, positives[0], positives[1])
    backward = jnp.where(positives[0] == u, 0, 1)
    partner = jnp.where(domain == 0, forward, backward)
    top = jnp.maximum(logits[0], logits[1])
    spread = jnp.log(jnp.exp(logits[0] - top) + jnp.exp(logits[1] - top)) + top
    loss[...] = spread - jnp.where(partner == 0, logits[0], logits[1])


def vmem():
    return pl.BlockSpec(memory_space=pltpu.VMEM)


def anywhere():
    return pl.BlockSpec(memory_space=pl.ANY)


def hbm():
    return pl.BlockSpec(memory_space=pltpu.HBM)


def smem():
    return pl.BlockSpec(memory_space=pltpu.SMEM)


def call(kernel, outs, in_specs, scratch, flops):
    return pl.pallas_call(
        kernel,
        out_shape=outs,
        in_specs=in_specs,
        out_specs=jax.tree.map(lambda _: vmem(), outs),
        scratch_shapes=scratch,
        compiler_params=pltpu.CompilerParams(vmem_limit_bytes=40 * 1024 * 1024),
        cost_estimate=pl.CostEstimate(flops=flops, bytes_accessed=2**21, transcendentals=0),
    )


def towers(history, qkv_weight, norm_gain, pool_gain, lengths, positives):
    events = history[0, 0]
    tokens, width = events.shape
    weight = qkv_weight[0]
    rows = weight.shape[0]
    f32, bf16 = jnp.float32, jnp.bfloat16
    shape = jax.ShapeDtypeStruct
    here = PLANE * PLANES

    def hop(a, target):
        pairs = [(i, target(i // PLANE) * PLANE + i % PLANE) for i in range(here) if target(i // PLANE) is not None]
        return lax.ppermute(a, ("seq", "dp"), pairs)

    def plane_hop(a, move):
        return lax.ppermute(a, ("seq", "dp"), [(i, i ^ move) for i in range(here)])

    def each(a):
        return [hop(a, lambda p: p ^ j) for j in range(1, PLANES)]

    wide = 3 * GROUP
    w_own, w_sent = call(
        pack_kernel, (shape((rows, wide), bf16),) * 2, [hbm()], [pltpu.SemaphoreType.DMA((6,))], 0
    )(weight)
    across = plane_hop(events, 1)
    two_own = hop(w_own, lambda p: p ^ 2)
    one_own = hop(w_own, lambda p: p ^ 1)
    near = plane_hop(events, 2)
    corner = plane_hop(events, 3)
    w_near = plane_hop(w_sent, 2)
    one_near = hop(call(gate_kernel, shape((rows, wide), bf16), [vmem()] + [anywhere()] * 1, [], 0)(w_near, one_own), lambda p: p ^ 1)
    far_own = hop(call(gate_kernel, shape((rows, wide), bf16), [vmem()] + [anywhere()] * 1, [], 0)(two_own, one_near), lambda p: p ^ 1)
    two_near = hop(w_near, lambda p: p ^ 2)
    far_near = hop(call(gate_kernel, shape((rows, wide), bf16), [vmem()] + [anywhere()] * 1, [], 0)(two_near, one_near), lambda p: p ^ 1)

    normed, sums, raw_short = call(
        norm_kernel,
        (shape((2 * tokens, width), bf16), shape((1, GROUP), f32), shape((tokens, width), bf16)),
        [smem()] + [anywhere()] * 4 + [vmem()],
        [pltpu.VMEM((2, tokens, width), bf16), pltpu.SemaphoreType.DMA((3,))],
        2 * 3 * tokens * width,
    )(lengths, events, near, across, corner, norm_gain)
    partial, weights = call(
        partial_kernel,
        (shape((2 * tokens, wide), f32), shape((width, wide), bf16)),
        [vmem()] * 7,
        [],
        2 * 2 * tokens * 3 * GROUP * wide,
    )(normed, w_own, w_near, one_own, one_near, two_own, two_near)
    feats, message, last = call(
        project_kernel,
        (shape((2 * tokens, wide), bf16), shape((MESSAGE, HEAD_DIM), bf16), shape((GROUP, wide), bf16)),
        [vmem()] * 4,
        [],
        2 * 2 * tokens * GROUP * wide,
    )(normed, partial, far_own, far_near)
    short = call(
        short_kernel, shape((1, GROUP), f32), [vmem()] * 4, [], 2 * tokens * width * wide
    )(raw_short, weights, last, norm_gain)
    part = call(
        pool_kernel,
        shape((2 * here, 1, 2 * GROUP + HEAD_DIM), f32),
        [smem()] + [vmem()] * 7,
        [],
        2 * 9 * tokens * tokens * GROUP,
    )(lengths, *each(message), feats, sums, short, pool_gain)
    parts = lax.all_to_all(part, ("seq", "dp", "domain"), 0, 0, tiled=True)
    vec, loss = call(
        loss_kernel,
        (shape((1, 1, width // 8), bf16), shape((1, 1), f32)),
        [smem(), vmem()],
        [pltpu.VMEM((1, width), f32)],
        2**14,
    )(positives, parts)
    return vec, loss


def solution(mesh):
    placed = (
        P("domain", "dp", "seq", None),
        P("domain", "seq", None),
        P("domain", None),
        P("domain", None),
        P("domain", "dp"),
        P(),
    )
    small = mesh.shape["seq"] == 2 * PLANES and mesh.shape["dp"] == 2
    return jax.shard_map(
        towers if small else shards,
        mesh=mesh,
        in_specs=placed,
        out_specs=(P("domain", "dp", "seq"), P("domain", "dp")),
        check_vma=False,
    )
```

```python
import functools

import jax
import jax.numpy as jnp
from jax import lax
from jax.experimental import pallas as pl
from jax.experimental.pallas import tpu as pltpu
from jax.sharding import PartitionSpec as P

HEADS = 8
HEAD_DIM = 128


logit_scale = 20.0
epsilon = 1e-06
highest = lax.Precision.HIGHEST


def carried_in(part, axis, combine, identity):
    place = lax.axis_index(axis)
    gathered = jax.tree.map(lambda a: lax.all_gather(a, axis), part)
    state = jax.tree.map(lambda a, e: jnp.zeros_like(a) + jnp.asarray(e, a.dtype), part, identity)

    def one(hop, state):
        return combine(
            state, jax.tree.map(lambda a: lax.dynamic_index_in_dim(a, hop, 0, False), gathered)
        )

    return lax.fori_loop(0, place, one, state)


def partner_2(block, axis, stride):
    count = lax.axis_size(axis)
    route = []
    for low in range(count):
        high = low | 1 << stride
        if high != low and high < count:
            route += [(low, high), (high, low)]
    return lax.ppermute(block, axis, route)


def feature_map(values):
    return jax.nn.elu(values) + 1.0


def add_pair(earlier, later):
    return (earlier[0] + later[0], earlier[1] + later[1])


def shards(history, qkv_weight, norm_gain, pool_gain, lengths, positives):
    seq_count = lax.axis_size("seq")
    seq_place = lax.axis_index("seq")
    group_place = lax.axis_index("dp")
    domain_place = lax.axis_index("domain")
    events = history[0]
    users_dev, tokens_dev, width = events.shape
    row_count = users_dev * tokens_dev
    wide = events.astype(jnp.float32)
    normed = (
        wide * lax.rsqrt(jnp.mean(wide * wide, -1, keepdims=True) + epsilon) * norm_gain[0]
    ).astype(jnp.bfloat16)
    normed = normed.reshape(row_count, width)
    rows_here = qkv_weight[0]
    projected = jnp.dot(
        normed,
        lax.all_gather(rows_here, "seq", axis=0, tiled=True),
        preferred_element_type=jnp.float32,
    )
    query_raw = projected[:, :width]
    key_raw = projected[:, width : 2 * width]
    value_raw = projected[:, 2 * width :]
    positions = seq_place * tokens_dev + jnp.arange(tokens_dev)
    valid = positions[None, :] < lengths[0][:, None]
    shape_heads = (users_dev, tokens_dev, HEADS, HEAD_DIM)
    queries = feature_map(query_raw).astype(jnp.bfloat16).reshape(shape_heads)
    key_feats = (
        jnp.where(valid.reshape(row_count)[:, None], feature_map(key_raw), 0.0)
        .astype(jnp.bfloat16)
        .reshape(shape_heads)
    )
    val_feats = value_raw.astype(jnp.bfloat16).reshape(shape_heads)
    local_state = jnp.einsum(
        "uthc,uthd->uhcd", key_feats, val_feats, preferred_element_type=jnp.float32
    )
    local_total = jnp.sum(key_feats.astype(jnp.float32), axis=1)
    state_before, total_before = carried_in(
        (local_state, local_total),
        "seq",
        add_pair,
        (jnp.zeros_like(local_state), jnp.zeros_like(local_total)),
    )
    causal = jnp.arange(tokens_dev)[:, None] >= jnp.arange(tokens_dev)[None, :]
    scores = jnp.einsum("uthc,ushc->uhts", queries, key_feats, preferred_element_type=jnp.float32)
    scores = jnp.where(causal, scores, 0.0)
    denominator = jnp.sum(scores, axis=-1) + jnp.einsum(
        "uthc,uhc->uht", queries.astype(jnp.float32), total_before, precision=highest
    )
    numerator = jnp.einsum(
        "uhts,ushc->uthc",
        scores.astype(jnp.bfloat16),
        val_feats,
        preferred_element_type=jnp.float32,
    )
    numerator = numerator + jnp.einsum(
        "uthc,uhcd->uthd",
        queries,
        state_before.astype(jnp.bfloat16),
        preferred_element_type=jnp.float32,
    )
    attended = numerator / jnp.transpose(denominator, (0, 2, 1))[..., None]
    attended = attended.reshape(users_dev, tokens_dev, width)
    partial_value = jnp.sum(jnp.where(valid[..., None], wide + attended, 0.0), axis=1)
    piece_width = width // seq_count
    gain_row = pool_gain[0]
    pooled = lax.psum(partial_value, "seq")
    factor = lax.rsqrt(jnp.mean(pooled * pooled, -1, keepdims=True) + epsilon)
    full_vec = (pooled * factor * gain_row).astype(jnp.bfloat16)
    out_vec = lax.dynamic_slice_in_dim(full_vec, seq_place * piece_width, piece_width, 1)
    group = lax.all_gather(full_vec, "dp", axis=0, tiled=True)
    other = partner_2(group, "domain", 0)
    logits = jnp.einsum("uc,vc->uv", full_vec, other, preferred_element_type=jnp.float32) * (
        logit_scale / width
    )
    users_all = other.shape[0]
    own_index = group_place * users_dev + jnp.arange(users_dev)
    targets = lax.dynamic_slice_in_dim(positives, group_place * users_dev, users_dev)
    forward_pair = targets[:, None] == jnp.arange(users_all)[None, :]
    backward_pair = positives[None, :] == own_index[:, None]
    partner = jnp.where(domain_place == 0, forward_pair, backward_pair)
    loss = jnp.log(jnp.sum(jnp.exp(logits), axis=-1)) - jnp.sum(
        jnp.where(partner, logits, 0.0), axis=-1
    )
    return (out_vec[None], loss[None])


PLANE = 4
PLANES = 4
GROUP = 256
DOT_T = (((0,), (0,)), ((), ()))
MESSAGE = GROUP + 16


def places():
    seq_place = lax.axis_index("seq")
    return lax.div(seq_place, 2), lax.rem(seq_place, 2), lax.axis_index("dp")


def head_sums(a):
    return [
        jnp.sum(a[:, h * HEAD_DIM : (h + 1) * HEAD_DIM], axis=1, keepdims=True)
        for h in range(GROUP // HEAD_DIM)
    ]


def by_head(columns):
    rows = columns[0].shape[0]
    return jnp.concatenate([jnp.broadcast_to(c, (rows, HEAD_DIM)) for c in columns], axis=1)


def split_two(a):
    high = a.astype(jnp.bfloat16)
    return high, (a - high.astype(jnp.float32)).astype(jnp.bfloat16)


def pack_kernel(weight, own, sent, sems):
    _, x, u = places()
    width = weight.shape[1] // 3
    copies = []
    for move, out in ((2, sent), (0, own)):
        group = jnp.bitwise_xor(2 * x + u, move)
        for part in range(3):
            start = pl.multiple_of(part * width + group * GROUP, GROUP)
            copies.append(
                pltpu.make_async_copy(
                    weight.at[:, pl.ds(start, GROUP)], out.at[:, pl.ds(part * GROUP, GROUP)], sems.at[len(copies)]
                )
            )
    for copy in copies:
        copy.start()
    for copy in copies:
        copy.wait()


def gate_kernel(values, *rest):
    rest[-1][...] = values[...]


def normalise(values, gain):
    wide = values.astype(jnp.float32)
    scale = lax.rsqrt(jnp.mean(wide * wide, axis=1, keepdims=True) + epsilon)
    return (wide * scale * gain).astype(jnp.bfloat16)


def features(out):
    raw = out[:, : 2 * GROUP]
    low = jnp.where(raw > 0.0, raw + 1.0, jnp.exp(jnp.minimum(raw, 0.0))).astype(jnp.bfloat16)
    return low[:, :GROUP], low[:, GROUP:], out[:, 2 * GROUP :].astype(jnp.bfloat16)


def norm_kernel(lengths, own, near, across, corner, gain, normed, sums, short, raw, sems):
    tokens = own.shape[0]
    _, x, u = places()
    long_u = jnp.where(lengths[0, 0] > tokens, u, 1 - u)
    for slot in range(3):
        from_x = 1 if slot == 1 else 0
        from_u = 1 - long_u if slot == 2 else long_u
        pick = jnp.bitwise_xor(x, from_x) + 2 * jnp.bitwise_xor(u, from_u)
        dest = short if slot == 2 else raw.at[slot]
        for j, ref in enumerate((own, near, across, corner)):

            @pl.when(pick == j)
            def _():
                pltpu.make_async_copy(ref, dest, sems.at[slot]).start()

    columns = pl.ds(pl.multiple_of((2 * x + u) * GROUP, GROUP), GROUP)
    total = jnp.zeros((1, GROUP), jnp.float32)
    for slot in range(2):
        pltpu.make_async_copy(own, raw.at[slot], sems.at[slot]).wait()
        normed[pl.ds(slot * tokens, tokens), :] = normalise(raw[slot], gain[...])
        total = total + jnp.sum(raw[slot, :, columns].astype(jnp.float32), axis=0, keepdims=True)
    sums[...] = total
    pltpu.make_async_copy(own, short, sems.at[2]).wait()


def place_rows(dest, start, x, here, there):
    rows = here.shape[0]
    for place, values in ((x, here), (1 - x, there)):
        dest[pl.ds(pl.multiple_of(start + place * rows, rows), rows), :] = values


def partial_kernel(normed, own, near, one_own, one_near, two_own, two_near, partial, weights):
    z, x, _ = places()
    parts = ((own, near), (one_own, one_near), (two_own, two_near), None)
    starts = [pl.multiple_of(jnp.bitwise_xor(z, j) * GROUP, GROUP) for j in range(PLANES)]
    for start, refs in zip(starts, parts):
        if refs is None:
            weights[pl.ds(start, GROUP), :] = jnp.zeros((GROUP, weights.shape[1]), weights.dtype)
        else:
            place_rows(weights, start, x, refs[0][...], refs[1][...])
    total = None
    for start in starts[:3]:
        rows = pl.ds(start, GROUP)
        out = jnp.dot(normed[:, rows], weights[rows, :], preferred_element_type=jnp.float32)
        total = out if total is None else total + out
    partial[...] = total


def project_kernel(normed, partial, far_own, far_near, feats, message, last):
    tokens = normed.shape[0]
    z, x, _ = places()
    place_rows(last, 0, x, far_own[...], far_near[...])
    columns = pl.ds(pl.multiple_of((3 - z) * GROUP, GROUP), GROUP)
    half = tokens // 2
    total = jnp.zeros((1, GROUP), jnp.float32)
    for part in range(2):
        at = pl.ds(part * half, half)
        out = partial[at, :] + jnp.dot(normed[at, columns], last[...], preferred_element_type=jnp.float32)
        query, key, value = features(out)
        feats[at, :GROUP] = query
        feats[at, GROUP : 2 * GROUP] = key
        feats[at, 2 * GROUP :] = value
        total = total + jnp.sum(key.astype(jnp.float32), axis=0, keepdims=True)
    high, low = split_two(total)
    for h in range(GROUP // HEAD_DIM):
        at = h * HEAD_DIM
        key = feats[:, GROUP + at : GROUP + at + HEAD_DIM]
        value = feats[:, 2 * GROUP + at : 2 * GROUP + at + HEAD_DIM]
        state = lax.dot_general(key, value, DOT_T, preferred_element_type=jnp.float32)
        message[at : at + HEAD_DIM, :] = state.astype(jnp.bfloat16)
    total_rows = [high[:, :HEAD_DIM], high[:, HEAD_DIM:], low[:, :HEAD_DIM], low[:, HEAD_DIM:]]
    message[GROUP:, :] = jnp.concatenate(total_rows * 4, axis=0)


def triangle(tokens, upper):
    row = lax.broadcasted_iota(jnp.int32, (tokens, tokens), 0)
    col = lax.broadcasted_iota(jnp.int32, (tokens, tokens), 1)
    return (row <= col if upper else row >= col).astype(jnp.bfloat16)


def shares(query, key, carry):
    prefix = jnp.dot(triangle(key.shape[0], False), key, preferred_element_type=jnp.float32) + carry
    wide = query.astype(jnp.float32)
    return wide / by_head(head_sums(wide * prefix)), prefix[key.shape[0] - 1 :, :]


def suffix(share):
    upper = triangle(share.shape[0], True)
    high, low = split_two(share)
    return jnp.dot(upper, high, preferred_element_type=jnp.float32) + jnp.dot(
        upper, low, preferred_element_type=jnp.float32
    )


def weighted(key, value, after):
    weight = by_head(head_sums(key.astype(jnp.float32) * after))
    return jnp.sum(weight * value.astype(jnp.float32), axis=0, keepdims=True)


def short_kernel(raw, weights, last, gain, out):
    z, x, u = places()
    out[...] = jnp.zeros(out.shape, jnp.float32)

    @pl.when(z == 0)
    def _():
        low = normalise(raw[...], gain[...])
        wide = jnp.dot(low, weights[...], preferred_element_type=jnp.float32)
        wide = wide + jnp.dot(low[:, 3 * GROUP :], last[...], preferred_element_type=jnp.float32)
        query, key, value = features(wide)
        share, _ = shares(query, key, jnp.zeros((1, GROUP), jnp.float32))
        columns = pl.ds(pl.multiple_of((2 * x + u) * GROUP, GROUP), GROUP)
        own = jnp.sum(raw[:, columns].astype(jnp.float32), axis=0, keepdims=True)
        out[...] = own + weighted(key, value, suffix(share))


def pool_kernel(lengths, state_1, state_2, state_3, feats, sums, short, gain, part):
    tokens = feats.shape[0] // 2
    z, x, u = places()
    long_u = jnp.where(lengths[0, 0] > tokens, u, 1 - u)
    states = [(jnp.bitwise_xor(z, j) < z, ref) for j, ref in enumerate((state_1, state_2, state_3), 1)]
    before = jnp.zeros((1, GROUP), jnp.float32)
    for earlier, ref in states:
        rows = ref[GROUP : GROUP + 16, :].astype(jnp.float32)
        total = jnp.concatenate([rows[0:1] + rows[2:3], rows[1:2] + rows[3:4]], axis=1)
        before = before + jnp.where(earlier, total, 0.0)

    def block(slot):
        at = pl.ds(slot * tokens, tokens)
        return feats[at, :GROUP], feats[at, GROUP : 2 * GROUP], feats[at, 2 * GROUP :]

    query_one, key_one, value_one = block(0)
    query_two, key_two, value_two = block(1)
    share_one, carry = shares(query_one, key_one, before)
    share_two, _ = shares(query_two, key_two, carry)
    after_two = suffix(share_two)
    after_one = suffix(share_one) + after_two[0:1, :]
    long_row = weighted(key_one, value_one, after_one) + weighted(key_two, value_two, after_two) + sums[...]
    weight = after_one[0:1, :]
    for earlier, ref in states:
        high, low = split_two(jnp.where(earlier, weight, 0.0))
        products = []
        for h in range(GROUP // HEAD_DIM):
            at = h * HEAD_DIM
            both = jnp.concatenate([high[:, at : at + HEAD_DIM]] * 8 + [low[:, at : at + HEAD_DIM]] * 8, axis=0)
            out = jnp.dot(both, ref[at : at + HEAD_DIM, :], preferred_element_type=jnp.float32)
            products.append(out[0:1] + out[8:9])
        long_row = long_row + jnp.concatenate(products, axis=1)

    short_row = short[...]
    first = jnp.where(long_u == 0, long_row, short_row)
    second = jnp.where(long_u == 0, short_row, long_row)
    own_gain = gain[:, pl.ds(pl.multiple_of((2 * x + u) * GROUP, GROUP), GROUP)]
    half = jnp.where(lax.rem(z, 2) == 0, own_gain[:, :HEAD_DIM], own_gain[:, HEAD_DIM:])
    part[...] = jnp.broadcast_to(jnp.concatenate([first, second, half], axis=1)[None], part.shape)


def loss_kernel(positives, parts, vec, loss, mine):
    z, x, u = places()
    domain = lax.axis_index("domain")
    width = mine.shape[1]
    piece = vec.shape[2]

    def collect(place):
        groups = []
        for group in range(PLANE):
            at = [parts[2 * (PLANE * plane + group) + place] for plane in range(PLANES)]
            total = (at[0][:, : 2 * GROUP] + at[1][:, : 2 * GROUP]) + (at[2][:, : 2 * GROUP] + at[3][:, : 2 * GROUP])
            gain = jnp.concatenate([at[0][:, 2 * GROUP :], at[1][:, 2 * GROUP :]], axis=1)
            groups.append((total[:, :GROUP], total[:, GROUP:], gain))
        return groups

    def reduced(terms):
        total = (terms[0] + terms[1]) + (terms[2] + terms[3])
        return jnp.sum(total, axis=1, keepdims=True)

    own = [(jnp.where(u == 0, a, b), gain) for a, b, gain in collect(domain)]
    other = collect(1 - domain)
    scaled = [a * gain for a, gain in own]
    for group in range(PLANE):
        mine[:, group * GROUP : (group + 1) * GROUP] = scaled[group]
    factor = lax.rsqrt(reduced([a * a for a, _ in own]) / width + epsilon)
    logits = []
    for user in range(2):
        norm = reduced([o[user] * o[user] for o in other])
        product = reduced([s * (o[user] * o[2]) for s, o in zip(scaled, other)])
        logits.append(product * factor * lax.rsqrt(norm / width + epsilon) * (logit_scale / width))
    start = pl.multiple_of((2 * z + x) * piece, piece)
    vec[0] = (mine[:, pl.ds(start, piece)] * factor).astype(jnp.bfloat16)
    forward = jnp.where(u == 0, positives[0], positives[1])
    backward = jnp.where(positives[0] == u, 0, 1)
    partner = jnp.where(domain == 0, forward, backward)
    top = jnp.maximum(logits[0], logits[1])
    spread = jnp.log(jnp.exp(logits[0] - top) + jnp.exp(logits[1] - top)) + top
    loss[...] = spread - jnp.where(partner == 0, logits[0], logits[1])


def vmem():
    return pl.BlockSpec(memory_space=pltpu.VMEM)


def anywhere():
    return pl.BlockSpec(memory_space=pl.ANY)


def hbm():
    return pl.BlockSpec(memory_space=pltpu.HBM)


def smem():
    return pl.BlockSpec(memory_space=pltpu.SMEM)


def call(kernel, outs, in_specs, scratch, flops):
    return pl.pallas_call(
        kernel,
        out_shape=outs,
        in_specs=in_specs,
        out_specs=jax.tree.map(lambda _: vmem(), outs),
        scratch_shapes=scratch,
        compiler_params=pltpu.CompilerParams(vmem_limit_bytes=40 * 1024 * 1024),
        cost_estimate=pl.CostEstimate(flops=flops, bytes_accessed=2**21, transcendentals=0),
    )


def towers(history, qkv_weight, norm_gain, pool_gain, lengths, positives):
    events = history[0, 0]
    tokens, width = events.shape
    weight = qkv_weight[0]
    rows = weight.shape[0]
    f32, bf16 = jnp.float32, jnp.bfloat16
    shape = jax.ShapeDtypeStruct
    here = PLANE * PLANES

    def hop(a, target):
        pairs = [(i, target(i // PLANE) * PLANE + i % PLANE) for i in range(here) if target(i // PLANE) is not None]
        return lax.ppermute(a, ("seq", "dp"), pairs)

    def plane_hop(a, move):
        return lax.ppermute(a, ("seq", "dp"), [(i, i ^ move) for i in range(here)])

    def each(a):
        return [hop(a, lambda p: p ^ j) for j in range(1, PLANES)]

    wide = 3 * GROUP
    w_own, w_sent = call(
        pack_kernel, (shape((rows, wide), bf16),) * 2, [hbm()], [pltpu.SemaphoreType.DMA((6,))], 0
    )(weight)
    w_near = plane_hop(w_sent, 2)
    two_near = hop(w_near, lambda p: p ^ 2)
    corner = plane_hop(events, 3)
    across = plane_hop(call(gate_kernel, shape((tokens, width), bf16), [vmem()] + [anywhere()] * 1, [], 0)(events, w_sent), 1)
    two_own = hop(w_own, lambda p: p ^ 2)
    one_own = hop(w_own, lambda p: p ^ 1)
    near = plane_hop(call(gate_kernel, shape((tokens, width), bf16), [vmem()] + [anywhere()] * 1, [], 0)(events, one_own), 2)
    one_near = hop(call(gate_kernel, shape((rows, wide), bf16), [vmem()] + [anywhere()] * 1, [], 0)(w_near, one_own), lambda p: p ^ 1)
    far_near = hop(call(gate_kernel, shape((rows, wide), bf16), [vmem()] + [anywhere()] * 1, [], 0)(two_near, one_near), lambda p: p ^ 1)
    far_own = hop(call(gate_kernel, shape((rows, wide), bf16), [vmem()] + [anywhere()] * 1, [], 0)(two_own, one_near), lambda p: p ^ 1)

    normed, sums, raw_short = call(
        norm_kernel,
        (shape((2 * tokens, width), bf16), shape((1, GROUP), f32), shape((tokens, width), bf16)),
        [smem()] + [anywhere()] * 4 + [vmem()],
        [pltpu.VMEM((2, tokens, width), bf16), pltpu.SemaphoreType.DMA((3,))],
        2 * 3 * tokens * width,
    )(lengths, events, near, across, corner, norm_gain)
    partial, weights = call(
        partial_kernel,
        (shape((2 * tokens, wide), f32), shape((width, wide), bf16)),
        [vmem()] * 7,
        [],
        2 * 2 * tokens * 3 * GROUP * wide,
    )(normed, w_own, w_near, one_own, one_near, two_own, two_near)
    feats, message, last = call(
        project_kernel,
        (shape((2 * tokens, wide), bf16), shape((MESSAGE, HEAD_DIM), bf16), shape((GROUP, wide), bf16)),
        [vmem()] * 4,
        [],
        2 * 2 * tokens * GROUP * wide,
    )(normed, partial, far_own, far_near)
    short = call(
        short_kernel, shape((1, GROUP), f32), [vmem()] * 4, [], 2 * tokens * width * wide
    )(raw_short, weights, last, norm_gain)
    part = call(
        pool_kernel,
        shape((2 * here, 1, 2 * GROUP + HEAD_DIM), f32),
        [smem()] + [vmem()] * 7,
        [],
        2 * 9 * tokens * tokens * GROUP,
    )(lengths, *each(message), feats, sums, short, pool_gain)
    parts = lax.all_to_all(part, ("seq", "dp", "domain"), 0, 0, tiled=True)
    vec, loss = call(
        loss_kernel,
        (shape((1, 1, width // 8), bf16), shape((1, 1), f32)),
        [smem(), vmem()],
        [pltpu.VMEM((1, width), f32)],
        2**14,
    )(positives, parts)
    return vec, loss


def solution(mesh):
    placed = (
        P("domain", "dp", "seq", None),
        P("domain", "seq", None),
        P("domain", None),
        P("domain", None),
        P("domain", "dp"),
        P(),
    )
    small = mesh.shape["seq"] == 2 * PLANES and mesh.shape["dp"] == 2
    return jax.shard_map(
        towers if small else shards,
        mesh=mesh,
        in_specs=placed,
        out_specs=(P("domain", "dp", "seq"), P("domain", "dp")),
        check_vma=False,
    )
```

```python
import functools

import jax
import jax.numpy as jnp
from jax import lax
from jax.experimental import pallas as pl
from jax.experimental.pallas import tpu as pltpu
from jax.sharding import PartitionSpec as P

HEADS = 8
HEAD_DIM = 128


logit_scale = 20.0
epsilon = 1e-06
highest = lax.Precision.HIGHEST


def carried_in(part, axis, combine, identity):
    place = lax.axis_index(axis)
    gathered = jax.tree.map(lambda a: lax.all_gather(a, axis), part)
    state = jax.tree.map(lambda a, e: jnp.zeros_like(a) + jnp.asarray(e, a.dtype), part, identity)

    def one(hop, state):
        return combine(
            state, jax.tree.map(lambda a: lax.dynamic_index_in_dim(a, hop, 0, False), gathered)
        )

    return lax.fori_loop(0, place, one, state)


def partner_2(block, axis, stride):
    count = lax.axis_size(axis)
    route = []
    for low in range(count):
        high = low | 1 << stride
        if high != low and high < count:
            route += [(low, high), (high, low)]
    return lax.ppermute(block, axis, route)


def feature_map(values):
    return jax.nn.elu(values) + 1.0


def add_pair(earlier, later):
    return (earlier[0] + later[0], earlier[1] + later[1])


def shards(history, qkv_weight, norm_gain, pool_gain, lengths, positives):
    seq_count = lax.axis_size("seq")
    seq_place = lax.axis_index("seq")
    group_place = lax.axis_index("dp")
    domain_place = lax.axis_index("domain")
    events = history[0]
    users_dev, tokens_dev, width = events.shape
    row_count = users_dev * tokens_dev
    wide = events.astype(jnp.float32)
    normed = (
        wide * lax.rsqrt(jnp.mean(wide * wide, -1, keepdims=True) + epsilon) * norm_gain[0]
    ).astype(jnp.bfloat16)
    normed = normed.reshape(row_count, width)
    rows_here = qkv_weight[0]
    projected = jnp.dot(
        normed,
        lax.all_gather(rows_here, "seq", axis=0, tiled=True),
        preferred_element_type=jnp.float32,
    )
    query_raw = projected[:, :width]
    key_raw = projected[:, width : 2 * width]
    value_raw = projected[:, 2 * width :]
    positions = seq_place * tokens_dev + jnp.arange(tokens_dev)
    valid = positions[None, :] < lengths[0][:, None]
    shape_heads = (users_dev, tokens_dev, HEADS, HEAD_DIM)
    queries = feature_map(query_raw).astype(jnp.bfloat16).reshape(shape_heads)
    key_feats = (
        jnp.where(valid.reshape(row_count)[:, None], feature_map(key_raw), 0.0)
        .astype(jnp.bfloat16)
        .reshape(shape_heads)
    )
    val_feats = value_raw.astype(jnp.bfloat16).reshape(shape_heads)
    local_state = jnp.einsum(
        "uthc,uthd->uhcd", key_feats, val_feats, preferred_element_type=jnp.float32
    )
    local_total = jnp.sum(key_feats.astype(jnp.float32), axis=1)
    state_before, total_before = carried_in(
        (local_state, local_total),
        "seq",
        add_pair,
        (jnp.zeros_like(local_state), jnp.zeros_like(local_total)),
    )
    causal = jnp.arange(tokens_dev)[:, None] >= jnp.arange(tokens_dev)[None, :]
    scores = jnp.einsum("uthc,ushc->uhts", queries, key_feats, preferred_element_type=jnp.float32)
    scores = jnp.where(causal, scores, 0.0)
    denominator = jnp.sum(scores, axis=-1) + jnp.einsum(
        "uthc,uhc->uht", queries.astype(jnp.float32), total_before, precision=highest
    )
    numerator = jnp.einsum(
        "uhts,ushc->uthc",
        scores.astype(jnp.bfloat16),
        val_feats,
        preferred_element_type=jnp.float32,
    )
    numerator = numerator + jnp.einsum(
        "uthc,uhcd->uthd",
        queries,
        state_before.astype(jnp.bfloat16),
        preferred_element_type=jnp.float32,
    )
    attended = numerator / jnp.transpose(denominator, (0, 2, 1))[..., None]
    attended = attended.reshape(users_dev, tokens_dev, width)
    partial_value = jnp.sum(jnp.where(valid[..., None], wide + attended, 0.0), axis=1)
    piece_width = width // seq_count
    gain_row = pool_gain[0]
    pooled = lax.psum(partial_value, "seq")
    factor = lax.rsqrt(jnp.mean(pooled * pooled, -1, keepdims=True) + epsilon)
    full_vec = (pooled * factor * gain_row).astype(jnp.bfloat16)
    out_vec = lax.dynamic_slice_in_dim(full_vec, seq_place * piece_width, piece_width, 1)
    group = lax.all_gather(full_vec, "dp", axis=0, tiled=True)
    other = partner_2(group, "domain", 0)
    logits = jnp.einsum("uc,vc->uv", full_vec, other, preferred_element_type=jnp.float32) * (
        logit_scale / width
    )
    users_all = other.shape[0]
    own_index = group_place * users_dev + jnp.arange(users_dev)
    targets = lax.dynamic_slice_in_dim(positives, group_place * users_dev, users_dev)
    forward_pair = targets[:, None] == jnp.arange(users_all)[None, :]
    backward_pair = positives[None, :] == own_index[:, None]
    partner = jnp.where(domain_place == 0, forward_pair, backward_pair)
    loss = jnp.log(jnp.sum(jnp.exp(logits), axis=-1)) - jnp.sum(
        jnp.where(partner, logits, 0.0), axis=-1
    )
    return (out_vec[None], loss[None])


PLANE = 4
PLANES = 4
GROUP = 256
DOT_T = (((0,), (0,)), ((), ()))
MESSAGE = GROUP + 16


def places():
    seq_place = lax.axis_index("seq")
    return lax.div(seq_place, 2), lax.rem(seq_place, 2), lax.axis_index("dp")


def head_sums(a):
    return [
        jnp.sum(a[:, h * HEAD_DIM : (h + 1) * HEAD_DIM], axis=1, keepdims=True)
        for h in range(GROUP // HEAD_DIM)
    ]


def by_head(columns):
    rows = columns[0].shape[0]
    return jnp.concatenate([jnp.broadcast_to(c, (rows, HEAD_DIM)) for c in columns], axis=1)


def split_two(a):
    high = a.astype(jnp.bfloat16)
    return high, (a - high.astype(jnp.float32)).astype(jnp.bfloat16)


def pack_kernel(weight, own, sent, sems):
    _, x, u = places()
    width = weight.shape[1] // 3
    copies = []
    for move, out in ((2, sent), (0, own)):
        group = jnp.bitwise_xor(2 * x + u, move)
        for part in range(3):
            start = pl.multiple_of(part * width + group * GROUP, GROUP)
            copies.append(
                pltpu.make_async_copy(
                    weight.at[:, pl.ds(start, GROUP)], out.at[:, pl.ds(part * GROUP, GROUP)], sems.at[len(copies)]
                )
            )
    for copy in copies:
        copy.start()
    for copy in copies:
        copy.wait()


def gate_kernel(values, *rest):
    rest[-1][...] = values[...]


def normalise(values, gain):
    wide = values.astype(jnp.float32)
    scale = lax.rsqrt(jnp.mean(wide * wide, axis=1, keepdims=True) + epsilon)
    return (wide * scale * gain).astype(jnp.bfloat16)


def features(out):
    raw = out[:, : 2 * GROUP]
    low = jnp.where(raw > 0.0, raw + 1.0, jnp.exp(jnp.minimum(raw, 0.0))).astype(jnp.bfloat16)
    return low[:, :GROUP], low[:, GROUP:], out[:, 2 * GROUP :].astype(jnp.bfloat16)


def place_rows(dest, start, x, here, there):
    rows = here.shape[0]
    for place, values in ((x, here), (1 - x, there)):
        dest[pl.ds(pl.multiple_of(start + place * rows, rows), rows), :] = values


def choose(pick, first, second, dest):
    @pl.when(pick)
    def _():
        dest[...] = first[...]

    @pl.when(jnp.logical_not(pick))
    def _():
        dest[...] = second[...]


def project(raw, gain, weights, feats, at):
    _, x, u = places()
    tokens = raw.shape[0]
    query, key, value = features(
        jnp.dot(normalise(raw[...], gain[...]), weights[...], preferred_element_type=jnp.float32)
    )
    rows = pl.ds(at, tokens)
    feats[rows, :GROUP] = query
    feats[rows, GROUP : 2 * GROUP] = key
    feats[rows, 2 * GROUP :] = value
    columns = pl.ds(pl.multiple_of((2 * x + u) * GROUP, GROUP), GROUP)
    return jnp.sum(raw[:, columns].astype(jnp.float32), axis=0, keepdims=True)


def first_kernel(lengths, own, across, gain, *refs):
    feats, sums, weights, raw = refs[2 * PLANES :]
    z, x, _ = places()
    for j in range(PLANES):
        start = pl.multiple_of(jnp.bitwise_xor(z, j) * GROUP, GROUP)
        place_rows(weights, start, x, refs[2 * j][...], refs[2 * j + 1][...])
    choose(lengths[0, 0] > own.shape[0], own, across, raw)
    sums[...] = project(raw, gain, weights, feats, 0)


def second_kernel(lengths, near, corner, gain, weights, first, first_sums, feats, message, sums, raw):
    tokens = near.shape[0]
    _, x, _ = places()
    choose(lengths[0, 0] > tokens, near, corner, raw)
    feats[pl.ds(pl.multiple_of(x * tokens, tokens), tokens), :] = first[...]
    sums[...] = first_sums[...] + project(raw, gain, weights, feats, pl.multiple_of((1 - x) * tokens, tokens))
    total = jnp.sum(feats[:, GROUP : 2 * GROUP].astype(jnp.float32), axis=0, keepdims=True)
    high, low = split_two(total)
    for h in range(GROUP // HEAD_DIM):
        at = h * HEAD_DIM
        key = feats[:, GROUP + at : GROUP + at + HEAD_DIM]
        value = feats[:, 2 * GROUP + at : 2 * GROUP + at + HEAD_DIM]
        state = lax.dot_general(key, value, DOT_T, preferred_element_type=jnp.float32)
        message[at : at + HEAD_DIM, :] = state.astype(jnp.bfloat16)
    total_rows = [high[:, :HEAD_DIM], high[:, HEAD_DIM:], low[:, :HEAD_DIM], low[:, HEAD_DIM:]]
    message[GROUP:, :] = jnp.concatenate(total_rows * 4, axis=0)


def triangle(tokens, upper):
    row = lax.broadcasted_iota(jnp.int32, (tokens, tokens), 0)
    col = lax.broadcasted_iota(jnp.int32, (tokens, tokens), 1)
    return (row <= col if upper else row >= col).astype(jnp.bfloat16)


def shares(query, key, carry):
    prefix = jnp.dot(triangle(key.shape[0], False), key, preferred_element_type=jnp.float32) + carry
    wide = query.astype(jnp.float32)
    return wide / by_head(head_sums(wide * prefix)), prefix[key.shape[0] - 1 :, :]


def suffix(share):
    upper = triangle(share.shape[0], True)
    high, low = split_two(share)
    return jnp.dot(upper, high, preferred_element_type=jnp.float32) + jnp.dot(
        upper, low, preferred_element_type=jnp.float32
    )


def weighted(key, value, after):
    weight = by_head(head_sums(key.astype(jnp.float32) * after))
    return jnp.sum(weight * value.astype(jnp.float32), axis=0, keepdims=True)


def short_kernel(lengths, own, near, across, corner, weights, gain, out, raw):
    tokens = own.shape[0]
    z, x, u = places()
    out[...] = jnp.zeros(out.shape, jnp.float32)

    @pl.when(z == 0)
    def _():
        own_long = lengths[0, 0] > tokens

        @pl.when(x == 0)
        def _():
            choose(own_long, across, own, raw)

        @pl.when(x != 0)
        def _():
            choose(own_long, corner, near, raw)

        wide = jnp.dot(normalise(raw[...], gain[...]), weights[...], preferred_element_type=jnp.float32)
        query, key, value = features(wide)
        share, _ = shares(query, key, jnp.zeros((1, GROUP), jnp.float32))
        columns = pl.ds(pl.multiple_of((2 * x + u) * GROUP, GROUP), GROUP)
        total = jnp.sum(raw[:, columns].astype(jnp.float32), axis=0, keepdims=True)
        out[...] = total + weighted(key, value, suffix(share))


def pool_kernel(lengths, state_3, state_2, state_1, feats, sums, short, gain, part):
    tokens = feats.shape[0] // 2
    z, x, u = places()
    long_u = jnp.where(lengths[0, 0] > tokens, u, 1 - u)
    states = [(jnp.bitwise_xor(z, j) < z, ref) for j, ref in enumerate((state_1, state_2, state_3), 1)]
    before = jnp.zeros((1, GROUP), jnp.float32)
    for earlier, ref in states:
        rows = ref[GROUP : GROUP + 16, :].astype(jnp.float32)
        total = jnp.concatenate([rows[0:1] + rows[2:3], rows[1:2] + rows[3:4]], axis=1)
        before = before + jnp.where(earlier, total, 0.0)

    def block(slot):
        at = pl.ds(slot * tokens, tokens)
        return feats[at, :GROUP], feats[at, GROUP : 2 * GROUP], feats[at, 2 * GROUP :]

    query_one, key_one, value_one = block(0)
    query_two, key_two, value_two = block(1)
    share_one, carry = shares(query_one, key_one, before)
    share_two, _ = shares(query_two, key_two, carry)
    after_two = suffix(share_two)
    after_one = suffix(share_one) + after_two[0:1, :]
    long_row = weighted(key_one, value_one, after_one) + weighted(key_two, value_two, after_two) + sums[...]
    weight = after_one[0:1, :]
    for earlier, ref in states:
        high, low = split_two(jnp.where(earlier, weight, 0.0))
        products = []
        for h in range(GROUP // HEAD_DIM):
            at = h * HEAD_DIM
            both = jnp.concatenate([high[:, at : at + HEAD_DIM]] * 8 + [low[:, at : at + HEAD_DIM]] * 8, axis=0)
            out = jnp.dot(both, ref[at : at + HEAD_DIM, :], preferred_element_type=jnp.float32)
            products.append(out[0:1] + out[8:9])
        long_row = long_row + jnp.concatenate(products, axis=1)

    short_row = short[...]
    first = jnp.where(long_u == 0, long_row, short_row)
    second = jnp.where(long_u == 0, short_row, long_row)
    own_gain = gain[:, pl.ds(pl.multiple_of((2 * x + u) * GROUP, GROUP), GROUP)]
    half = jnp.where(lax.rem(z, 2) == 0, own_gain[:, :HEAD_DIM], own_gain[:, HEAD_DIM:])
    part[...] = jnp.broadcast_to(jnp.concatenate([first, second, half], axis=1)[None], part.shape)


def loss_kernel(positives, parts, vec, loss, mine):
    z, x, u = places()
    domain = lax.axis_index("domain")
    width = mine.shape[1]
    piece = vec.shape[2]

    def collect(place):
        groups = []
        for group in range(PLANE):
            at = [parts[2 * (PLANE * plane + group) + place] for plane in range(PLANES)]
            total = (at[0][:, : 2 * GROUP] + at[1][:, : 2 * GROUP]) + (at[2][:, : 2 * GROUP] + at[3][:, : 2 * GROUP])
            gain = jnp.concatenate([at[0][:, 2 * GROUP :], at[1][:, 2 * GROUP :]], axis=1)
            groups.append((total[:, :GROUP], total[:, GROUP:], gain))
        return groups

    def reduced(terms):
        total = (terms[0] + terms[1]) + (terms[2] + terms[3])
        return jnp.sum(total, axis=1, keepdims=True)

    own = [(jnp.where(u == 0, a, b), gain) for a, b, gain in collect(domain)]
    other = collect(1 - domain)
    scaled = [a * gain for a, gain in own]
    for group in range(PLANE):
        mine[:, group * GROUP : (group + 1) * GROUP] = scaled[group]
    factor = lax.rsqrt(reduced([a * a for a, _ in own]) / width + epsilon)
    logits = []
    for user in range(2):
        norm = reduced([o[user] * o[user] for o in other])
        product = reduced([s * (o[user] * o[2]) for s, o in zip(scaled, other)])
        logits.append(product * factor * lax.rsqrt(norm / width + epsilon) * (logit_scale / width))
    start = pl.multiple_of((2 * z + x) * piece, piece)
    vec[0] = (mine[:, pl.ds(start, piece)] * factor).astype(jnp.bfloat16)
    forward = jnp.where(u == 0, positives[0], positives[1])
    backward = jnp.where(positives[0] == u, 0, 1)
    partner = jnp.where(domain == 0, forward, backward)
    top = jnp.maximum(logits[0], logits[1])
    spread = jnp.log(jnp.exp(logits[0] - top) + jnp.exp(logits[1] - top)) + top
    loss[...] = spread - jnp.where(partner == 0, logits[0], logits[1])


def vmem():
    return pl.BlockSpec(memory_space=pltpu.VMEM)


def anywhere():
    return pl.BlockSpec(memory_space=pl.ANY)


def hbm():
    return pl.BlockSpec(memory_space=pltpu.HBM)


def smem():
    return pl.BlockSpec(memory_space=pltpu.SMEM)


def call(kernel, outs, in_specs, scratch, flops):
    return pl.pallas_call(
        kernel,
        out_shape=outs,
        in_specs=in_specs,
        out_specs=jax.tree.map(lambda _: vmem(), outs),
        scratch_shapes=scratch,
        compiler_params=pltpu.CompilerParams(vmem_limit_bytes=40 * 1024 * 1024),
        cost_estimate=pl.CostEstimate(flops=flops, bytes_accessed=2**21, transcendentals=0),
    )


def towers(history, qkv_weight, norm_gain, pool_gain, lengths, positives):
    events = history[0, 0]
    tokens, width = events.shape
    weight = qkv_weight[0]
    rows = weight.shape[0]
    f32, bf16 = jnp.float32, jnp.bfloat16
    shape = jax.ShapeDtypeStruct
    here = PLANE * PLANES

    def hop(a, target):
        pairs = [(i, target(i // PLANE) * PLANE + i % PLANE) for i in range(here) if target(i // PLANE) is not None]
        return lax.ppermute(a, ("seq", "dp"), pairs)

    def plane_hop(a, move):
        return lax.ppermute(a, ("seq", "dp"), [(i, i ^ move) for i in range(here)])

    def each(a):
        return [hop(a, lambda p: p ^ j) for j in range(1, PLANES)]

    wide = 3 * GROUP
    w_own, w_sent = call(
        pack_kernel, (shape((rows, wide), bf16),) * 2, [hbm()], [pltpu.SemaphoreType.DMA((6,))], 0
    )(weight)
    near = plane_hop(events, 2)
    across = plane_hop(events, 1)
    w_near = plane_hop(w_sent, 2)
    two_own = hop(call(gate_kernel, shape((rows, wide), bf16), [vmem()] + [anywhere()] * 1, [], 0)(w_own, w_sent), lambda p: p ^ 2)
    two_near = hop(w_near, lambda p: p ^ 2)
    one_own = hop(w_own, lambda p: p ^ 1)
    one_near = hop(call(gate_kernel, shape((rows, wide), bf16), [vmem()] + [anywhere()] * 1, [], 0)(w_near, one_own), lambda p: p ^ 1)
    far_own = hop(call(gate_kernel, shape((rows, wide), bf16), [vmem()] + [anywhere()] * 1, [], 0)(two_own, one_near), lambda p: p ^ 1)
    far_near = hop(call(gate_kernel, shape((rows, wide), bf16), [vmem()] + [anywhere()] * 1, [], 0)(two_near, one_near), lambda p: p ^ 1)
    corner = plane_hop(call(gate_kernel, shape((tokens, width), bf16), [vmem()] + [anywhere()] * 2, [], 0)(events, one_own, w_near), 3)

    first, first_sums, weights = call(
        first_kernel,
        (shape((tokens, wide), bf16), shape((1, GROUP), f32), shape((width, wide), bf16)),
        [smem()] + [vmem()] * (3 + 2 * PLANES),
        [pltpu.VMEM((tokens, width), bf16)],
        2 * tokens * width * wide,
    )(lengths, events, across, norm_gain, w_own, w_near, one_own, one_near, two_own, two_near, far_own, far_near)
    feats, message, sums = call(
        second_kernel,
        (shape((2 * tokens, wide), bf16), shape((MESSAGE, HEAD_DIM), bf16), shape((1, GROUP), f32)),
        [smem()] + [vmem()] * 6,
        [pltpu.VMEM((tokens, width), bf16)],
        2 * tokens * width * wide,
    )(lengths, near, corner, norm_gain, weights, first, first_sums)
    short = call(
        short_kernel,
        shape((1, GROUP), f32),
        [smem()] + [vmem()] * 6,
        [pltpu.VMEM((tokens, width), bf16)],
        2 * tokens * width * wide,
    )(lengths, events, near, across, corner, weights, norm_gain)
    part = call(
        pool_kernel,
        shape((2 * here, 1, 2 * GROUP + HEAD_DIM), f32),
        [smem()] + [vmem()] * 7,
        [],
        2 * 9 * tokens * tokens * GROUP,
    )(lengths, *each(message)[::-1], feats, sums, short, pool_gain)
    parts = lax.all_to_all(part, ("seq", "dp", "domain"), 0, 0, tiled=True)
    vec, loss = call(
        loss_kernel,
        (shape((1, 1, width // 8), bf16), shape((1, 1), f32)),
        [smem(), vmem()],
        [pltpu.VMEM((1, width), f32)],
        2**14,
    )(positives, parts)
    return vec, loss


def solution(mesh):
    placed = (
        P("domain", "dp", "seq", None),
        P("domain", "seq", None),
        P("domain", None),
        P("domain", None),
        P("domain", "dp"),
        P(),
    )
    small = mesh.shape["seq"] == 2 * PLANES and mesh.shape["dp"] == 2
    return jax.shard_map(
        towers if small else shards,
        mesh=mesh,
        in_specs=placed,
        out_specs=(P("domain", "dp", "seq"), P("domain", "dp")),
        check_vma=False,
    )
```

```python
import functools

import jax
import jax.numpy as jnp
from jax import lax
from jax.experimental import pallas as pl
from jax.experimental.pallas import tpu as pltpu
from jax.sharding import PartitionSpec as P

HEADS = 8
HEAD_DIM = 128


logit_scale = 20.0
epsilon = 1e-06
highest = lax.Precision.HIGHEST


def carried_in(part, axis, combine, identity):
    place = lax.axis_index(axis)
    gathered = jax.tree.map(lambda a: lax.all_gather(a, axis), part)
    state = jax.tree.map(lambda a, e: jnp.zeros_like(a) + jnp.asarray(e, a.dtype), part, identity)

    def one(hop, state):
        return combine(
            state, jax.tree.map(lambda a: lax.dynamic_index_in_dim(a, hop, 0, False), gathered)
        )

    return lax.fori_loop(0, place, one, state)


def partner_2(block, axis, stride):
    count = lax.axis_size(axis)
    route = []
    for low in range(count):
        high = low | 1 << stride
        if high != low and high < count:
            route += [(low, high), (high, low)]
    return lax.ppermute(block, axis, route)


def feature_map(values):
    return jax.nn.elu(values) + 1.0


def add_pair(earlier, later):
    return (earlier[0] + later[0], earlier[1] + later[1])


def shards(history, qkv_weight, norm_gain, pool_gain, lengths, positives):
    seq_count = lax.axis_size("seq")
    seq_place = lax.axis_index("seq")
    group_place = lax.axis_index("dp")
    domain_place = lax.axis_index("domain")
    events = history[0]
    users_dev, tokens_dev, width = events.shape
    row_count = users_dev * tokens_dev
    wide = events.astype(jnp.float32)
    normed = (
        wide * lax.rsqrt(jnp.mean(wide * wide, -1, keepdims=True) + epsilon) * norm_gain[0]
    ).astype(jnp.bfloat16)
    normed = normed.reshape(row_count, width)
    rows_here = qkv_weight[0]
    projected = jnp.dot(
        normed,
        lax.all_gather(rows_here, "seq", axis=0, tiled=True),
        preferred_element_type=jnp.float32,
    )
    query_raw = projected[:, :width]
    key_raw = projected[:, width : 2 * width]
    value_raw = projected[:, 2 * width :]
    positions = seq_place * tokens_dev + jnp.arange(tokens_dev)
    valid = positions[None, :] < lengths[0][:, None]
    shape_heads = (users_dev, tokens_dev, HEADS, HEAD_DIM)
    queries = feature_map(query_raw).astype(jnp.bfloat16).reshape(shape_heads)
    key_feats = (
        jnp.where(valid.reshape(row_count)[:, None], feature_map(key_raw), 0.0)
        .astype(jnp.bfloat16)
        .reshape(shape_heads)
    )
    val_feats = value_raw.astype(jnp.bfloat16).reshape(shape_heads)
    local_state = jnp.einsum(
        "uthc,uthd->uhcd", key_feats, val_feats, preferred_element_type=jnp.float32
    )
    local_total = jnp.sum(key_feats.astype(jnp.float32), axis=1)
    state_before, total_before = carried_in(
        (local_state, local_total),
        "seq",
        add_pair,
        (jnp.zeros_like(local_state), jnp.zeros_like(local_total)),
    )
    causal = jnp.arange(tokens_dev)[:, None] >= jnp.arange(tokens_dev)[None, :]
    scores = jnp.einsum("uthc,ushc->uhts", queries, key_feats, preferred_element_type=jnp.float32)
    scores = jnp.where(causal, scores, 0.0)
    denominator = jnp.sum(scores, axis=-1) + jnp.einsum(
        "uthc,uhc->uht", queries.astype(jnp.float32), total_before, precision=highest
    )
    numerator = jnp.einsum(
        "uhts,ushc->uthc",
        scores.astype(jnp.bfloat16),
        val_feats,
        preferred_element_type=jnp.float32,
    )
    numerator = numerator + jnp.einsum(
        "uthc,uhcd->uthd",
        queries,
        state_before.astype(jnp.bfloat16),
        preferred_element_type=jnp.float32,
    )
    attended = numerator / jnp.transpose(denominator, (0, 2, 1))[..., None]
    attended = attended.reshape(users_dev, tokens_dev, width)
    partial_value = jnp.sum(jnp.where(valid[..., None], wide + attended, 0.0), axis=1)
    piece_width = width // seq_count
    gain_row = pool_gain[0]
    pooled = lax.psum(partial_value, "seq")
    factor = lax.rsqrt(jnp.mean(pooled * pooled, -1, keepdims=True) + epsilon)
    full_vec = (pooled * factor * gain_row).astype(jnp.bfloat16)
    out_vec = lax.dynamic_slice_in_dim(full_vec, seq_place * piece_width, piece_width, 1)
    group = lax.all_gather(full_vec, "dp", axis=0, tiled=True)
    other = partner_2(group, "domain", 0)
    logits = jnp.einsum("uc,vc->uv", full_vec, other, preferred_element_type=jnp.float32) * (
        logit_scale / width
    )
    users_all = other.shape[0]
    own_index = group_place * users_dev + jnp.arange(users_dev)
    targets = lax.dynamic_slice_in_dim(positives, group_place * users_dev, users_dev)
    forward_pair = targets[:, None] == jnp.arange(users_all)[None, :]
    backward_pair = positives[None, :] == own_index[:, None]
    partner = jnp.where(domain_place == 0, forward_pair, backward_pair)
    loss = jnp.log(jnp.sum(jnp.exp(logits), axis=-1)) - jnp.sum(
        jnp.where(partner, logits, 0.0), axis=-1
    )
    return (out_vec[None], loss[None])


PLANE = 4
PLANES = 4
GROUP = 256
DOT_T = (((0,), (0,)), ((), ()))
DOT_NT = (((1,), (1,)), ((), ()))
MESSAGE = GROUP + 16


def places():
    seq_place = lax.axis_index("seq")
    return lax.div(seq_place, 2), lax.rem(seq_place, 2), lax.axis_index("dp")


def head_sums(a):
    return [
        jnp.sum(a[:, h * HEAD_DIM : (h + 1) * HEAD_DIM], axis=1, keepdims=True)
        for h in range(GROUP // HEAD_DIM)
    ]


def by_head(columns):
    rows = columns[0].shape[0]
    return jnp.concatenate([jnp.broadcast_to(c, (rows, HEAD_DIM)) for c in columns], axis=1)


def split_two(a):
    high = a.astype(jnp.bfloat16)
    return high, (a - high.astype(jnp.float32)).astype(jnp.bfloat16)


def pack_kernel(weight, own, sent, sems):
    _, x, u = places()
    width = weight.shape[1] // 3
    copies = []
    for move, out in ((2, sent), (0, own)):
        group = jnp.bitwise_xor(2 * x + u, move)
        for part in range(3):
            start = pl.multiple_of(part * width + group * GROUP, GROUP)
            copies.append(
                pltpu.make_async_copy(
                    weight.at[:, pl.ds(start, GROUP)], out.at[:, pl.ds(part * GROUP, GROUP)], sems.at[len(copies)]
                )
            )
    for copy in copies:
        copy.start()
    for copy in copies:
        copy.wait()


def gate_kernel(values, *rest):
    rest[-1][...] = values[...]


def normalise(values, gain):
    wide = values.astype(jnp.float32)
    scale = lax.rsqrt(jnp.mean(wide * wide, axis=1, keepdims=True) + epsilon)
    return (wide * scale * gain).astype(jnp.bfloat16)


def features(out):
    raw = out[:, : 2 * GROUP]
    low = jnp.where(raw > 0.0, raw + 1.0, jnp.exp(jnp.minimum(raw, 0.0))).astype(jnp.bfloat16)
    return low[:, :GROUP], low[:, GROUP:], out[:, 2 * GROUP :].astype(jnp.bfloat16)


def place_rows(dest, start, x, here, there):
    rows = here.shape[0]
    for place, values in ((x, here), (1 - x, there)):
        dest[pl.ds(pl.multiple_of(start + place * rows, rows), rows), :] = values


def choose(pick, first, second, dest):
    @pl.when(pick)
    def _():
        dest[...] = first[...]

    @pl.when(jnp.logical_not(pick))
    def _():
        dest[...] = second[...]


def project(raw, gain, weights, feats, at):
    _, x, u = places()
    tokens = raw.shape[0]
    query, key, value = features(
        jnp.dot(normalise(raw[...], gain[...]), weights[...], preferred_element_type=jnp.float32)
    )
    rows = pl.ds(at, tokens)
    feats[rows, :GROUP] = query
    feats[rows, GROUP : 2 * GROUP] = key
    feats[rows, 2 * GROUP :] = value
    columns = pl.ds(pl.multiple_of((2 * x + u) * GROUP, GROUP), GROUP)
    return jnp.sum(raw[:, columns].astype(jnp.float32), axis=0, keepdims=True)


def first_kernel(lengths, own, across, gain, *refs):
    feats, sums, weights, raw = refs[2 * PLANES :]
    z, x, _ = places()
    for j in range(PLANES):
        start = pl.multiple_of(jnp.bitwise_xor(z, j) * GROUP, GROUP)
        place_rows(weights, start, x, refs[2 * j][...], refs[2 * j + 1][...])
    choose(lengths[0, 0] > own.shape[0], own, across, raw)
    sums[...] = project(raw, gain, weights, feats, 0)


def second_kernel(lengths, near, corner, gain, weights, first, first_sums, feats, message, sums, raw):
    tokens = near.shape[0]
    _, x, _ = places()
    choose(lengths[0, 0] > tokens, near, corner, raw)
    feats[pl.ds(pl.multiple_of(x * tokens, tokens), tokens), :] = first[...]
    sums[...] = first_sums[...] + project(raw, gain, weights, feats, pl.multiple_of((1 - x) * tokens, tokens))
    total = jnp.sum(feats[:, GROUP : 2 * GROUP].astype(jnp.float32), axis=0, keepdims=True)
    high, low = split_two(total)
    for h in range(GROUP // HEAD_DIM):
        at = h * HEAD_DIM
        key = feats[:, GROUP + at : GROUP + at + HEAD_DIM]
        value = feats[:, 2 * GROUP + at : 2 * GROUP + at + HEAD_DIM]
        state = lax.dot_general(key, value, DOT_T, preferred_element_type=jnp.float32)
        message[at : at + HEAD_DIM, :] = state.astype(jnp.bfloat16)
    total_rows = [high[:, :HEAD_DIM], high[:, HEAD_DIM:], low[:, :HEAD_DIM], low[:, HEAD_DIM:]]
    message[GROUP:, :] = jnp.concatenate(total_rows * 4, axis=0)


def triangle(tokens, upper):
    row = lax.broadcasted_iota(jnp.int32, (tokens, tokens), 0)
    col = lax.broadcasted_iota(jnp.int32, (tokens, tokens), 1)
    return (row <= col if upper else row >= col).astype(jnp.bfloat16)


def shares(query, key, carry):
    prefix = jnp.dot(triangle(key.shape[0], False), key, preferred_element_type=jnp.float32) + carry
    wide = query.astype(jnp.float32)
    return wide / by_head(head_sums(wide * prefix)), prefix[key.shape[0] - 1 :, :]


def suffix(share):
    upper = triangle(share.shape[0], True)
    high, low = split_two(share)
    return jnp.dot(upper, high, preferred_element_type=jnp.float32) + jnp.dot(
        upper, low, preferred_element_type=jnp.float32
    )


def weighted(key, value, after):
    weight = by_head(head_sums(key.astype(jnp.float32) * after))
    return jnp.sum(weight * value.astype(jnp.float32), axis=0, keepdims=True)


def local_kernel(feats, local):
    tokens = feats.shape[0] // 2
    lower = triangle(tokens, False)
    carry = jnp.zeros((1, GROUP), jnp.float32)
    for slot in range(2):
        at = pl.ds(slot * tokens, tokens)
        prefix = jnp.dot(lower, feats[at, GROUP : 2 * GROUP], preferred_element_type=jnp.float32) + carry
        local[at, :] = by_head(head_sums(feats[at, :GROUP].astype(jnp.float32) * prefix))
        carry = prefix[tokens - 1 :, :]


def short_kernel(lengths, own, near, across, corner, weights, gain, out, raw):
    tokens = own.shape[0]
    z, x, u = places()
    out[...] = jnp.zeros(out.shape, jnp.float32)

    @pl.when(z == 0)
    def _():
        own_long = lengths[0, 0] > tokens

        @pl.when(x == 0)
        def _():
            choose(own_long, across, own, raw)

        @pl.when(x != 0)
        def _():
            choose(own_long, corner, near, raw)

        wide = jnp.dot(normalise(raw[...], gain[...]), weights[...], preferred_element_type=jnp.float32)
        query, key, value = features(wide)
        share, _ = shares(query, key, jnp.zeros((1, GROUP), jnp.float32))
        columns = pl.ds(pl.multiple_of((2 * x + u) * GROUP, GROUP), GROUP)
        total = jnp.sum(raw[:, columns].astype(jnp.float32), axis=0, keepdims=True)
        out[...] = total + weighted(key, value, suffix(share))


def pool_kernel(lengths, state_3, state_2, state_1, feats, local, sums, short, gain, part):
    tokens = feats.shape[0] // 2
    z, x, u = places()
    long_u = jnp.where(lengths[0, 0] > tokens, u, 1 - u)
    states = [(jnp.bitwise_xor(z, j) < z, ref) for j, ref in enumerate((state_1, state_2, state_3), 1)]
    before = jnp.zeros((1, GROUP), jnp.float32)
    for earlier, ref in states:
        rows = ref[GROUP : GROUP + 16, :].astype(jnp.float32)
        total = jnp.concatenate([rows[0:1] + rows[2:3], rows[1:2] + rows[3:4]], axis=1)
        before = before + jnp.where(earlier, total, 0.0)

    def block(slot):
        at = pl.ds(slot * tokens, tokens)
        return feats[at, :GROUP], feats[at, GROUP : 2 * GROUP], feats[at, 2 * GROUP :]

    query_one, key_one, value_one = block(0)
    query_two, key_two, value_two = block(1)
    row = lax.broadcasted_iota(jnp.int32, (GROUP, GROUP), 0) < HEAD_DIM
    col = lax.broadcasted_iota(jnp.int32, (GROUP, GROUP), 1) < HEAD_DIM
    same_head = jnp.where(row == col, jnp.broadcast_to(before, (GROUP, GROUP)), 0.0)
    high, low = split_two(same_head)

    def share(query, at):
        total = local[at : at + tokens, :]
        for table in (high, low):
            total = total + lax.dot_general(query, table, DOT_NT, preferred_element_type=jnp.float32)
        return query.astype(jnp.float32) / total

    share_one = share(query_one, 0)
    share_two = share(query_two, tokens)
    after_two = suffix(share_two)
    after_one = suffix(share_one) + after_two[0:1, :]
    long_row = weighted(key_one, value_one, after_one) + weighted(key_two, value_two, after_two) + sums[...]
    weight = after_one[0:1, :]
    for earlier, ref in states:
        high, low = split_two(jnp.where(earlier, weight, 0.0))
        products = []
        for h in range(GROUP // HEAD_DIM):
            at = h * HEAD_DIM
            both = jnp.concatenate([high[:, at : at + HEAD_DIM]] * 8 + [low[:, at : at + HEAD_DIM]] * 8, axis=0)
            out = jnp.dot(both, ref[at : at + HEAD_DIM, :], preferred_element_type=jnp.float32)
            products.append(out[0:1] + out[8:9])
        long_row = long_row + jnp.concatenate(products, axis=1)

    short_row = short[...]
    first = jnp.where(long_u == 0, long_row, short_row)
    second = jnp.where(long_u == 0, short_row, long_row)
    own_gain = gain[:, pl.ds(pl.multiple_of((2 * x + u) * GROUP, GROUP), GROUP)]
    half = jnp.where(lax.rem(z, 2) == 0, own_gain[:, :HEAD_DIM], own_gain[:, HEAD_DIM:])
    part[...] = jnp.broadcast_to(jnp.concatenate([first, second, half], axis=1)[None], part.shape)


def loss_kernel(positives, parts, vec, loss, mine):
    z, x, u = places()
    domain = lax.axis_index("domain")
    width = mine.shape[1]
    piece = vec.shape[2]

    def collect(place):
        groups = []
        for group in range(PLANE):
            at = [parts[2 * (PLANE * plane + group) + place] for plane in range(PLANES)]
            total = (at[0][:, : 2 * GROUP] + at[1][:, : 2 * GROUP]) + (at[2][:, : 2 * GROUP] + at[3][:, : 2 * GROUP])
            gain = jnp.concatenate([at[0][:, 2 * GROUP :], at[1][:, 2 * GROUP :]], axis=1)
            groups.append((total[:, :GROUP], total[:, GROUP:], gain))
        return groups

    def reduced(terms):
        total = (terms[0] + terms[1]) + (terms[2] + terms[3])
        return jnp.sum(total, axis=1, keepdims=True)

    own = [(jnp.where(u == 0, a, b), gain) for a, b, gain in collect(domain)]
    other = collect(1 - domain)
    scaled = [a * gain for a, gain in own]
    for group in range(PLANE):
        mine[:, group * GROUP : (group + 1) * GROUP] = scaled[group]
    factor = lax.rsqrt(reduced([a * a for a, _ in own]) / width + epsilon)
    logits = []
    for user in range(2):
        norm = reduced([o[user] * o[user] for o in other])
        product = reduced([s * (o[user] * o[2]) for s, o in zip(scaled, other)])
        logits.append(product * factor * lax.rsqrt(norm / width + epsilon) * (logit_scale / width))
    start = pl.multiple_of((2 * z + x) * piece, piece)
    vec[0] = (mine[:, pl.ds(start, piece)] * factor).astype(jnp.bfloat16)
    forward = jnp.where(u == 0, positives[0], positives[1])
    backward = jnp.where(positives[0] == u, 0, 1)
    partner = jnp.where(domain == 0, forward, backward)
    top = jnp.maximum(logits[0], logits[1])
    spread = jnp.log(jnp.exp(logits[0] - top) + jnp.exp(logits[1] - top)) + top
    loss[...] = spread - jnp.where(partner == 0, logits[0], logits[1])


def vmem():
    return pl.BlockSpec(memory_space=pltpu.VMEM)


def anywhere():
    return pl.BlockSpec(memory_space=pl.ANY)


def hbm():
    return pl.BlockSpec(memory_space=pltpu.HBM)


def smem():
    return pl.BlockSpec(memory_space=pltpu.SMEM)


def call(kernel, outs, in_specs, scratch, flops):
    return pl.pallas_call(
        kernel,
        out_shape=outs,
        in_specs=in_specs,
        out_specs=jax.tree.map(lambda _: vmem(), outs),
        scratch_shapes=scratch,
        compiler_params=pltpu.CompilerParams(vmem_limit_bytes=40 * 1024 * 1024),
        cost_estimate=pl.CostEstimate(flops=flops, bytes_accessed=2**21, transcendentals=0),
    )


def towers(history, qkv_weight, norm_gain, pool_gain, lengths, positives):
    events = history[0, 0]
    tokens, width = events.shape
    weight = qkv_weight[0]
    rows = weight.shape[0]
    f32, bf16 = jnp.float32, jnp.bfloat16
    shape = jax.ShapeDtypeStruct
    here = PLANE * PLANES

    def hop(a, target):
        pairs = [(i, target(i // PLANE) * PLANE + i % PLANE) for i in range(here) if target(i // PLANE) is not None]
        return lax.ppermute(a, ("seq", "dp"), pairs)

    def plane_hop(a, move):
        return lax.ppermute(a, ("seq", "dp"), [(i, i ^ move) for i in range(here)])

    def each(a):
        return [hop(a, lambda p: p ^ j) for j in range(1, PLANES)]

    wide = 3 * GROUP
    w_own, w_sent = call(
        pack_kernel, (shape((rows, wide), bf16),) * 2, [hbm()], [pltpu.SemaphoreType.DMA((6,))], 0
    )(pltpu.with_memory_space_constraint(weight, pltpu.HBM))
    near = plane_hop(events, 2)
    across = plane_hop(events, 1)
    w_near = plane_hop(w_sent, 2)
    two_own = hop(call(gate_kernel, shape((rows, wide), bf16), [vmem()] + [anywhere()] * 1, [], 0)(w_own, w_sent), lambda p: p ^ 2)
    two_near = hop(w_near, lambda p: p ^ 2)
    one_own = hop(w_own, lambda p: p ^ 1)
    one_near = hop(call(gate_kernel, shape((rows, wide), bf16), [vmem()] + [anywhere()] * 1, [], 0)(w_near, one_own), lambda p: p ^ 1)
    far_own = hop(call(gate_kernel, shape((rows, wide), bf16), [vmem()] + [anywhere()] * 1, [], 0)(two_own, one_near), lambda p: p ^ 1)
    far_near = hop(call(gate_kernel, shape((rows, wide), bf16), [vmem()] + [anywhere()] * 1, [], 0)(two_near, one_near), lambda p: p ^ 1)
    corner = plane_hop(call(gate_kernel, shape((tokens, width), bf16), [vmem()] + [anywhere()] * 2, [], 0)(events, one_own, w_near), 3)

    first, first_sums, weights = call(
        first_kernel,
        (shape((tokens, wide), bf16), shape((1, GROUP), f32), shape((width, wide), bf16)),
        [smem()] + [vmem()] * (3 + 2 * PLANES),
        [pltpu.VMEM((tokens, width), bf16)],
        2 * tokens * width * wide,
    )(lengths, events, across, norm_gain, w_own, w_near, one_own, one_near, two_own, two_near, far_own, far_near)
    feats, message, sums = call(
        second_kernel,
        (shape((2 * tokens, wide), bf16), shape((MESSAGE, HEAD_DIM), bf16), shape((1, GROUP), f32)),
        [smem()] + [vmem()] * 6,
        [pltpu.VMEM((tokens, width), bf16)],
        2 * tokens * width * wide,
    )(lengths, near, corner, norm_gain, weights, first, first_sums)
    short = call(
        short_kernel,
        shape((1, GROUP), f32),
        [smem()] + [vmem()] * 6,
        [pltpu.VMEM((tokens, width), bf16)],
        2 * tokens * width * wide,
    )(lengths, events, near, across, corner, weights, norm_gain)
    local = call(
        local_kernel, shape((2 * tokens, GROUP), f32), [vmem()], [], 2 * 2 * tokens * tokens * GROUP
    )(feats)
    part = call(
        pool_kernel,
        shape((2 * here, 1, 2 * GROUP + HEAD_DIM), f32),
        [smem()] + [vmem()] * 8,
        [],
        2 * 9 * tokens * tokens * GROUP,
    )(lengths, *each(message)[::-1], feats, local, sums, short, pool_gain)
    parts = lax.all_to_all(part, ("seq", "dp", "domain"), 0, 0, tiled=True)
    vec, loss = call(
        loss_kernel,
        (shape((1, 1, width // 8), bf16), shape((1, 1), f32)),
        [smem(), vmem()],
        [pltpu.VMEM((1, width), f32)],
        2**14,
    )(positives, parts)
    return vec, loss


def solution(mesh):
    placed = (
        P("domain", "dp", "seq", None),
        P("domain", "seq", None),
        P("domain", None),
        P("domain", None),
        P("domain", "dp"),
        P(),
    )
    small = mesh.shape["seq"] == 2 * PLANES and mesh.shape["dp"] == 2
    return jax.shard_map(
        towers if small else shards,
        mesh=mesh,
        in_specs=placed,
        out_specs=(P("domain", "dp", "seq"), P("domain", "dp")),
        check_vma=False,
    )
```

```python
import functools

import jax
import jax.numpy as jnp
from jax import lax
from jax.experimental import pallas as pl
from jax.experimental.pallas import tpu as pltpu
from jax.sharding import PartitionSpec as P

HEADS = 8
HEAD_DIM = 128


logit_scale = 20.0
epsilon = 1e-06
highest = lax.Precision.HIGHEST


def carried_in(part, axis, combine, identity):
    place = lax.axis_index(axis)
    gathered = jax.tree.map(lambda a: lax.all_gather(a, axis), part)
    state = jax.tree.map(lambda a, e: jnp.zeros_like(a) + jnp.asarray(e, a.dtype), part, identity)

    def one(hop, state):
        return combine(
            state, jax.tree.map(lambda a: lax.dynamic_index_in_dim(a, hop, 0, False), gathered)
        )

    return lax.fori_loop(0, place, one, state)


def partner_2(block, axis, stride):
    count = lax.axis_size(axis)
    route = []
    for low in range(count):
        high = low | 1 << stride
        if high != low and high < count:
            route += [(low, high), (high, low)]
    return lax.ppermute(block, axis, route)


def feature_map(values):
    return jax.nn.elu(values) + 1.0


def add_pair(earlier, later):
    return (earlier[0] + later[0], earlier[1] + later[1])


def shards(history, qkv_weight, norm_gain, pool_gain, lengths, positives):
    seq_count = lax.axis_size("seq")
    seq_place = lax.axis_index("seq")
    group_place = lax.axis_index("dp")
    domain_place = lax.axis_index("domain")
    events = history[0]
    users_dev, tokens_dev, width = events.shape
    row_count = users_dev * tokens_dev
    wide = events.astype(jnp.float32)
    normed = (
        wide * lax.rsqrt(jnp.mean(wide * wide, -1, keepdims=True) + epsilon) * norm_gain[0]
    ).astype(jnp.bfloat16)
    normed = normed.reshape(row_count, width)
    rows_here = qkv_weight[0]
    projected = jnp.dot(
        normed,
        lax.all_gather(rows_here, "seq", axis=0, tiled=True),
        preferred_element_type=jnp.float32,
    )
    query_raw = projected[:, :width]
    key_raw = projected[:, width : 2 * width]
    value_raw = projected[:, 2 * width :]
    positions = seq_place * tokens_dev + jnp.arange(tokens_dev)
    valid = positions[None, :] < lengths[0][:, None]
    shape_heads = (users_dev, tokens_dev, HEADS, HEAD_DIM)
    queries = feature_map(query_raw).astype(jnp.bfloat16).reshape(shape_heads)
    key_feats = (
        jnp.where(valid.reshape(row_count)[:, None], feature_map(key_raw), 0.0)
        .astype(jnp.bfloat16)
        .reshape(shape_heads)
    )
    val_feats = value_raw.astype(jnp.bfloat16).reshape(shape_heads)
    local_state = jnp.einsum(
        "uthc,uthd->uhcd", key_feats, val_feats, preferred_element_type=jnp.float32
    )
    local_total = jnp.sum(key_feats.astype(jnp.float32), axis=1)
    state_before, total_before = carried_in(
        (local_state, local_total),
        "seq",
        add_pair,
        (jnp.zeros_like(local_state), jnp.zeros_like(local_total)),
    )
    causal = jnp.arange(tokens_dev)[:, None] >= jnp.arange(tokens_dev)[None, :]
    scores = jnp.einsum("uthc,ushc->uhts", queries, key_feats, preferred_element_type=jnp.float32)
    scores = jnp.where(causal, scores, 0.0)
    denominator = jnp.sum(scores, axis=-1) + jnp.einsum(
        "uthc,uhc->uht", queries.astype(jnp.float32), total_before, precision=highest
    )
    numerator = jnp.einsum(
        "uhts,ushc->uthc",
        scores.astype(jnp.bfloat16),
        val_feats,
        preferred_element_type=jnp.float32,
    )
    numerator = numerator + jnp.einsum(
        "uthc,uhcd->uthd",
        queries,
        state_before.astype(jnp.bfloat16),
        preferred_element_type=jnp.float32,
    )
    attended = numerator / jnp.transpose(denominator, (0, 2, 1))[..., None]
    attended = attended.reshape(users_dev, tokens_dev, width)
    partial_value = jnp.sum(jnp.where(valid[..., None], wide + attended, 0.0), axis=1)
    piece_width = width // seq_count
    gain_row = pool_gain[0]
    pooled = lax.psum(partial_value, "seq")
    factor = lax.rsqrt(jnp.mean(pooled * pooled, -1, keepdims=True) + epsilon)
    full_vec = (pooled * factor * gain_row).astype(jnp.bfloat16)
    out_vec = lax.dynamic_slice_in_dim(full_vec, seq_place * piece_width, piece_width, 1)
    group = lax.all_gather(full_vec, "dp", axis=0, tiled=True)
    other = partner_2(group, "domain", 0)
    logits = jnp.einsum("uc,vc->uv", full_vec, other, preferred_element_type=jnp.float32) * (
        logit_scale / width
    )
    users_all = other.shape[0]
    own_index = group_place * users_dev + jnp.arange(users_dev)
    targets = lax.dynamic_slice_in_dim(positives, group_place * users_dev, users_dev)
    forward_pair = targets[:, None] == jnp.arange(users_all)[None, :]
    backward_pair = positives[None, :] == own_index[:, None]
    partner = jnp.where(domain_place == 0, forward_pair, backward_pair)
    loss = jnp.log(jnp.sum(jnp.exp(logits), axis=-1)) - jnp.sum(
        jnp.where(partner, logits, 0.0), axis=-1
    )
    return (out_vec[None], loss[None])


PLANE = 4
PLANES = 4
GROUP = 256
DOT_T = (((0,), (0,)), ((), ()))
DOT_NT = (((1,), (1,)), ((), ()))
MESSAGE = GROUP + 16


def places():
    seq_place = lax.axis_index("seq")
    return lax.div(seq_place, 2), lax.rem(seq_place, 2), lax.axis_index("dp")


def head_sums(a):
    return [
        jnp.sum(a[:, h * HEAD_DIM : (h + 1) * HEAD_DIM], axis=1, keepdims=True)
        for h in range(GROUP // HEAD_DIM)
    ]


def by_head(columns):
    rows = columns[0].shape[0]
    return jnp.concatenate([jnp.broadcast_to(c, (rows, HEAD_DIM)) for c in columns], axis=1)


def split_two(a):
    high = a.astype(jnp.bfloat16)
    return high, (a - high.astype(jnp.float32)).astype(jnp.bfloat16)


def pack_kernel(weight, own, sent, sems):
    _, x, u = places()
    width = weight.shape[1] // 3
    copies = []
    for move, out in ((2, sent), (0, own)):
        group = jnp.bitwise_xor(2 * x + u, move)
        for part in range(3):
            start = pl.multiple_of(part * width + group * GROUP, GROUP)
            copies.append(
                pltpu.make_async_copy(
                    weight.at[:, pl.ds(start, GROUP)], out.at[:, pl.ds(part * GROUP, GROUP)], sems.at[len(copies)]
                )
            )
    for copy in copies:
        copy.start()
    for copy in copies:
        copy.wait()


def gate_kernel(values, *rest):
    rest[-1][...] = values[...]


def normalise(values, gain):
    wide = values.astype(jnp.float32)
    scale = lax.rsqrt(jnp.mean(wide * wide, axis=1, keepdims=True) + epsilon)
    return (wide * scale * gain).astype(jnp.bfloat16)


def features(out):
    raw = out[:, : 2 * GROUP]
    low = jnp.where(raw > 0.0, raw + 1.0, jnp.exp(jnp.minimum(raw, 0.0))).astype(jnp.bfloat16)
    return low[:, :GROUP], low[:, GROUP:], out[:, 2 * GROUP :].astype(jnp.bfloat16)


def place_rows(dest, start, x, here, there):
    rows = here.shape[0]
    for place, values in ((x, here), (1 - x, there)):
        dest[pl.ds(pl.multiple_of(start + place * rows, rows), rows), :] = values


def choose(pick, first, second, dest):
    @pl.when(pick)
    def _():
        dest[...] = first[...]

    @pl.when(jnp.logical_not(pick))
    def _():
        dest[...] = second[...]


def column_sum(raw):
    _, x, u = places()
    columns = pl.ds(pl.multiple_of((2 * x + u) * GROUP, GROUP), GROUP)
    return jnp.sum(raw[:, columns].astype(jnp.float32), axis=0, keepdims=True)


def store(out, feats, at):
    query, key, value = features(out)
    rows = pl.ds(at, out.shape[0])
    feats[rows, :GROUP] = query
    feats[rows, GROUP : 2 * GROUP] = key
    feats[rows, 2 * GROUP :] = value


def early_kernel(lengths, own, across, gain, *refs):
    normed, partial, sums, weights, raw = refs[2 * PLANES - 2 :]
    z, x, _ = places()
    choose(lengths[0, 0] > own.shape[0], own, across, raw)
    normed[...] = normalise(raw[...], gain[...])
    sums[...] = column_sum(raw)
    total = jnp.zeros(partial.shape, jnp.float32)
    for j in range(PLANES - 1):
        start = pl.multiple_of(jnp.bitwise_xor(z, j) * GROUP, GROUP)
        place_rows(weights, start, x, refs[2 * j][...], refs[2 * j + 1][...])
        rows = pl.ds(start, GROUP)
        total = total + jnp.dot(normed[:, rows], weights[rows, :], preferred_element_type=jnp.float32)
    weights[pl.ds(pl.multiple_of((PLANES - 1 - z) * GROUP, GROUP), GROUP), :] = jnp.zeros(
        (GROUP, weights.shape[1]), weights.dtype
    )
    partial[...] = total


def first_kernel(normed, partial, far_own, far_near, feats, last):
    z, x, _ = places()
    place_rows(last, 0, x, far_own[...], far_near[...])
    columns = pl.ds(pl.multiple_of((PLANES - 1 - z) * GROUP, GROUP), GROUP)
    store(partial[...] + jnp.dot(normed[:, columns], last[...], preferred_element_type=jnp.float32), feats, 0)


def second_kernel(lengths, near, corner, gain, early, last, first, first_sums, feats, message, sums, weights, raw):
    tokens = near.shape[0]
    z, x, _ = places()
    weights[...] = early[...]
    weights[pl.ds(pl.multiple_of((PLANES - 1 - z) * GROUP, GROUP), GROUP), :] = last[...]
    choose(lengths[0, 0] > tokens, near, corner, raw)
    feats[pl.ds(pl.multiple_of(x * tokens, tokens), tokens), :] = first[...]
    out = jnp.dot(normalise(raw[...], gain[...]), weights[...], preferred_element_type=jnp.float32)
    store(out, feats, pl.multiple_of((1 - x) * tokens, tokens))
    sums[...] = first_sums[...] + column_sum(raw)
    total = jnp.sum(feats[:, GROUP : 2 * GROUP].astype(jnp.float32), axis=0, keepdims=True)
    high, low = split_two(total)
    for h in range(GROUP // HEAD_DIM):
        at = h * HEAD_DIM
        key = feats[:, GROUP + at : GROUP + at + HEAD_DIM]
        value = feats[:, 2 * GROUP + at : 2 * GROUP + at + HEAD_DIM]
        state = lax.dot_general(key, value, DOT_T, preferred_element_type=jnp.float32)
        message[at : at + HEAD_DIM, :] = state.astype(jnp.bfloat16)
    total_rows = [high[:, :HEAD_DIM], high[:, HEAD_DIM:], low[:, :HEAD_DIM], low[:, HEAD_DIM:]]
    message[GROUP:, :] = jnp.concatenate(total_rows * 4, axis=0)


def triangle(tokens, upper):
    row = lax.broadcasted_iota(jnp.int32, (tokens, tokens), 0)
    col = lax.broadcasted_iota(jnp.int32, (tokens, tokens), 1)
    return (row <= col if upper else row >= col).astype(jnp.bfloat16)


def shares(query, key, carry):
    prefix = jnp.dot(triangle(key.shape[0], False), key, preferred_element_type=jnp.float32) + carry
    wide = query.astype(jnp.float32)
    return wide / by_head(head_sums(wide * prefix)), prefix[key.shape[0] - 1 :, :]


def suffix(share):
    upper = triangle(share.shape[0], True)
    high, low = split_two(share)
    return jnp.dot(upper, high, preferred_element_type=jnp.float32) + jnp.dot(
        upper, low, preferred_element_type=jnp.float32
    )


def weighted(key, value, after):
    weight = by_head(head_sums(key.astype(jnp.float32) * after))
    return jnp.sum(weight * value.astype(jnp.float32), axis=0, keepdims=True)


def local_kernel(feats, local):
    tokens = feats.shape[0] // 2
    lower = triangle(tokens, False)
    carry = jnp.zeros((1, GROUP), jnp.float32)
    for slot in range(2):
        at = pl.ds(slot * tokens, tokens)
        prefix = jnp.dot(lower, feats[at, GROUP : 2 * GROUP], preferred_element_type=jnp.float32) + carry
        local[at, :] = by_head(head_sums(feats[at, :GROUP].astype(jnp.float32) * prefix))
        carry = prefix[tokens - 1 :, :]


def short_kernel(lengths, own, near, across, corner, weights, gain, out, raw):
    tokens = own.shape[0]
    z, x, u = places()
    out[...] = jnp.zeros(out.shape, jnp.float32)

    @pl.when(z == 0)
    def _():
        own_long = lengths[0, 0] > tokens

        @pl.when(x == 0)
        def _():
            choose(own_long, across, own, raw)

        @pl.when(x != 0)
        def _():
            choose(own_long, corner, near, raw)

        wide = jnp.dot(normalise(raw[...], gain[...]), weights[...], preferred_element_type=jnp.float32)
        query, key, value = features(wide)
        share, _ = shares(query, key, jnp.zeros((1, GROUP), jnp.float32))
        columns = pl.ds(pl.multiple_of((2 * x + u) * GROUP, GROUP), GROUP)
        total = jnp.sum(raw[:, columns].astype(jnp.float32), axis=0, keepdims=True)
        out[...] = total + weighted(key, value, suffix(share))


def pool_kernel(lengths, state_1, state_2, state_3, feats, local, sums, short, gain, part):
    tokens = feats.shape[0] // 2
    z, x, u = places()
    long_u = jnp.where(lengths[0, 0] > tokens, u, 1 - u)
    states = [(jnp.bitwise_xor(z, j) < z, ref) for j, ref in enumerate((state_1, state_2, state_3), 1)]
    before = jnp.zeros((1, GROUP), jnp.float32)
    for earlier, ref in states:
        rows = ref[GROUP : GROUP + 16, :].astype(jnp.float32)
        total = jnp.concatenate([rows[0:1] + rows[2:3], rows[1:2] + rows[3:4]], axis=1)
        before = before + jnp.where(earlier, total, 0.0)

    def block(slot):
        at = pl.ds(slot * tokens, tokens)
        return feats[at, :GROUP], feats[at, GROUP : 2 * GROUP], feats[at, 2 * GROUP :]

    query_one, key_one, value_one = block(0)
    query_two, key_two, value_two = block(1)
    row = lax.broadcasted_iota(jnp.int32, (GROUP, GROUP), 0) < HEAD_DIM
    col = lax.broadcasted_iota(jnp.int32, (GROUP, GROUP), 1) < HEAD_DIM
    same_head = jnp.where(row == col, jnp.broadcast_to(before, (GROUP, GROUP)), 0.0)
    high, low = split_two(same_head)

    def share(query, at):
        total = local[at : at + tokens, :]
        for table in (high, low):
            total = total + lax.dot_general(query, table, DOT_NT, preferred_element_type=jnp.float32)
        return query.astype(jnp.float32) / total

    share_one = share(query_one, 0)
    share_two = share(query_two, tokens)
    after_two = suffix(share_two)
    after_one = suffix(share_one) + after_two[0:1, :]
    long_row = weighted(key_one, value_one, after_one) + weighted(key_two, value_two, after_two) + sums[...]
    weight = after_one[0:1, :]
    for earlier, ref in states:
        high, low = split_two(jnp.where(earlier, weight, 0.0))
        products = []
        for h in range(GROUP // HEAD_DIM):
            at = h * HEAD_DIM
            both = jnp.concatenate([high[:, at : at + HEAD_DIM]] * 8 + [low[:, at : at + HEAD_DIM]] * 8, axis=0)
            out = jnp.dot(both, ref[at : at + HEAD_DIM, :], preferred_element_type=jnp.float32)
            products.append(out[0:1] + out[8:9])
        long_row = long_row + jnp.concatenate(products, axis=1)

    short_row = short[...]
    first = jnp.where(long_u == 0, long_row, short_row)
    second = jnp.where(long_u == 0, short_row, long_row)
    own_gain = gain[:, pl.ds(pl.multiple_of((2 * x + u) * GROUP, GROUP), GROUP)]
    half = jnp.where(lax.rem(z, 2) == 0, own_gain[:, :HEAD_DIM], own_gain[:, HEAD_DIM:])
    part[...] = jnp.broadcast_to(jnp.concatenate([first, second, half], axis=1)[None], part.shape)


def loss_kernel(positives, parts, vec, loss, mine):
    z, x, u = places()
    domain = lax.axis_index("domain")
    width = mine.shape[1]
    piece = vec.shape[2]

    def collect(place):
        groups = []
        for group in range(PLANE):
            at = [parts[2 * (PLANE * plane + group) + place] for plane in range(PLANES)]
            total = (at[0][:, : 2 * GROUP] + at[1][:, : 2 * GROUP]) + (at[2][:, : 2 * GROUP] + at[3][:, : 2 * GROUP])
            gain = jnp.concatenate([at[0][:, 2 * GROUP :], at[1][:, 2 * GROUP :]], axis=1)
            groups.append((total[:, :GROUP], total[:, GROUP:], gain))
        return groups

    def reduced(terms):
        total = (terms[0] + terms[1]) + (terms[2] + terms[3])
        return jnp.sum(total, axis=1, keepdims=True)

    own = [(jnp.where(u == 0, a, b), gain) for a, b, gain in collect(domain)]
    other = collect(1 - domain)
    scaled = [a * gain for a, gain in own]
    for group in range(PLANE):
        mine[:, group * GROUP : (group + 1) * GROUP] = scaled[group]
    factor = lax.rsqrt(reduced([a * a for a, _ in own]) / width + epsilon)
    logits = []
    for user in range(2):
        norm = reduced([o[user] * o[user] for o in other])
        product = reduced([s * (o[user] * o[2]) for s, o in zip(scaled, other)])
        logits.append(product * factor * lax.rsqrt(norm / width + epsilon) * (logit_scale / width))
    start = pl.multiple_of((2 * z + x) * piece, piece)
    vec[0] = (mine[:, pl.ds(start, piece)] * factor).astype(jnp.bfloat16)
    forward = jnp.where(u == 0, positives[0], positives[1])
    backward = jnp.where(positives[0] == u, 0, 1)
    partner = jnp.where(domain == 0, forward, backward)
    top = jnp.maximum(logits[0], logits[1])
    spread = jnp.log(jnp.exp(logits[0] - top) + jnp.exp(logits[1] - top)) + top
    loss[...] = spread - jnp.where(partner == 0, logits[0], logits[1])


def vmem():
    return pl.BlockSpec(memory_space=pltpu.VMEM)


def anywhere():
    return pl.BlockSpec(memory_space=pl.ANY)


def hbm():
    return pl.BlockSpec(memory_space=pltpu.HBM)


def smem():
    return pl.BlockSpec(memory_space=pltpu.SMEM)


def call(kernel, outs, in_specs, scratch, flops):
    return pl.pallas_call(
        kernel,
        out_shape=outs,
        in_specs=in_specs,
        out_specs=jax.tree.map(lambda _: vmem(), outs),
        scratch_shapes=scratch,
        compiler_params=pltpu.CompilerParams(vmem_limit_bytes=40 * 1024 * 1024),
        cost_estimate=pl.CostEstimate(flops=flops, bytes_accessed=2**21, transcendentals=0),
    )


def towers(history, qkv_weight, norm_gain, pool_gain, lengths, positives):
    events = history[0, 0]
    tokens, width = events.shape
    weight = qkv_weight[0]
    rows = weight.shape[0]
    f32, bf16 = jnp.float32, jnp.bfloat16
    shape = jax.ShapeDtypeStruct
    here = PLANE * PLANES

    def hop(a, target):
        pairs = [(i, target(i // PLANE) * PLANE + i % PLANE) for i in range(here) if target(i // PLANE) is not None]
        return lax.ppermute(a, ("seq", "dp"), pairs)

    def plane_hop(a, move):
        return lax.ppermute(a, ("seq", "dp"), [(i, i ^ move) for i in range(here)])

    def each(a):
        return [hop(a, lambda p: p ^ j) for j in range(1, PLANES)]

    wide = 3 * GROUP
    w_own, w_sent = call(
        pack_kernel, (shape((rows, wide), bf16),) * 2, [hbm()], [pltpu.SemaphoreType.DMA((6,))], 0
    )(pltpu.with_memory_space_constraint(weight, pltpu.HBM))
    near = plane_hop(events, 2)
    across = plane_hop(events, 1)
    w_near = plane_hop(w_sent, 2)
    two_own = hop(call(gate_kernel, shape((rows, wide), bf16), [vmem()] + [anywhere()] * 1, [], 0)(w_own, w_sent), lambda p: p ^ 2)
    two_near = hop(w_near, lambda p: p ^ 2)
    one_own = hop(w_own, lambda p: p ^ 1)
    one_near = hop(call(gate_kernel, shape((rows, wide), bf16), [vmem()] + [anywhere()] * 1, [], 0)(w_near, one_own), lambda p: p ^ 1)
    far_own = hop(call(gate_kernel, shape((rows, wide), bf16), [vmem()] + [anywhere()] * 1, [], 0)(two_own, one_near), lambda p: p ^ 1)
    far_near = hop(call(gate_kernel, shape((rows, wide), bf16), [vmem()] + [anywhere()] * 1, [], 0)(two_near, one_near), lambda p: p ^ 1)
    corner = plane_hop(call(gate_kernel, shape((tokens, width), bf16), [vmem()] + [anywhere()] * 2, [], 0)(events, one_own, w_near), 3)

    normed, partial, first_sums, early = call(
        early_kernel,
        (shape((tokens, width), bf16), shape((tokens, wide), f32), shape((1, GROUP), f32), shape((width, wide), bf16)),
        [smem()] + [vmem()] * (1 + 2 * PLANES),
        [pltpu.VMEM((tokens, width), bf16)],
        2 * tokens * 3 * GROUP * wide,
    )(lengths, events, across, norm_gain, w_own, w_near, one_own, one_near, two_own, two_near)
    first, last = call(
        first_kernel,
        (shape((tokens, wide), bf16), shape((GROUP, wide), bf16)),
        [vmem()] * 4,
        [],
        2 * tokens * GROUP * wide,
    )(normed, partial, far_own, far_near)
    feats, message, sums, weights = call(
        second_kernel,
        (
            shape((2 * tokens, wide), bf16),
            shape((MESSAGE, HEAD_DIM), bf16),
            shape((1, GROUP), f32),
            shape((width, wide), bf16),
        ),
        [smem()] + [vmem()] * 7,
        [pltpu.VMEM((tokens, width), bf16)],
        2 * tokens * width * wide,
    )(lengths, near, corner, norm_gain, early, last, first, first_sums)
    short = call(
        short_kernel,
        shape((1, GROUP), f32),
        [smem()] + [vmem()] * 6,
        [pltpu.VMEM((tokens, width), bf16)],
        2 * tokens * width * wide,
    )(lengths, events, near, across, corner, weights, norm_gain)
    local = call(
        local_kernel, shape((2 * tokens, GROUP), f32), [vmem()], [], 2 * 2 * tokens * tokens * GROUP
    )(feats)
    part = call(
        pool_kernel,
        shape((2 * here, 1, 2 * GROUP + HEAD_DIM), f32),
        [smem()] + [vmem()] * 8,
        [],
        2 * 9 * tokens * tokens * GROUP,
    )(lengths, *each(message), feats, local, sums, short, pool_gain)
    parts = lax.all_to_all(part, ("seq", "dp", "domain"), 0, 0, tiled=True)
    vec, loss = call(
        loss_kernel,
        (shape((1, 1, width // 8), bf16), shape((1, 1), f32)),
        [smem(), vmem()],
        [pltpu.VMEM((1, width), f32)],
        2**14,
    )(positives, parts)
    return vec, loss


def solution(mesh):
    placed = (
        P("domain", "dp", "seq", None),
        P("domain", "seq", None),
        P("domain", None),
        P("domain", None),
        P("domain", "dp"),
        P(),
    )
    small = mesh.shape["seq"] == 2 * PLANES and mesh.shape["dp"] == 2
    return jax.shard_map(
        towers if small else shards,
        mesh=mesh,
        in_specs=placed,
        out_specs=(P("domain", "dp", "seq"), P("domain", "dp")),
        check_vma=False,
    )
```

```python
import functools

import jax
import jax.numpy as jnp
from jax import lax
from jax.experimental import pallas as pl
from jax.experimental.pallas import tpu as pltpu
from jax.sharding import PartitionSpec as P

HEADS = 8
HEAD_DIM = 128


logit_scale = 20.0
epsilon = 1e-06
highest = lax.Precision.HIGHEST


def carried_in(part, axis, combine, identity):
    place = lax.axis_index(axis)
    gathered = jax.tree.map(lambda a: lax.all_gather(a, axis), part)
    state = jax.tree.map(lambda a, e: jnp.zeros_like(a) + jnp.asarray(e, a.dtype), part, identity)

    def one(hop, state):
        return combine(
            state, jax.tree.map(lambda a: lax.dynamic_index_in_dim(a, hop, 0, False), gathered)
        )

    return lax.fori_loop(0, place, one, state)


def partner_2(block, axis, stride):
    count = lax.axis_size(axis)
    route = []
    for low in range(count):
        high = low | 1 << stride
        if high != low and high < count:
            route += [(low, high), (high, low)]
    return lax.ppermute(block, axis, route)


def feature_map(values):
    return jax.nn.elu(values) + 1.0


def add_pair(earlier, later):
    return (earlier[0] + later[0], earlier[1] + later[1])


def shards(history, qkv_weight, norm_gain, pool_gain, lengths, positives):
    seq_count = lax.axis_size("seq")
    seq_place = lax.axis_index("seq")
    group_place = lax.axis_index("dp")
    domain_place = lax.axis_index("domain")
    events = history[0]
    users_dev, tokens_dev, width = events.shape
    row_count = users_dev * tokens_dev
    wide = events.astype(jnp.float32)
    normed = (
        wide * lax.rsqrt(jnp.mean(wide * wide, -1, keepdims=True) + epsilon) * norm_gain[0]
    ).astype(jnp.bfloat16)
    normed = normed.reshape(row_count, width)
    rows_here = qkv_weight[0]
    projected = jnp.dot(
        normed,
        lax.all_gather(rows_here, "seq", axis=0, tiled=True),
        preferred_element_type=jnp.float32,
    )
    query_raw = projected[:, :width]
    key_raw = projected[:, width : 2 * width]
    value_raw = projected[:, 2 * width :]
    positions = seq_place * tokens_dev + jnp.arange(tokens_dev)
    valid = positions[None, :] < lengths[0][:, None]
    shape_heads = (users_dev, tokens_dev, HEADS, HEAD_DIM)
    queries = feature_map(query_raw).astype(jnp.bfloat16).reshape(shape_heads)
    key_feats = (
        jnp.where(valid.reshape(row_count)[:, None], feature_map(key_raw), 0.0)
        .astype(jnp.bfloat16)
        .reshape(shape_heads)
    )
    val_feats = value_raw.astype(jnp.bfloat16).reshape(shape_heads)
    local_state = jnp.einsum(
        "uthc,uthd->uhcd", key_feats, val_feats, preferred_element_type=jnp.float32
    )
    local_total = jnp.sum(key_feats.astype(jnp.float32), axis=1)
    state_before, total_before = carried_in(
        (local_state, local_total),
        "seq",
        add_pair,
        (jnp.zeros_like(local_state), jnp.zeros_like(local_total)),
    )
    causal = jnp.arange(tokens_dev)[:, None] >= jnp.arange(tokens_dev)[None, :]
    scores = jnp.einsum("uthc,ushc->uhts", queries, key_feats, preferred_element_type=jnp.float32)
    scores = jnp.where(causal, scores, 0.0)
    denominator = jnp.sum(scores, axis=-1) + jnp.einsum(
        "uthc,uhc->uht", queries.astype(jnp.float32), total_before, precision=highest
    )
    numerator = jnp.einsum(
        "uhts,ushc->uthc",
        scores.astype(jnp.bfloat16),
        val_feats,
        preferred_element_type=jnp.float32,
    )
    numerator = numerator + jnp.einsum(
        "uthc,uhcd->uthd",
        queries,
        state_before.astype(jnp.bfloat16),
        preferred_element_type=jnp.float32,
    )
    attended = numerator / jnp.transpose(denominator, (0, 2, 1))[..., None]
    attended = attended.reshape(users_dev, tokens_dev, width)
    partial_value = jnp.sum(jnp.where(valid[..., None], wide + attended, 0.0), axis=1)
    piece_width = width // seq_count
    gain_row = pool_gain[0]
    pooled = lax.psum(partial_value, "seq")
    factor = lax.rsqrt(jnp.mean(pooled * pooled, -1, keepdims=True) + epsilon)
    full_vec = (pooled * factor * gain_row).astype(jnp.bfloat16)
    out_vec = lax.dynamic_slice_in_dim(full_vec, seq_place * piece_width, piece_width, 1)
    group = lax.all_gather(full_vec, "dp", axis=0, tiled=True)
    other = partner_2(group, "domain", 0)
    logits = jnp.einsum("uc,vc->uv", full_vec, other, preferred_element_type=jnp.float32) * (
        logit_scale / width
    )
    users_all = other.shape[0]
    own_index = group_place * users_dev + jnp.arange(users_dev)
    targets = lax.dynamic_slice_in_dim(positives, group_place * users_dev, users_dev)
    forward_pair = targets[:, None] == jnp.arange(users_all)[None, :]
    backward_pair = positives[None, :] == own_index[:, None]
    partner = jnp.where(domain_place == 0, forward_pair, backward_pair)
    loss = jnp.log(jnp.sum(jnp.exp(logits), axis=-1)) - jnp.sum(
        jnp.where(partner, logits, 0.0), axis=-1
    )
    return (out_vec[None], loss[None])


PLANE = 4
PLANES = 4
GROUP = 256
DOT_T = (((0,), (0,)), ((), ()))
DOT_NT = (((1,), (1,)), ((), ()))
MESSAGE = GROUP + 16


def places():
    seq_place = lax.axis_index("seq")
    return lax.div(seq_place, 2), lax.rem(seq_place, 2), lax.axis_index("dp")


def head_sums(a):
    return [
        jnp.sum(a[:, h * HEAD_DIM : (h + 1) * HEAD_DIM], axis=1, keepdims=True)
        for h in range(GROUP // HEAD_DIM)
    ]


def by_head(columns):
    rows = columns[0].shape[0]
    return jnp.concatenate([jnp.broadcast_to(c, (rows, HEAD_DIM)) for c in columns], axis=1)


def split_two(a):
    high = a.astype(jnp.bfloat16)
    return high, (a - high.astype(jnp.float32)).astype(jnp.bfloat16)


def pack_kernel(weight, own, sent, sems):
    _, x, u = places()
    width = weight.shape[1] // 3
    copies = []
    for move, out in ((2, sent), (0, own)):
        group = jnp.bitwise_xor(2 * x + u, move)
        for part in range(3):
            start = pl.multiple_of(part * width + group * GROUP, GROUP)
            copies.append(
                pltpu.make_async_copy(
                    weight.at[:, pl.ds(start, GROUP)], out.at[:, pl.ds(part * GROUP, GROUP)], sems.at[len(copies)]
                )
            )
    for copy in copies:
        copy.start()
    for copy in copies:
        copy.wait()


def gate_kernel(values, *rest):
    rest[-1][...] = values[...]


def normalise(values, gain):
    wide = values.astype(jnp.float32)
    scale = lax.rsqrt(jnp.mean(wide * wide, axis=1, keepdims=True) + epsilon)
    return (wide * scale * gain).astype(jnp.bfloat16)


def features(out):
    raw = out[:, : 2 * GROUP]
    low = jnp.where(raw > 0.0, raw + 1.0, jnp.exp(jnp.minimum(raw, 0.0))).astype(jnp.bfloat16)
    return low[:, :GROUP], low[:, GROUP:], out[:, 2 * GROUP :].astype(jnp.bfloat16)


def place_rows(dest, start, x, here, there):
    rows = here.shape[0]
    for place, values in ((x, here), (1 - x, there)):
        dest[pl.ds(pl.multiple_of(start + place * rows, rows), rows), :] = values


def choose(pick, first, second, dest):
    @pl.when(pick)
    def _():
        dest[...] = first[...]

    @pl.when(jnp.logical_not(pick))
    def _():
        dest[...] = second[...]


def column_sum(raw):
    _, x, u = places()
    columns = pl.ds(pl.multiple_of((2 * x + u) * GROUP, GROUP), GROUP)
    return jnp.sum(raw[:, columns].astype(jnp.float32), axis=0, keepdims=True)


def store(out, feats, at):
    query, key, value = features(out)
    rows = pl.ds(at, out.shape[0])
    feats[rows, :GROUP] = query
    feats[rows, GROUP : 2 * GROUP] = key
    feats[rows, 2 * GROUP :] = value


def early_kernel(lengths, own, across, gain, *refs):
    normed, partial, sums, weights, raw = refs[2 * PLANES - 2 :]
    z, x, _ = places()
    choose(lengths[0, 0] > own.shape[0], own, across, raw)
    normed[...] = normalise(raw[...], gain[...])
    sums[...] = column_sum(raw)
    total = jnp.zeros(partial.shape, jnp.float32)
    for j in range(PLANES - 1):
        start = pl.multiple_of(jnp.bitwise_xor(z, j) * GROUP, GROUP)
        place_rows(weights, start, x, refs[2 * j][...], refs[2 * j + 1][...])
        rows = pl.ds(start, GROUP)
        total = total + jnp.dot(normed[:, rows], weights[rows, :], preferred_element_type=jnp.float32)
    weights[pl.ds(pl.multiple_of((PLANES - 1 - z) * GROUP, GROUP), GROUP), :] = jnp.zeros(
        (GROUP, weights.shape[1]), weights.dtype
    )
    partial[...] = total


def first_kernel(normed, partial, far_own, far_near, feats, last):
    z, x, _ = places()
    place_rows(last, 0, x, far_own[...], far_near[...])
    columns = pl.ds(pl.multiple_of((PLANES - 1 - z) * GROUP, GROUP), GROUP)
    store(partial[...] + jnp.dot(normed[:, columns], last[...], preferred_element_type=jnp.float32), feats, 0)


def second_kernel(lengths, near, corner, gain, early, last, first, first_sums, feats, message, sums, raw, normed):
    tokens = near.shape[0]
    z, x, _ = places()
    choose(lengths[0, 0] > tokens, near, corner, raw)
    feats[pl.ds(pl.multiple_of(x * tokens, tokens), tokens), :] = first[...]
    normed[...] = normalise(raw[...], gain[...])
    columns = pl.ds(pl.multiple_of((PLANES - 1 - z) * GROUP, GROUP), GROUP)
    out = jnp.dot(normed[:, columns], last[...], preferred_element_type=jnp.float32)
    for j in range(PLANES - 1):
        rows = pl.ds(pl.multiple_of(jnp.bitwise_xor(z, j) * GROUP, GROUP), GROUP)
        out = out + jnp.dot(normed[:, rows], early[rows, :], preferred_element_type=jnp.float32)
    store(out, feats, pl.multiple_of((1 - x) * tokens, tokens))
    sums[...] = first_sums[...] + column_sum(raw)
    total = jnp.sum(feats[:, GROUP : 2 * GROUP].astype(jnp.float32), axis=0, keepdims=True)
    high, low = split_two(total)
    for h in range(GROUP // HEAD_DIM):
        at = h * HEAD_DIM
        key = feats[:, GROUP + at : GROUP + at + HEAD_DIM]
        value = feats[:, 2 * GROUP + at : 2 * GROUP + at + HEAD_DIM]
        state = lax.dot_general(key, value, DOT_T, preferred_element_type=jnp.float32)
        message[at : at + HEAD_DIM, :] = state.astype(jnp.bfloat16)
    total_rows = [high[:, :HEAD_DIM], high[:, HEAD_DIM:], low[:, :HEAD_DIM], low[:, HEAD_DIM:]]
    message[GROUP:, :] = jnp.concatenate(total_rows * 4, axis=0)


def triangle(tokens, upper):
    row = lax.broadcasted_iota(jnp.int32, (tokens, tokens), 0)
    col = lax.broadcasted_iota(jnp.int32, (tokens, tokens), 1)
    return (row <= col if upper else row >= col).astype(jnp.bfloat16)


def shares(query, key, carry):
    prefix = jnp.dot(triangle(key.shape[0], False), key, preferred_element_type=jnp.float32) + carry
    wide = query.astype(jnp.float32)
    return wide / by_head(head_sums(wide * prefix)), prefix[key.shape[0] - 1 :, :]


def suffix(share):
    upper = triangle(share.shape[0], True)
    high, low = split_two(share)
    return jnp.dot(upper, high, preferred_element_type=jnp.float32) + jnp.dot(
        upper, low, preferred_element_type=jnp.float32
    )


def weighted(key, value, after):
    weight = by_head(head_sums(key.astype(jnp.float32) * after))
    return jnp.sum(weight * value.astype(jnp.float32), axis=0, keepdims=True)


def local_kernel(feats, local):
    tokens = feats.shape[0] // 2
    lower = triangle(tokens, False)
    carry = jnp.zeros((1, GROUP), jnp.float32)
    for slot in range(2):
        at = pl.ds(slot * tokens, tokens)
        prefix = jnp.dot(lower, feats[at, GROUP : 2 * GROUP], preferred_element_type=jnp.float32) + carry
        local[at, :] = by_head(head_sums(feats[at, :GROUP].astype(jnp.float32) * prefix))
        carry = prefix[tokens - 1 :, :]


def short_kernel(lengths, own, near, across, corner, early, last, gain, out, raw):
    tokens = own.shape[0]
    z, x, u = places()
    out[...] = jnp.zeros(out.shape, jnp.float32)

    @pl.when(z == 0)
    def _():
        own_long = lengths[0, 0] > tokens

        @pl.when(x == 0)
        def _():
            choose(own_long, across, own, raw)

        @pl.when(x != 0)
        def _():
            choose(own_long, corner, near, raw)

        low = normalise(raw[...], gain[...])
        wide = jnp.dot(low, early[...], preferred_element_type=jnp.float32)
        wide = wide + jnp.dot(low[:, 3 * GROUP :], last[...], preferred_element_type=jnp.float32)
        query, key, value = features(wide)
        share, _ = shares(query, key, jnp.zeros((1, GROUP), jnp.float32))
        columns = pl.ds(pl.multiple_of((2 * x + u) * GROUP, GROUP), GROUP)
        total = jnp.sum(raw[:, columns].astype(jnp.float32), axis=0, keepdims=True)
        out[...] = total + weighted(key, value, suffix(share))


def pool_kernel(lengths, state_3, state_2, state_1, feats, local, sums, short, gain, part):
    tokens = feats.shape[0] // 2
    z, x, u = places()
    long_u = jnp.where(lengths[0, 0] > tokens, u, 1 - u)
    states = [(jnp.bitwise_xor(z, j) < z, ref) for j, ref in enumerate((state_1, state_2, state_3), 1)]
    before = jnp.zeros((1, GROUP), jnp.float32)
    for earlier, ref in states:
        rows = ref[GROUP : GROUP + 16, :].astype(jnp.float32)
        total = jnp.concatenate([rows[0:1] + rows[2:3], rows[1:2] + rows[3:4]], axis=1)
        before = before + jnp.where(earlier, total, 0.0)

    def block(slot):
        at = pl.ds(slot * tokens, tokens)
        return feats[at, :GROUP], feats[at, GROUP : 2 * GROUP], feats[at, 2 * GROUP :]

    query_one, key_one, value_one = block(0)
    query_two, key_two, value_two = block(1)
    row = lax.broadcasted_iota(jnp.int32, (GROUP, GROUP), 0) < HEAD_DIM
    col = lax.broadcasted_iota(jnp.int32, (GROUP, GROUP), 1) < HEAD_DIM
    same_head = jnp.where(row == col, jnp.broadcast_to(before, (GROUP, GROUP)), 0.0)
    high, low = split_two(same_head)

    def share(query, at):
        total = local[at : at + tokens, :]
        for table in (high, low):
            total = total + lax.dot_general(query, table, DOT_NT, preferred_element_type=jnp.float32)
        return query.astype(jnp.float32) / total

    share_one = share(query_one, 0)
    share_two = share(query_two, tokens)
    after_two = suffix(share_two)
    after_one = suffix(share_one) + after_two[0:1, :]
    long_row = weighted(key_one, value_one, after_one) + weighted(key_two, value_two, after_two) + sums[...]
    weight = after_one[0:1, :]
    for earlier, ref in states:
        high, low = split_two(jnp.where(earlier, weight, 0.0))
        products = []
        for h in range(GROUP // HEAD_DIM):
            at = h * HEAD_DIM
            both = jnp.concatenate([high[:, at : at + HEAD_DIM]] * 8 + [low[:, at : at + HEAD_DIM]] * 8, axis=0)
            out = jnp.dot(both, ref[at : at + HEAD_DIM, :], preferred_element_type=jnp.float32)
            products.append(out[0:1] + out[8:9])
        long_row = long_row + jnp.concatenate(products, axis=1)

    short_row = short[...]
    first = jnp.where(long_u == 0, long_row, short_row)
    second = jnp.where(long_u == 0, short_row, long_row)
    own_gain = gain[:, pl.ds(pl.multiple_of((2 * x + u) * GROUP, GROUP), GROUP)]
    half = jnp.where(lax.rem(z, 2) == 0, own_gain[:, :HEAD_DIM], own_gain[:, HEAD_DIM:])
    part[...] = jnp.broadcast_to(jnp.concatenate([first, second, half], axis=1)[None], part.shape)


def loss_kernel(positives, parts, vec, loss, mine):
    z, x, u = places()
    domain = lax.axis_index("domain")
    width = mine.shape[1]
    piece = vec.shape[2]

    def collect(place):
        groups = []
        for group in range(PLANE):
            at = [parts[2 * (PLANE * plane + group) + place] for plane in range(PLANES)]
            total = (at[0][:, : 2 * GROUP] + at[1][:, : 2 * GROUP]) + (at[2][:, : 2 * GROUP] + at[3][:, : 2 * GROUP])
            gain = jnp.concatenate([at[0][:, 2 * GROUP :], at[1][:, 2 * GROUP :]], axis=1)
            groups.append((total[:, :GROUP], total[:, GROUP:], gain))
        return groups

    def reduced(terms):
        total = (terms[0] + terms[1]) + (terms[2] + terms[3])
        return jnp.sum(total, axis=1, keepdims=True)

    own = [(jnp.where(u == 0, a, b), gain) for a, b, gain in collect(domain)]
    other = collect(1 - domain)
    scaled = [a * gain for a, gain in own]
    for group in range(PLANE):
        mine[:, group * GROUP : (group + 1) * GROUP] = scaled[group]
    factor = lax.rsqrt(reduced([a * a for a, _ in own]) / width + epsilon)
    logits = []
    for user in range(2):
        norm = reduced([o[user] * o[user] for o in other])
        product = reduced([s * (o[user] * o[2]) for s, o in zip(scaled, other)])
        logits.append(product * factor * lax.rsqrt(norm / width + epsilon) * (logit_scale / width))
    start = pl.multiple_of((2 * z + x) * piece, piece)
    vec[0] = (mine[:, pl.ds(start, piece)] * factor).astype(jnp.bfloat16)
    forward = jnp.where(u == 0, positives[0], positives[1])
    backward = jnp.where(positives[0] == u, 0, 1)
    partner = jnp.where(domain == 0, forward, backward)
    top = jnp.maximum(logits[0], logits[1])
    spread = jnp.log(jnp.exp(logits[0] - top) + jnp.exp(logits[1] - top)) + top
    loss[...] = spread - jnp.where(partner == 0, logits[0], logits[1])


def vmem():
    return pl.BlockSpec(memory_space=pltpu.VMEM)


def anywhere():
    return pl.BlockSpec(memory_space=pl.ANY)


def hbm():
    return pl.BlockSpec(memory_space=pltpu.HBM)


def smem():
    return pl.BlockSpec(memory_space=pltpu.SMEM)


def call(kernel, outs, in_specs, scratch, flops):
    return pl.pallas_call(
        kernel,
        out_shape=outs,
        in_specs=in_specs,
        out_specs=jax.tree.map(lambda _: vmem(), outs),
        scratch_shapes=scratch,
        compiler_params=pltpu.CompilerParams(vmem_limit_bytes=40 * 1024 * 1024),
        cost_estimate=pl.CostEstimate(flops=flops, bytes_accessed=2**21, transcendentals=0),
    )


def towers(history, qkv_weight, norm_gain, pool_gain, lengths, positives):
    events = history[0, 0]
    tokens, width = events.shape
    weight = qkv_weight[0]
    rows = weight.shape[0]
    f32, bf16 = jnp.float32, jnp.bfloat16
    shape = jax.ShapeDtypeStruct
    here = PLANE * PLANES

    def hop(a, target):
        pairs = [(i, target(i // PLANE) * PLANE + i % PLANE) for i in range(here) if target(i // PLANE) is not None]
        return lax.ppermute(a, ("seq", "dp"), pairs)

    def plane_hop(a, move):
        return lax.ppermute(a, ("seq", "dp"), [(i, i ^ move) for i in range(here)])

    def each(a):
        return [hop(a, lambda p: p ^ j) for j in range(1, PLANES)]

    wide = 3 * GROUP
    w_own, w_sent = call(
        pack_kernel, (shape((rows, wide), bf16),) * 2, [hbm()], [pltpu.SemaphoreType.DMA((6,))], 0
    )(pltpu.with_memory_space_constraint(weight, pltpu.HBM))
    near = plane_hop(events, 2)
    across = plane_hop(events, 1)
    w_near = plane_hop(w_sent, 2)
    two_own = hop(call(gate_kernel, shape((rows, wide), bf16), [vmem()] + [anywhere()] * 1, [], 0)(w_own, w_sent), lambda p: p ^ 2)
    two_near = hop(w_near, lambda p: p ^ 2)
    one_own = hop(w_own, lambda p: p ^ 1)
    one_near = hop(call(gate_kernel, shape((rows, wide), bf16), [vmem()] + [anywhere()] * 1, [], 0)(w_near, one_own), lambda p: p ^ 1)
    far_own = hop(call(gate_kernel, shape((rows, wide), bf16), [vmem()] + [anywhere()] * 1, [], 0)(two_own, one_near), lambda p: p ^ 1)
    far_near = hop(call(gate_kernel, shape((rows, wide), bf16), [vmem()] + [anywhere()] * 1, [], 0)(two_near, one_near), lambda p: p ^ 1)
    corner = plane_hop(call(gate_kernel, shape((tokens, width), bf16), [vmem()] + [anywhere()] * 2, [], 0)(events, one_own, w_near), 3)

    normed, partial, first_sums, early = call(
        early_kernel,
        (shape((tokens, width), bf16), shape((tokens, wide), f32), shape((1, GROUP), f32), shape((width, wide), bf16)),
        [smem()] + [vmem()] * (1 + 2 * PLANES),
        [pltpu.VMEM((tokens, width), bf16)],
        2 * tokens * 3 * GROUP * wide,
    )(lengths, events, across, norm_gain, w_own, w_near, one_own, one_near, two_own, two_near)
    first, last = call(
        first_kernel,
        (shape((tokens, wide), bf16), shape((GROUP, wide), bf16)),
        [vmem()] * 4,
        [],
        2 * tokens * GROUP * wide,
    )(normed, partial, far_own, far_near)
    feats, message, sums = call(
        second_kernel,
        (
            shape((2 * tokens, wide), bf16),
            shape((MESSAGE, HEAD_DIM), bf16),
            shape((1, GROUP), f32),
        ),
        [smem()] + [vmem()] * 7,
        [pltpu.VMEM((tokens, width), bf16)] * 2,
        2 * tokens * width * wide,
    )(lengths, near, corner, norm_gain, early, last, first, first_sums)
    short = call(
        short_kernel,
        shape((1, GROUP), f32),
        [smem()] + [vmem()] * 7,
        [pltpu.VMEM((tokens, width), bf16)],
        2 * tokens * width * wide,
    )(lengths, events, near, across, corner, early, last, norm_gain)
    local = call(
        local_kernel, shape((2 * tokens, GROUP), f32), [vmem()], [], 2 * 2 * tokens * tokens * GROUP
    )(feats)
    part = call(
        pool_kernel,
        shape((2 * here, 1, 2 * GROUP + HEAD_DIM), f32),
        [smem()] + [vmem()] * 8,
        [],
        2 * 9 * tokens * tokens * GROUP,
    )(lengths, *each(message)[::-1], feats, local, sums, short, pool_gain)
    parts = lax.all_to_all(part, ("seq", "dp", "domain"), 0, 0, tiled=True)
    vec, loss = call(
        loss_kernel,
        (shape((1, 1, width // 8), bf16), shape((1, 1), f32)),
        [smem(), vmem()],
        [pltpu.VMEM((1, width), f32)],
        2**14,
    )(positives, parts)
    return vec, loss


def solution(mesh):
    placed = (
        P("domain", "dp", "seq", None),
        P("domain", "seq", None),
        P("domain", None),
        P("domain", None),
        P("domain", "dp"),
        P(),
    )
    small = mesh.shape["seq"] == 2 * PLANES and mesh.shape["dp"] == 2
    return jax.shard_map(
        towers if small else shards,
        mesh=mesh,
        in_specs=placed,
        out_specs=(P("domain", "dp", "seq"), P("domain", "dp")),
        check_vma=False,
    )
```

```python
import functools

import jax
import jax.numpy as jnp
from jax import lax
from jax.experimental import pallas as pl
from jax.experimental.pallas import tpu as pltpu
from jax.sharding import PartitionSpec as P

HEADS = 8
HEAD_DIM = 128


logit_scale = 20.0
epsilon = 1e-06
highest = lax.Precision.HIGHEST


def carried_in(part, axis, combine, identity):
    place = lax.axis_index(axis)
    gathered = jax.tree.map(lambda a: lax.all_gather(a, axis), part)
    state = jax.tree.map(lambda a, e: jnp.zeros_like(a) + jnp.asarray(e, a.dtype), part, identity)

    def one(hop, state):
        return combine(
            state, jax.tree.map(lambda a: lax.dynamic_index_in_dim(a, hop, 0, False), gathered)
        )

    return lax.fori_loop(0, place, one, state)


def partner_2(block, axis, stride):
    count = lax.axis_size(axis)
    route = []
    for low in range(count):
        high = low | 1 << stride
        if high != low and high < count:
            route += [(low, high), (high, low)]
    return lax.ppermute(block, axis, route)


def feature_map(values):
    return jax.nn.elu(values) + 1.0


def add_pair(earlier, later):
    return (earlier[0] + later[0], earlier[1] + later[1])


def shards(history, qkv_weight, norm_gain, pool_gain, lengths, positives):
    seq_count = lax.axis_size("seq")
    seq_place = lax.axis_index("seq")
    group_place = lax.axis_index("dp")
    domain_place = lax.axis_index("domain")
    events = history[0]
    users_dev, tokens_dev, width = events.shape
    row_count = users_dev * tokens_dev
    wide = events.astype(jnp.float32)
    normed = (
        wide * lax.rsqrt(jnp.mean(wide * wide, -1, keepdims=True) + epsilon) * norm_gain[0]
    ).astype(jnp.bfloat16)
    normed = normed.reshape(row_count, width)
    rows_here = qkv_weight[0]
    projected = jnp.dot(
        normed,
        lax.all_gather(rows_here, "seq", axis=0, tiled=True),
        preferred_element_type=jnp.float32,
    )
    query_raw = projected[:, :width]
    key_raw = projected[:, width : 2 * width]
    value_raw = projected[:, 2 * width :]
    positions = seq_place * tokens_dev + jnp.arange(tokens_dev)
    valid = positions[None, :] < lengths[0][:, None]
    shape_heads = (users_dev, tokens_dev, HEADS, HEAD_DIM)
    queries = feature_map(query_raw).astype(jnp.bfloat16).reshape(shape_heads)
    key_feats = (
        jnp.where(valid.reshape(row_count)[:, None], feature_map(key_raw), 0.0)
        .astype(jnp.bfloat16)
        .reshape(shape_heads)
    )
    val_feats = value_raw.astype(jnp.bfloat16).reshape(shape_heads)
    local_state = jnp.einsum(
        "uthc,uthd->uhcd", key_feats, val_feats, preferred_element_type=jnp.float32
    )
    local_total = jnp.sum(key_feats.astype(jnp.float32), axis=1)
    state_before, total_before = carried_in(
        (local_state, local_total),
        "seq",
        add_pair,
        (jnp.zeros_like(local_state), jnp.zeros_like(local_total)),
    )
    causal = jnp.arange(tokens_dev)[:, None] >= jnp.arange(tokens_dev)[None, :]
    scores = jnp.einsum("uthc,ushc->uhts", queries, key_feats, preferred_element_type=jnp.float32)
    scores = jnp.where(causal, scores, 0.0)
    denominator = jnp.sum(scores, axis=-1) + jnp.einsum(
        "uthc,uhc->uht", queries.astype(jnp.float32), total_before, precision=highest
    )
    numerator = jnp.einsum(
        "uhts,ushc->uthc",
        scores.astype(jnp.bfloat16),
        val_feats,
        preferred_element_type=jnp.float32,
    )
    numerator = numerator + jnp.einsum(
        "uthc,uhcd->uthd",
        queries,
        state_before.astype(jnp.bfloat16),
        preferred_element_type=jnp.float32,
    )
    attended = numerator / jnp.transpose(denominator, (0, 2, 1))[..., None]
    attended = attended.reshape(users_dev, tokens_dev, width)
    partial_value = jnp.sum(jnp.where(valid[..., None], wide + attended, 0.0), axis=1)
    piece_width = width // seq_count
    gain_row = pool_gain[0]
    pooled = lax.psum(partial_value, "seq")
    factor = lax.rsqrt(jnp.mean(pooled * pooled, -1, keepdims=True) + epsilon)
    full_vec = (pooled * factor * gain_row).astype(jnp.bfloat16)
    out_vec = lax.dynamic_slice_in_dim(full_vec, seq_place * piece_width, piece_width, 1)
    group = lax.all_gather(full_vec, "dp", axis=0, tiled=True)
    other = partner_2(group, "domain", 0)
    logits = jnp.einsum("uc,vc->uv", full_vec, other, preferred_element_type=jnp.float32) * (
        logit_scale / width
    )
    users_all = other.shape[0]
    own_index = group_place * users_dev + jnp.arange(users_dev)
    targets = lax.dynamic_slice_in_dim(positives, group_place * users_dev, users_dev)
    forward_pair = targets[:, None] == jnp.arange(users_all)[None, :]
    backward_pair = positives[None, :] == own_index[:, None]
    partner = jnp.where(domain_place == 0, forward_pair, backward_pair)
    loss = jnp.log(jnp.sum(jnp.exp(logits), axis=-1)) - jnp.sum(
        jnp.where(partner, logits, 0.0), axis=-1
    )
    return (out_vec[None], loss[None])


PLANE = 4
PLANES = 4
GROUP = 256
DOT_T = (((0,), (0,)), ((), ()))
DOT_NT = (((1,), (1,)), ((), ()))
MESSAGE = GROUP + 16


def places():
    seq_place = lax.axis_index("seq")
    return lax.div(seq_place, 2), lax.rem(seq_place, 2), lax.axis_index("dp")


def head_sums(a):
    return [
        jnp.sum(a[:, h * HEAD_DIM : (h + 1) * HEAD_DIM], axis=1, keepdims=True)
        for h in range(GROUP // HEAD_DIM)
    ]


def by_head(columns):
    rows = columns[0].shape[0]
    return jnp.concatenate([jnp.broadcast_to(c, (rows, HEAD_DIM)) for c in columns], axis=1)


def split_two(a):
    high = a.astype(jnp.bfloat16)
    return high, (a - high.astype(jnp.float32)).astype(jnp.bfloat16)


def pack_kernel(weight, own, sent, sems):
    _, x, u = places()
    width = weight.shape[1] // 3
    copies = []
    for move, out in ((2, sent), (0, own)):
        group = jnp.bitwise_xor(2 * x + u, move)
        for part in range(3):
            start = pl.multiple_of(part * width + group * GROUP, GROUP)
            copies.append(
                pltpu.make_async_copy(
                    weight.at[:, pl.ds(start, GROUP)], out.at[:, pl.ds(part * GROUP, GROUP)], sems.at[len(copies)]
                )
            )
    for copy in copies:
        copy.start()
    for copy in copies:
        copy.wait()


def gate_kernel(values, *rest):
    rest[-1][...] = values[...]


def normalise(values, gain):
    wide = values.astype(jnp.float32)
    scale = lax.rsqrt(jnp.mean(wide * wide, axis=1, keepdims=True) + epsilon)
    return (wide * scale * gain).astype(jnp.bfloat16)


def features(out):
    raw = out[:, : 2 * GROUP]
    low = jnp.where(raw > 0.0, raw + 1.0, jnp.exp(jnp.minimum(raw, 0.0))).astype(jnp.bfloat16)
    return low[:, :GROUP], low[:, GROUP:], out[:, 2 * GROUP :].astype(jnp.bfloat16)


def place_rows(dest, start, x, here, there):
    rows = here.shape[0]
    for place, values in ((x, here), (1 - x, there)):
        dest[pl.ds(pl.multiple_of(start + place * rows, rows), rows), :] = values


def choose(pick, first, second, dest):
    @pl.when(pick)
    def _():
        dest[...] = first[...]

    @pl.when(jnp.logical_not(pick))
    def _():
        dest[...] = second[...]


def column_sum(raw):
    _, x, u = places()
    columns = pl.ds(pl.multiple_of((2 * x + u) * GROUP, GROUP), GROUP)
    return jnp.sum(raw[:, columns].astype(jnp.float32), axis=0, keepdims=True)


def store(out, feats, at):
    query, key, value = features(out)
    rows = pl.ds(at, out.shape[0])
    feats[rows, :GROUP] = query
    feats[rows, GROUP : 2 * GROUP] = key
    feats[rows, 2 * GROUP :] = value


def early_kernel(lengths, own, across, gain, *refs):
    normed, partial, sums, weights, raw = refs[2 * PLANES - 2 :]
    z, x, _ = places()
    choose(lengths[0, 0] > own.shape[0], own, across, raw)
    normed[...] = normalise(raw[...], gain[...])
    sums[...] = column_sum(raw)
    total = jnp.zeros(partial.shape, jnp.float32)
    for j in range(PLANES - 1):
        start = pl.multiple_of(jnp.bitwise_xor(z, j) * GROUP, GROUP)
        place_rows(weights, start, x, refs[2 * j][...], refs[2 * j + 1][...])
        rows = pl.ds(start, GROUP)
        total = total + jnp.dot(normed[:, rows], weights[rows, :], preferred_element_type=jnp.float32)
    weights[pl.ds(pl.multiple_of((PLANES - 1 - z) * GROUP, GROUP), GROUP), :] = jnp.zeros(
        (GROUP, weights.shape[1]), weights.dtype
    )
    partial[...] = total


def first_kernel(normed, partial, far_own, far_near, feats, last):
    z, x, _ = places()
    place_rows(last, 0, x, far_own[...], far_near[...])
    columns = pl.ds(pl.multiple_of((PLANES - 1 - z) * GROUP, GROUP), GROUP)
    store(partial[...] + jnp.dot(normed[:, columns], last[...], preferred_element_type=jnp.float32), feats, 0)


def second_kernel(lengths, near, corner, gain, early, last, first, first_sums, feats, message, sums, weights, raw):
    tokens = near.shape[0]
    z, x, _ = places()
    del early
    weights[pl.ds(pl.multiple_of((PLANES - 1 - z) * GROUP, GROUP), GROUP), :] = last[...]
    choose(lengths[0, 0] > tokens, near, corner, raw)
    feats[pl.ds(pl.multiple_of(x * tokens, tokens), tokens), :] = first[...]
    out = jnp.dot(normalise(raw[...], gain[...]), weights[...], preferred_element_type=jnp.float32)
    store(out, feats, pl.multiple_of((1 - x) * tokens, tokens))
    sums[...] = first_sums[...] + column_sum(raw)
    total = jnp.sum(feats[:, GROUP : 2 * GROUP].astype(jnp.float32), axis=0, keepdims=True)
    high, low = split_two(total)
    for h in range(GROUP // HEAD_DIM):
        at = h * HEAD_DIM
        key = feats[:, GROUP + at : GROUP + at + HEAD_DIM]
        value = feats[:, 2 * GROUP + at : 2 * GROUP + at + HEAD_DIM]
        state = lax.dot_general(key, value, DOT_T, preferred_element_type=jnp.float32)
        message[at : at + HEAD_DIM, :] = state.astype(jnp.bfloat16)
    total_rows = [high[:, :HEAD_DIM], high[:, HEAD_DIM:], low[:, :HEAD_DIM], low[:, HEAD_DIM:]]
    message[GROUP:, :] = jnp.concatenate(total_rows * 4, axis=0)


def triangle(tokens, upper):
    row = lax.broadcasted_iota(jnp.int32, (tokens, tokens), 0)
    col = lax.broadcasted_iota(jnp.int32, (tokens, tokens), 1)
    return (row <= col if upper else row >= col).astype(jnp.bfloat16)


def shares(query, key, carry):
    prefix = jnp.dot(triangle(key.shape[0], False), key, preferred_element_type=jnp.float32) + carry
    wide = query.astype(jnp.float32)
    return wide / by_head(head_sums(wide * prefix)), prefix[key.shape[0] - 1 :, :]


def suffix(share):
    upper = triangle(share.shape[0], True)
    high, low = split_two(share)
    return jnp.dot(upper, high, preferred_element_type=jnp.float32) + jnp.dot(
        upper, low, preferred_element_type=jnp.float32
    )


def weighted(key, value, after):
    weight = by_head(head_sums(key.astype(jnp.float32) * after))
    return jnp.sum(weight * value.astype(jnp.float32), axis=0, keepdims=True)


def local_kernel(feats, local):
    tokens = feats.shape[0] // 2
    lower = triangle(tokens, False)
    carry = jnp.zeros((1, GROUP), jnp.float32)
    for slot in range(2):
        at = pl.ds(slot * tokens, tokens)
        prefix = jnp.dot(lower, feats[at, GROUP : 2 * GROUP], preferred_element_type=jnp.float32) + carry
        local[at, :] = by_head(head_sums(feats[at, :GROUP].astype(jnp.float32) * prefix))
        carry = prefix[tokens - 1 :, :]


def short_kernel(lengths, own, near, across, corner, weights, gain, out, raw):
    tokens = own.shape[0]
    z, x, u = places()
    out[...] = jnp.zeros(out.shape, jnp.float32)

    @pl.when(z == 0)
    def _():
        own_long = lengths[0, 0] > tokens

        @pl.when(x == 0)
        def _():
            choose(own_long, across, own, raw)

        @pl.when(x != 0)
        def _():
            choose(own_long, corner, near, raw)

        wide = jnp.dot(normalise(raw[...], gain[...]), weights[...], preferred_element_type=jnp.float32)
        query, key, value = features(wide)
        share, _ = shares(query, key, jnp.zeros((1, GROUP), jnp.float32))
        columns = pl.ds(pl.multiple_of((2 * x + u) * GROUP, GROUP), GROUP)
        total = jnp.sum(raw[:, columns].astype(jnp.float32), axis=0, keepdims=True)
        out[...] = total + weighted(key, value, suffix(share))


def pool_kernel(lengths, state_1, state_2, state_3, feats, local, sums, short, gain, part):
    tokens = feats.shape[0] // 2
    z, x, u = places()
    long_u = jnp.where(lengths[0, 0] > tokens, u, 1 - u)
    states = [(jnp.bitwise_xor(z, j) < z, ref) for j, ref in enumerate((state_1, state_2, state_3), 1)]
    before = jnp.zeros((1, GROUP), jnp.float32)
    for earlier, ref in states:
        rows = ref[GROUP : GROUP + 16, :].astype(jnp.float32)
        total = jnp.concatenate([rows[0:1] + rows[2:3], rows[1:2] + rows[3:4]], axis=1)
        before = before + jnp.where(earlier, total, 0.0)

    def block(slot):
        at = pl.ds(slot * tokens, tokens)
        return feats[at, :GROUP], feats[at, GROUP : 2 * GROUP], feats[at, 2 * GROUP :]

    query_one, key_one, value_one = block(0)
    query_two, key_two, value_two = block(1)
    row = lax.broadcasted_iota(jnp.int32, (GROUP, GROUP), 0) < HEAD_DIM
    col = lax.broadcasted_iota(jnp.int32, (GROUP, GROUP), 1) < HEAD_DIM
    same_head = jnp.where(row == col, jnp.broadcast_to(before, (GROUP, GROUP)), 0.0)
    high, low = split_two(same_head)

    def share(query, at):
        total = local[at : at + tokens, :]
        for table in (high, low):
            total = total + lax.dot_general(query, table, DOT_NT, preferred_element_type=jnp.float32)
        return query.astype(jnp.float32) / total

    share_one = share(query_one, 0)
    share_two = share(query_two, tokens)
    after_two = suffix(share_two)
    after_one = suffix(share_one) + after_two[0:1, :]
    long_row = weighted(key_one, value_one, after_one) + weighted(key_two, value_two, after_two) + sums[...]
    weight = after_one[0:1, :]
    for earlier, ref in states:
        high, low = split_two(jnp.where(earlier, weight, 0.0))
        products = []
        for h in range(GROUP // HEAD_DIM):
            at = h * HEAD_DIM
            both = jnp.concatenate([high[:, at : at + HEAD_DIM]] * 8 + [low[:, at : at + HEAD_DIM]] * 8, axis=0)
            out = jnp.dot(both, ref[at : at + HEAD_DIM, :], preferred_element_type=jnp.float32)
            products.append(out[0:1] + out[8:9])
        long_row = long_row + jnp.concatenate(products, axis=1)

    short_row = short[...]
    first = jnp.where(long_u == 0, long_row, short_row)
    second = jnp.where(long_u == 0, short_row, long_row)
    own_gain = gain[:, pl.ds(pl.multiple_of((2 * x + u) * GROUP, GROUP), GROUP)]
    half = jnp.where(lax.rem(z, 2) == 0, own_gain[:, :HEAD_DIM], own_gain[:, HEAD_DIM:])
    part[...] = jnp.broadcast_to(jnp.concatenate([first, second, half], axis=1)[None], part.shape)


def loss_kernel(positives, parts, vec, loss, mine):
    z, x, u = places()
    domain = lax.axis_index("domain")
    width = mine.shape[1]
    piece = vec.shape[2]

    def collect(place):
        groups = []
        for group in range(PLANE):
            at = [parts[2 * (PLANE * plane + group) + place] for plane in range(PLANES)]
            total = (at[0][:, : 2 * GROUP] + at[1][:, : 2 * GROUP]) + (at[2][:, : 2 * GROUP] + at[3][:, : 2 * GROUP])
            gain = jnp.concatenate([at[0][:, 2 * GROUP :], at[1][:, 2 * GROUP :]], axis=1)
            groups.append((total[:, :GROUP], total[:, GROUP:], gain))
        return groups

    def reduced(terms):
        total = (terms[0] + terms[1]) + (terms[2] + terms[3])
        return jnp.sum(total, axis=1, keepdims=True)

    own = [(jnp.where(u == 0, a, b), gain) for a, b, gain in collect(domain)]
    other = collect(1 - domain)
    scaled = [a * gain for a, gain in own]
    for group in range(PLANE):
        mine[:, group * GROUP : (group + 1) * GROUP] = scaled[group]
    factor = lax.rsqrt(reduced([a * a for a, _ in own]) / width + epsilon)
    logits = []
    for user in range(2):
        norm = reduced([o[user] * o[user] for o in other])
        product = reduced([s * (o[user] * o[2]) for s, o in zip(scaled, other)])
        logits.append(product * factor * lax.rsqrt(norm / width + epsilon) * (logit_scale / width))
    start = pl.multiple_of((2 * z + x) * piece, piece)
    vec[0] = (mine[:, pl.ds(start, piece)] * factor).astype(jnp.bfloat16)
    forward = jnp.where(u == 0, positives[0], positives[1])
    backward = jnp.where(positives[0] == u, 0, 1)
    partner = jnp.where(domain == 0, forward, backward)
    top = jnp.maximum(logits[0], logits[1])
    spread = jnp.log(jnp.exp(logits[0] - top) + jnp.exp(logits[1] - top)) + top
    loss[...] = spread - jnp.where(partner == 0, logits[0], logits[1])


def vmem():
    return pl.BlockSpec(memory_space=pltpu.VMEM)


def anywhere():
    return pl.BlockSpec(memory_space=pl.ANY)


def hbm():
    return pl.BlockSpec(memory_space=pltpu.HBM)


def smem():
    return pl.BlockSpec(memory_space=pltpu.SMEM)


def call(kernel, outs, in_specs, scratch, flops, aliases=None):
    return pl.pallas_call(
        kernel,
        out_shape=outs,
        in_specs=in_specs,
        out_specs=jax.tree.map(lambda _: vmem(), outs),
        scratch_shapes=scratch,
        input_output_aliases=aliases or {},
        compiler_params=pltpu.CompilerParams(vmem_limit_bytes=40 * 1024 * 1024),
        cost_estimate=pl.CostEstimate(flops=flops, bytes_accessed=2**21, transcendentals=0),
    )


def towers(history, qkv_weight, norm_gain, pool_gain, lengths, positives):
    events = history[0, 0]
    tokens, width = events.shape
    weight = qkv_weight[0]
    rows = weight.shape[0]
    f32, bf16 = jnp.float32, jnp.bfloat16
    shape = jax.ShapeDtypeStruct
    here = PLANE * PLANES

    def hop(a, target):
        pairs = [(i, target(i // PLANE) * PLANE + i % PLANE) for i in range(here) if target(i // PLANE) is not None]
        return lax.ppermute(a, ("seq", "dp"), pairs)

    def plane_hop(a, move):
        return lax.ppermute(a, ("seq", "dp"), [(i, i ^ move) for i in range(here)])

    def each(a):
        return [hop(a, lambda p: p ^ j) for j in range(1, PLANES)]

    wide = 3 * GROUP
    w_own, w_sent = call(
        pack_kernel, (shape((rows, wide), bf16),) * 2, [hbm()], [pltpu.SemaphoreType.DMA((6,))], 0
    )(pltpu.with_memory_space_constraint(weight, pltpu.HBM))
    near = plane_hop(events, 2)
    across = plane_hop(events, 1)
    w_near = plane_hop(w_sent, 2)
    two_own = hop(call(gate_kernel, shape((rows, wide), bf16), [vmem()] + [anywhere()] * 1, [], 0)(w_own, w_sent), lambda p: p ^ 2)
    two_near = hop(w_near, lambda p: p ^ 2)
    one_own = hop(w_own, lambda p: p ^ 1)
    one_near = hop(call(gate_kernel, shape((rows, wide), bf16), [vmem()] + [anywhere()] * 1, [], 0)(w_near, one_own), lambda p: p ^ 1)
    far_own = hop(call(gate_kernel, shape((rows, wide), bf16), [vmem()] + [anywhere()] * 1, [], 0)(two_own, one_near), lambda p: p ^ 1)
    far_near = hop(call(gate_kernel, shape((rows, wide), bf16), [vmem()] + [anywhere()] * 1, [], 0)(two_near, one_near), lambda p: p ^ 1)
    corner = plane_hop(call(gate_kernel, shape((tokens, width), bf16), [vmem()] + [anywhere()] * 2, [], 0)(events, one_own, w_near), 3)

    normed, partial, first_sums, early = call(
        early_kernel,
        (shape((tokens, width), bf16), shape((tokens, wide), f32), shape((1, GROUP), f32), shape((width, wide), bf16)),
        [smem()] + [vmem()] * (1 + 2 * PLANES),
        [pltpu.VMEM((tokens, width), bf16)],
        2 * tokens * 3 * GROUP * wide,
    )(lengths, events, across, norm_gain, w_own, w_near, one_own, one_near, two_own, two_near)
    first, last = call(
        first_kernel,
        (shape((tokens, wide), bf16), shape((GROUP, wide), bf16)),
        [vmem()] * 4,
        [],
        2 * tokens * GROUP * wide,
    )(normed, partial, far_own, far_near)
    feats, message, sums, weights = call(
        second_kernel,
        (
            shape((2 * tokens, wide), bf16),
            shape((MESSAGE, HEAD_DIM), bf16),
            shape((1, GROUP), f32),
            shape((width, wide), bf16),
        ),
        [smem()] + [vmem()] * 7,
        [pltpu.VMEM((tokens, width), bf16)],
        2 * tokens * width * wide,
        {4: 3},
    )(lengths, near, corner, norm_gain, early, last, first, first_sums)
    short = call(
        short_kernel,
        shape((1, GROUP), f32),
        [smem()] + [vmem()] * 6,
        [pltpu.VMEM((tokens, width), bf16)],
        2 * tokens * width * wide,
    )(lengths, events, near, across, corner, weights, norm_gain)
    local = call(
        local_kernel, shape((2 * tokens, GROUP), f32), [vmem()], [], 2 * 2 * tokens * tokens * GROUP
    )(feats)
    part = call(
        pool_kernel,
        shape((2 * here, 1, 2 * GROUP + HEAD_DIM), f32),
        [smem()] + [vmem()] * 8,
        [],
        2 * 9 * tokens * tokens * GROUP,
    )(lengths, *each(message), feats, local, sums, short, pool_gain)
    parts = lax.all_to_all(part, ("seq", "dp", "domain"), 0, 0, tiled=True)
    vec, loss = call(
        loss_kernel,
        (shape((1, 1, width // 8), bf16), shape((1, 1), f32)),
        [smem(), vmem()],
        [pltpu.VMEM((1, width), f32)],
        2**14,
    )(positives, parts)
    return vec, loss


def solution(mesh):
    placed = (
        P("domain", "dp", "seq", None),
        P("domain", "seq", None),
        P("domain", None),
        P("domain", None),
        P("domain", "dp"),
        P(),
    )
    small = mesh.shape["seq"] == 2 * PLANES and mesh.shape["dp"] == 2
    return jax.shard_map(
        towers if small else shards,
        mesh=mesh,
        in_specs=placed,
        out_specs=(P("domain", "dp", "seq"), P("domain", "dp")),
        check_vma=False,
    )
```
